32 devices in a mesh: gy: 4 (over z), gx: 8 (over y, x, core).
Axes of the slice: x: 2, y: 2, z: 4, core: 2. Of those that a mesh axis runs over, the one named last changes fastest.
Arguments:
- observed: float32 [16, 128, 1024], P(None, 'gy', 'gx'), may hold values from 0 to 20, as said below
- profiles: float32 [64, 3, 9], replicated, may hold values from 0.03 to 0.25
- tile_index: int32 [4, 8], replicated, may hold values from 0 to 63
Outputs:
- estimate: float32 [16, 128, 1024], P(None, 'gy', 'gx')
The draws below stay inside these ranges and needn't reach their ends.
Inputs may be any that keep to these rules, and one draw needn't show every extreme that they name: `observed`: nonnegative intensities.
All inputs are finite; a program needn't handle non-finite values.
Results may differ from the reference program's by a relative error of at most 0.0003.
Values sent between devices are 32-bit elements; how exact they have to be, the bound alone decides.
No kernel may reach another device: no remote copies, remote signals or barrier semaphores. Data moves between devices by JAX's collectives and lax.ppermute only.
A program may use at most 64 MiB of HBM per device.

```python
import math
import jax
import jax.numpy as jnp
from jax import lax

Z = 16
CY = 32
CX = 128
ITERS = 2
TAPS = 9
KERNELS = 64
NY = 128
NX = 1024
GRID_ROWS = 4
GRID_COLS = 8
N_GY = 4
N_GX = 8


def draw_observed(key, part):
    uniform_key = jax.random.fold_in(key, 0)
    uniform_part = jax.random.uniform(uniform_key, (Z, NY, NX), jnp.float32)
    rising = (1.0 + 2.0 * jnp.arange(NY, dtype=jnp.float32) / NY)[:, None] * (1.0 + 0.5 * jnp.arange(NX, dtype=jnp.float32) / NX)[None, :]
    return uniform_part * rising[None]


def plant(result, stream_key, low, largest):
    place = [jax.random.randint(jax.random.fold_in(stream_key, axis), (), 0, length) for axis, length in enumerate(result.shape)]
    main_axis = result.shape.index(max(result.shape))
    beside = place[:main_axis] + [(place[main_axis] + 1) % result.shape[main_axis]] + place[main_axis + 1:]
    return result.at[tuple(place)].set(low).at[tuple(beside)].set(largest)


def setup_inputs(seed: int = 0) -> dict:
    splits = jax.random.split(jax.random.key(seed), 4)
    observed = draw_observed(jax.random.fold_in(splits[3], 71), 0)
    profiles = jnp.clip(jnp.exp(jax.random.uniform(splits[1], (KERNELS, 3, TAPS), jnp.float32, math.log(0.03), math.log(0.25))), 0.03, 0.25)
    tile_index = plant(jax.random.randint(splits[2], (GRID_ROWS, GRID_COLS), 0, KERNELS), jax.random.fold_in(splits[2], 1), 0, KERNELS - 1).astype(jnp.int32)
    return dict(observed=observed, profiles=profiles, tile_index=tile_index)


WEIGHT_TV = 0.02
SMOOTHING = 0.1
DAMPING = 0.05
START_STEP = 0.5

def shifted_sum(padded, profile, dimension, extent):
    radius = (profile.shape[0] - 1) // 2
    summed = jnp.zeros_like(lax.slice_in_dim(padded, 0, extent, axis=dimension))
    for offset in range(profile.shape[0]):
        opening = 2 * radius - offset
        summed = summed + profile[offset] * lax.slice_in_dim(padded, opening, opening + extent, axis=dimension)
    return summed

def blur_window(window, profile):
    radius = (profile.shape[1] - 1) // 2
    depth_padded = jnp.pad(window, ((radius, radius), (0, 0), (0, 0)))
    along_depth = shifted_sum(depth_padded, profile[0], 0, Z)
    along_rows = shifted_sum(along_depth, profile[1], 1, CY)
    return shifted_sum(along_rows, profile[2], 2, CX)

def blur_volume(estimate, profiles, tile_index):
    radius = (profiles.shape[2] - 1) // 2
    padded = jnp.pad(estimate, ((0, 0), (radius, radius), (radius, radius)))

    def one_block(number):
        block_row = number // N_GX
        block_col = number % N_GX
        window = lax.dynamic_slice(padded, (jnp.int32(0), (block_row * CY).astype(jnp.int32), (block_col * CX).astype(jnp.int32)), (Z, CY + 2 * radius, CX + 2 * radius))
        return blur_window(window, profiles[tile_index[block_row, block_col]])
    blocks = lax.map(one_block, jnp.arange(N_GY * N_GX, dtype=jnp.int32))
    blocks = blocks.reshape(N_GY, N_GX, Z, CY, CX).transpose(2, 0, 3, 1, 4)
    return blocks.reshape(Z, N_GY * CY, N_GX * CX)

def variation(estimate):
    diff_depth = jnp.concatenate([estimate[1:] - estimate[:-1], jnp.zeros_like(estimate[:1])], 0)
    diff_rows = jnp.concatenate([estimate[:, 1:] - estimate[:, :-1], jnp.zeros_like(estimate[:, :1])], 1)
    diff_cols = jnp.concatenate([estimate[:, :, 1:] - estimate[:, :, :-1], jnp.zeros_like(estimate[:, :, :1])], 2)
    return jnp.sum(jnp.sqrt(diff_depth * diff_depth + diff_rows * diff_rows + diff_cols * diff_cols + SMOOTHING * SMOOTHING))

def gradient(estimate, observed, profiles, tile_index):
    blurred, pullback = jax.vjp(lambda value: blur_volume(value, profiles, tile_index), estimate)
    pulled = pullback(blurred - observed)[0]
    return pulled + WEIGHT_TV * jax.grad(variation)(estimate) + DAMPING * estimate

def reference(observed, profiles, tile_index):
    previous = observed
    prev_descent = gradient(previous, observed, profiles, tile_index)
    current = previous - START_STEP * prev_descent
    for iteration in range(ITERS):
        descent = gradient(current, observed, profiles, tile_index)
        change = current - previous
        growth = descent - prev_descent
        step_size = jnp.sum(change * change) / jnp.sum(change * growth)
        previous, prev_descent = (current, descent)
        current = current - step_size * descent
    return current
```

```python
import functools
import jax
import jax.numpy as jnp
from jax import lax
from jax.experimental import pallas as pl
from jax.experimental.pallas import tpu as pltpu
from jax.sharding import PartitionSpec as P

ITERS = 2
WEIGHT_TV = 0.02
SMOOTHING = 0.1
DAMPING = 0.05
START_STEP = 0.5
SUB = 8
F32 = jnp.float32
BF16 = jnp.bfloat16
VMEM_BYTES = 44 * 1024 * 1024


def plan(layers, height, breadth, taps):
    radius = (taps - 1) // 2
    halo = 6 * radius
    off = -(-halo // SUB) * SUB + SUB
    slot = 1
    while slot < halo:
        slot *= 2
    return dict(
        layers=layers, height=height, breadth=breadth, taps=taps, radius=radius, halo=halo, off=off,
        rows=height + 2 * off, slot=slot, per_pack=breadth // slot, first=off // SUB, last=(off + height) // SUB,
        tiles=(height + 2 * off) // SUB,
    )


def reach(s, extent):
    low = (s["off"] - extent) // SUB
    high = -(-(s["off"] + s["height"] + extent) // SUB)
    return low, high


def bands(s):
    return ((0, s["first"]), (s["first"], s["last"]), (s["last"], s["tiles"]))


def place():
    return lax.axis_index("gy"), lax.axis_index("gx"), lax.axis_size("gy"), lax.axis_size("gx")


def weights_kernel(s, index_ref, profiles_ref, taps_ref, high_ref, low_ref):
    gy, gx, ny, nx = place()
    breadth, taps, radius = s["breadth"], s["taps"], s["radius"]
    ring = 2 * breadth
    lane = lax.broadcasted_iota(jnp.int32, (SUB, breadth), 1)
    chunk = 32
    for band in range(3):
        row = gy + (band - 1)
        picked = []
        for side in range(3):
            col = gx + (side - 1)
            inside = (row >= 0) & (row < ny) & (col >= 0) & (col < nx)
            number = index_ref[jnp.clip(row, 0, ny - 1), jnp.clip(col, 0, nx - 1)]
            picked.append((inside, number))
        columns = []
        for dim in range(3):
            for tap in range(taps):
                left, centre, right = [
                    jnp.where(inside, profiles_ref[tap, dim, number], 0.0) for inside, number in picked
                ]
                main = jnp.full((SUB, breadth), centre, F32)
                side = jnp.where(lane < breadth // 2, right, left)
                if dim < 2:
                    taps_ref[band, dim, 0, tap] = main
                    taps_ref[band, dim, 1, tap] = side
                else:
                    columns.append(jnp.concatenate([main, side], axis=1)[:1])

        def build(piece, carry, band=band, columns=columns):
            start = pl.multiple_of(piece * chunk, chunk)
            source = lax.broadcasted_iota(jnp.int32, (chunk, ring), 0) + start
            target = lax.broadcasted_iota(jnp.int32, (chunk, ring), 1)
            distance = target - source + radius
            distance = jnp.where(distance < 0, distance + ring, distance)
            distance = jnp.where(distance >= ring, distance - ring, distance)
            total = jnp.zeros((chunk, ring), F32)
            for tap in range(taps):
                total = jnp.where(distance == tap, columns[tap], total)
            upper = total.astype(BF16)
            high_ref[band, pl.ds(start, chunk), :] = upper
            low_ref[band, pl.ds(start, chunk), :] = (total - upper.astype(F32)).astype(BF16)
            return carry

        lax.fori_loop(0, ring // chunk, build, 0)


def pack_kernel(s, tile_ref, even_ref, odd_ref, first_ref, second_ref):
    gy, gx, _, _ = place()
    halo, height, slot, per = s["halo"], s["height"], s["slot"], s["per_pack"]
    breadth = s["breadth"]
    row_even, col_even = lax.rem(gy, 2) == 0, lax.rem(gx, 2) == 0
    lane = lax.broadcasted_iota(jnp.int32, (1, breadth), 1)
    pieces = ((0, None, halo), (halo, tile_ref, height), (halo + height, None, halo))
    for start, ref, count in pieces:
        for group in range(s["layers"] // per):
            first = jnp.zeros((count, breadth), F32)
            second = jnp.zeros((count, breadth), F32)
            for member in range(per):
                layer = group * per + member
                if ref is not None:
                    value = ref[layer]
                elif start == 0:
                    value = jnp.where(row_even, odd_ref[layer], even_ref[layer])
                else:
                    value = jnp.where(row_even, even_ref[layer], odd_ref[layer])
                mine = (lane >= member * slot) & (lane < (member + 1) * slot)
                to_left = member * slot
                to_right = (member * slot + slot) % breadth
                first = jnp.where(mine, pltpu.roll(value, jnp.where(col_even, to_right, to_left), 1), first)
                second = jnp.where(mine, pltpu.roll(value, jnp.where(col_even, to_left, to_right), 1), second)
            first_ref[group, start:start + count, :] = first
            second_ref[group, start:start + count, :] = second


def dot_split(value, high, low, contract):
    dims = (((1,), (contract,)), ((), ()))
    upper = value.astype(BF16)
    lower = (value - upper.astype(F32)).astype(BF16)
    mul = functools.partial(lax.dot_general, dimension_numbers=dims, preferred_element_type=F32)
    return mul(upper, high) + (mul(upper, low) + mul(lower, high))


def rows_of(ref, low, high):
    count = (high - low) * SUB
    pair = [ref[half, :, low * SUB:high * SUB, :] for half in range(2)]
    layers, breadth = pair[0].shape[0], pair[0].shape[2]
    return jnp.concatenate([p.reshape(layers * count, breadth) for p in pair], axis=1)


def column_pass(s, source, target, low, high, m_high, m_low, contract, add):
    if low >= high:
        return
    layers, breadth, count = s["layers"], s["breadth"], (high - low) * SUB
    result = dot_split(rows_of(source, low, high), m_high, m_low, contract)
    for half in range(2):
        piece = result[:, half * breadth:(half + 1) * breadth].reshape(layers, count, breadth)
        if add:
            piece = piece + target[half, :, low * SUB:high * SUB, :]
        target[half, :, low * SUB:high * SUB, :] = piece


def row_depth(s, source, half, tile, row_taps, depth_taps, transposed):
    layers, taps, radius = s["layers"], s["taps"], s["radius"]
    start = tile * SUB
    mixed = []
    for layer in range(layers):
        total = None
        for tap in range(taps):
            shift = tap - radius if transposed else radius - tap
            term = row_taps[tap] * source[half, layer, pl.ds(start + shift, SUB), :]
            total = term if total is None else total + term
        mixed.append(total)
    outs = []
    for layer in range(layers):
        total = None
        for tap in range(taps):
            shift = tap - radius if transposed else radius - tap
            if 0 <= layer + shift < layers:
                term = depth_taps[tap] * mixed[layer + shift]
                total = term if total is None else total + term
        outs.append(total)
    return outs


def row_depth_pass(s, taps_ref, band, source, low, high, transposed, emit):
    def body(tile, carry):
        for half in range(2):
            row_taps = [taps_ref[band, 1, half, t] for t in range(s["taps"])]
            depth_taps = [taps_ref[band, 0, half, t] for t in range(s["taps"])]
            emit(half, tile, row_depth(s, source, half, tile, row_taps, depth_taps, transposed))
        return carry

    if low < high:
        lax.fori_loop(low, high, body, 0)


def slope_pass(s, source, shift, low, high, divergence, flux_rows, where):
    gy, gx, ny, nx = where
    layers, height, breadth = s["layers"], s["height"], s["breadth"]
    ring = 2 * breadth
    lane = lax.broadcasted_iota(jnp.int32, (SUB, ring), 1)
    col = gx * breadth + jnp.where(lane < breadth + breadth // 2, lane, lane - ring)
    col_mask = jnp.where((col >= 0) & (col < nx * breadth - 1), 1.0, 0.0).astype(F32)

    def body(tile, carry):
        start = tile * SUB
        row = gy * height + start - s["off"] + shift + lax.broadcasted_iota(jnp.int32, (SUB, ring), 0)
        row_mask = jnp.where((row >= 0) & (row < ny * height - 1), 1.0, 0.0).astype(F32)

        def load(layer, begin):
            return jnp.concatenate([source[half, layer, pl.ds(begin, SUB), :] for half in range(2)], axis=1)

        here = load(0, start)
        flux_before = None
        for layer in range(layers):
            below = load(layer, start + 1)
            step_rows = (below - here) * row_mask
            step_cols = (pltpu.roll(here, ring - 1, 1) - here) * col_mask
            square = step_rows * step_rows + step_cols * step_cols + SMOOTHING * SMOOTHING
            if layer + 1 < layers:
                after = load(layer + 1, start)
                step_depth = after - here
                square = square + step_depth * step_depth
            inverse = lax.rsqrt(square)
            f_rows, f_cols = step_rows * inverse, step_cols * inverse
            total = pltpu.roll(f_cols, 1, 1) - f_cols - f_rows
            if flux_before is not None:
                total = total + flux_before
            if layer + 1 < layers:
                flux_before = step_depth * inverse
                total = total - flux_before
                here = after
            for half in range(2):
                part = slice(half * breadth, (half + 1) * breadth)
                divergence[half, layer, pl.ds(start, SUB), :] = total[:, part]
                flux_rows[half, layer, pl.ds(start, SUB), :] = f_rows[:, part]
        return carry

    lax.fori_loop(low - 1, high, body, 0)


def main_kernel(s, tile_ref, even_ref, odd_ref, first_ref, second_ref, taps_ref, high_ref, low_ref,
                x1_ref, g1_ref, pull_ref, again_ref, part_ref,
                x0, x1, g0, y0, y1, y2, r0, r1, r2, q0, q1, q2, acc, div, flux):
    where = place()
    gy, gx, ny, nx = where
    layers, height, breadth, off = s["layers"], s["height"], s["breadth"], s["off"]
    halo, slot, per, radius = s["halo"], s["slot"], s["per_pack"], s["radius"]
    first_tile, last_tile = s["first"], s["last"]
    row_even, col_even = lax.rem(gy, 2) == 0, lax.rem(gx, 2) == 0
    lane = lax.broadcasted_iota(jnp.int32, (1, breadth), 1)
    ys, rs, qs = (y0, y1, y2), (r0, r1, r2), (q0, q1, q2)
    span = bands(s)

    top = off - halo
    x0[:, :, :top, :] = jnp.zeros((2, layers, top, breadth), F32)
    x0[:, :, off + height + halo:, :] = jnp.zeros((2, layers, top, breadth), F32)
    x0[0, :, top:off, :] = jnp.where(row_even, odd_ref[...], even_ref[...])
    x0[0, :, off:off + height, :] = tile_ref[...]
    x0[0, :, off + height:off + height + halo, :] = jnp.where(row_even, even_ref[...], odd_ref[...])

    def unpack(group, carry):
        first, second = first_ref[group], second_ref[group]
        right = jnp.where(col_even, first, second)
        left = jnp.where(col_even, second, first)
        for member in range(per):
            value = jnp.where(lane < slot, pltpu.roll(right, (breadth - member * slot) % breadth, 1), 0.0)
            value = jnp.where(lane >= breadth - slot, pltpu.roll(left, (breadth - slot - member * slot) % breadth, 1), value)
            x0[1, group * per + member, top:top + 2 * halo + height, :] = value
        return carry

    lax.fori_loop(0, layers // per, unpack, 0)

    zero = jnp.zeros((2, layers, SUB, breadth), F32)
    y0[:, :, :SUB, :] = zero
    y2[:, :, (s["tiles"] - 1) * SUB:, :] = zero
    for tile in (first_tile, first_tile + 1):
        r0[:, :, tile * SUB:(tile + 1) * SUB, :] = zero
    for tile in (first_tile - 2, first_tile - 1, last_tile, last_tile + 1):
        r1[:, :, tile * SUB:(tile + 1) * SUB, :] = zero
    for tile in (last_tile - 2, last_tile - 1):
        r2[:, :, tile * SUB:(tile + 1) * SUB, :] = zero

    def forward(source, extent, emit):
        low, high = reach(s, extent)
        in_low, in_high = reach(s, extent + radius)
        for band in range(3):
            out_low, out_high = max(low, span[band][0]), min(high, span[band][1])
            column_pass(s, source, ys[band], max(out_low - 1, in_low), min(out_high + 1, in_high),
                        high_ref[band], low_ref[band], 0, False)
            row_depth_pass(s, taps_ref, band, ys[band], out_low, out_high, False,
                           functools.partial(emit, band))

    def backward(extent):
        low, high = reach(s, extent)
        for band in range(3):
            out_low, out_high = max(low, span[band][0] - 1), min(high, span[band][1] + 1)

            def emit(half, tile, outs, band=band):
                for layer in range(layers):
                    qs[band][half, layer, pl.ds(pl.multiple_of(tile * SUB, SUB), SUB), :] = outs[layer]

            row_depth_pass(s, taps_ref, band, rs[band], out_low, out_high, True, emit)
        middle = span[1]
        column_pass(s, q1, acc, max(low, middle[0] - 1), min(high, middle[1] + 1), high_ref[1], low_ref[1], 1, False)
        if low < middle[0] - 1:
            acc[:, :, low * SUB:(middle[0] - 1) * SUB, :] = jnp.zeros((2, layers, (middle[0] - 1 - low) * SUB, breadth), F32)
            acc[:, :, (middle[1] + 1) * SUB:high * SUB, :] = jnp.zeros((2, layers, (high - middle[1] - 1) * SUB, breadth), F32)
        for band in (0, 2):
            out_low, out_high = max(low, span[band][0] - 1), min(high, span[band][1] + 1)
            column_pass(s, qs[band], acc, out_low, out_high, high_ref[band], low_ref[band], 1, True)

    def residual(band, half, tile, outs):
        at = pl.ds(pl.multiple_of(tile * SUB, SUB), SUB)
        for layer in range(layers):
            rs[band][half, layer, at, :] = outs[layer] - x0[half, layer, at, :]

    def plain(band, half, tile, outs):
        at = pl.ds(pl.multiple_of(tile * SUB, SUB), SUB)
        for layer in range(layers):
            rs[band][half, layer, at, :] = outs[layer]

    def inside(tile, half):
        row = gy * height + tile * SUB - off + lax.broadcasted_iota(jnp.int32, (SUB, breadth), 0)
        here = lax.broadcasted_iota(jnp.int32, (SUB, breadth), 1)
        if half == 1:
            here = jnp.where(here < breadth // 2, here + breadth, here - breadth)
        col = gx * breadth + here
        return (row >= 0) & (row < ny * height) & (col >= 0) & (col < nx * breadth)

    def slope(source, half, tile):
        at = pl.ds(pl.multiple_of(tile * SUB, SUB), SUB)
        before = pl.ds(tile * SUB - 1, SUB)
        keep = inside(tile, half)
        values = []
        for layer in range(layers):
            total = acc[half, layer, at, :] + WEIGHT_TV * (div[half, layer, at, :] + flux[half, layer, before, :])
            total = total + DAMPING * source[half, layer, at, :]
            values.append(jnp.where(keep, total, 0.0))
        return at, values

    slope_pass(s, x0, 0, *reach(s, 4 * radius), div, flux, where)
    forward(x0, 5 * radius, residual)
    backward(4 * radius)

    def first_step(tile, carry):
        for half in range(2):
            at, values = slope(x0, half, tile)
            for layer in range(layers):
                g0[half, layer, at, :] = values[layer]
                x1[half, layer, at, :] = x0[half, layer, at, :] - START_STEP * values[layer]
        return carry

    lax.fori_loop(*reach(s, 4 * radius), first_step, 0)

    slope_pass(s, x1, 0, *reach(s, 2 * radius), div, flux, where)
    forward(x1, 3 * radius, residual)
    backward(2 * radius)
    low, high = reach(s, 2 * radius)

    def second_step(tile, carry):
        for half in range(2):
            at, values = slope(x1, half, tile)
            local = pl.ds(pl.multiple_of((tile - low) * SUB, SUB), SUB)
            for layer in range(layers):
                g1_ref[half, layer, local, :] = values[layer]
                x1_ref[half, layer, local, :] = x1[half, layer, at, :]
                x1[half, layer, at, :] = values[layer]
        return carry

    lax.fori_loop(low, high, second_step, 0)
    centre = slice(first_tile * SUB, last_tile * SUB)
    pull_ref[...] = acc[0, :, centre, :]

    forward(x1, radius, plain)
    backward(0)
    again_ref[...] = acc[0, :, centre, :]

    def sums(tile, carry):
        at = pl.ds(pl.multiple_of(tile * SUB, SUB), SUB)
        zero_sq, cross, one_sq = carry
        for layer in range(layers):
            a, b = g0[0, layer, at, :], x1[0, layer, at, :]
            zero_sq, cross, one_sq = zero_sq + a * a, cross + a * (b - a), one_sq + b * b
        return zero_sq, cross, one_sq

    start = jnp.zeros((SUB, breadth), F32)
    totals = lax.fori_loop(first_tile, last_tile, sums, (start, start, start))
    zero_sq, cross, one_sq = [jnp.sum(t, axis=(0, 1), keepdims=True) for t in totals]
    row = jnp.where(lane == 0, zero_sq, jnp.where(lane == 1, cross, one_sq))
    part_ref[...] = jnp.broadcast_to(row, part_ref.shape)


def step_kernel(s, sums_ref, x1_ref, g1_ref, pull_ref, again_ref, x2_ref, g2_ref, part_ref, keep_ref, x2, div, flux):
    where = place()
    layers, height, breadth = s["layers"], s["height"], s["breadth"]
    low, high = reach(s, 2 * s["radius"])
    lane = lax.broadcasted_iota(jnp.int32, (1, breadth), 1)
    total = jnp.sum(sums_ref[...], axis=0, keepdims=True)
    zero_sq, cross, one_sq = [
        jnp.sum(jnp.where(lane == number, total, 0.0), axis=(0, 1), keepdims=True) for number in range(3)
    ]
    step = (START_STEP * START_STEP * zero_sq) / (-START_STEP * cross)
    count = (high - low) * SUB
    for half in range(2):
        for layer in range(layers):
            x2[half, layer, :count, :] = x1_ref[half, layer] - step * g1_ref[half, layer]
    begin = s["first"] - low
    slope_pass(s, x2, low * SUB, begin, begin + height // SUB, div, flux, where)

    def body(tile, carry):
        at = pl.ds(pl.multiple_of(tile * SUB, SUB), SUB)
        before = pl.ds(tile * SUB - 1, SUB)
        out = pl.ds(pl.multiple_of((tile - begin) * SUB, SUB), SUB)
        for layer in range(layers):
            here = x2[0, layer, at, :]
            slope = pull_ref[layer, out, :] - step * again_ref[layer, out, :]
            slope = slope + WEIGHT_TV * (div[0, layer, at, :] + flux[0, layer, before, :]) + DAMPING * here
            x2_ref[layer, out, :] = here
            g2_ref[layer, out, :] = slope
            old = g1_ref[0, layer, at, :]
            carry = carry + old * (slope - old)
        return carry

    total = lax.fori_loop(begin, begin + height // SUB, body, jnp.zeros((SUB, breadth), F32))
    growth = -step * jnp.sum(total, axis=(0, 1), keepdims=True)
    part_ref[...] = jnp.broadcast_to(growth, part_ref.shape)
    keep_ref[...] = jnp.broadcast_to(step * step * one_sq, keep_ref.shape)


def final_kernel(sums_ref, keep_ref, x2_ref, g2_ref, out_ref):
    step = keep_ref[:1, :] / jnp.sum(sums_ref[...], axis=0, keepdims=True)
    for layer in range(x2_ref.shape[0]):
        out_ref[layer] = x2_ref[layer] - step * g2_ref[layer]


def pairings(count):
    def both(start):
        pairs = []
        for i in range(start, count - 1, 2):
            pairs += [(i, i + 1), (i + 1, i)]
        return pairs

    return both(0), both(1)


def call(kernel, outs, scratch=(), inputs=None):
    whole = pl.BlockSpec(memory_space=pltpu.VMEM)
    return pl.pallas_call(
        kernel,
        out_shape=outs,
        in_specs=inputs,
        out_specs=jax.tree.map(lambda _: whole, outs),
        scratch_shapes=list(scratch),
        compiler_params=pltpu.CompilerParams(vmem_limit_bytes=VMEM_BYTES),
    )


def per_device(observed, profiles, tile_index):
    layers, height, breadth = observed.shape
    s = plan(layers, height, breadth, profiles.shape[2])
    halo, rows, taps = s["halo"], s["rows"], s["taps"]
    ring = 2 * breadth
    gy = lax.axis_index("gy")
    n = lax.axis_size("gy") * lax.axis_size("gx")
    vmem, smem = pl.BlockSpec(memory_space=pltpu.VMEM), pl.BlockSpec(memory_space=pltpu.SMEM)
    sds = jax.ShapeDtypeStruct

    even = lax.rem(gy, 2) == 0
    bottom, top = jnp.int32(height - halo), jnp.int32(0)
    to_even = lax.dynamic_slice_in_dim(observed, jnp.where(even, bottom, top), halo, axis=1)
    to_odd = lax.dynamic_slice_in_dim(observed, jnp.where(even, top, bottom), halo, axis=1)
    first_pairs, second_pairs = pairings(lax.axis_size("gy"))
    from_even = lax.ppermute(to_even, "gy", first_pairs)
    from_odd = lax.ppermute(to_odd, "gy", second_pairs)

    taps_all, m_high, m_low = call(
        functools.partial(weights_kernel, s),
        (sds((3, 2, 2, taps, SUB, breadth), F32), sds((3, ring, ring), BF16), sds((3, ring, ring), BF16)),
        inputs=[smem, smem],
    )(tile_index, profiles.transpose(2, 1, 0))

    packed = (layers // s["per_pack"], height + 2 * halo, breadth)
    first, second = call(
        functools.partial(pack_kernel, s), (sds(packed, F32), sds(packed, F32)), inputs=[vmem] * 3
    )(observed, from_even, from_odd)
    first_pairs, second_pairs = pairings(lax.axis_size("gx"))
    got_first = lax.ppermute(first, "gx", first_pairs)
    got_second = lax.ppermute(second, "gx", second_pairs)

    big = pltpu.VMEM((2, layers, rows, breadth), F32)
    low, high = reach(s, 2 * s["radius"])
    wide = (2, layers, (high - low) * SUB, breadth)
    tile = sds((layers, height, breadth), F32)
    x1, g1, pull, again, part = call(
        functools.partial(main_kernel, s),
        (sds(wide, F32), sds(wide, F32), tile, tile, sds((n, breadth), F32)),
        scratch=[big] * 15,
        inputs=[vmem] * 8,
    )(observed, from_even, from_odd, got_first, got_second, taps_all, m_high, m_low)
    sums = lax.all_to_all(part, ("gy", "gx"), 0, 0, tiled=True)
    work = pltpu.VMEM((2, layers, (high - low + 1) * SUB, breadth), F32)
    x2, g2, part, keep = call(
        functools.partial(step_kernel, s),
        (tile, tile, sds((n, breadth), F32), sds((SUB, breadth), F32)),
        scratch=[work] * 3,
        inputs=[vmem] * 5,
    )(sums, x1, g1, pull, again)
    sums = lax.all_to_all(part, ("gy", "gx"), 0, 0, tiled=True)
    return call(final_kernel, tile, inputs=[vmem] * 4)(sums, keep, x2, g2)


def solution(mesh):
    in_specs = (P(None, "gy", "gx"), P(), P())
    out_specs = P(None, "gy", "gx")
    return jax.shard_map(
        per_device, mesh=mesh, in_specs=in_specs, out_specs=out_specs, check_vma=False
    )
```

```python
import functools
import jax
import jax.numpy as jnp
from jax import lax
from jax.experimental import pallas as pl
from jax.experimental.pallas import tpu as pltpu
from jax.sharding import PartitionSpec as P

ITERS = 2
WEIGHT_TV = 0.02
SMOOTHING = 0.1
DAMPING = 0.05
START_STEP = 0.5
SUB = 8
F32 = jnp.float32
BF16 = jnp.bfloat16
VMEM_BYTES = 44 * 1024 * 1024


def plan(layers, height, breadth, taps):
    radius = (taps - 1) // 2
    halo = 6 * radius
    off = -(-halo // SUB) * SUB + SUB
    return dict(
        layers=layers, height=height, breadth=breadth, taps=taps, radius=radius, halo=halo, off=off,
        rows=height + 2 * off, groups=-(-layers * halo // breadth), first=off // SUB, last=(off + height) // SUB,
        tiles=(height + 2 * off) // SUB,
    )


def reach(s, extent):
    low = (s["off"] - extent) // SUB
    high = -(-(s["off"] + s["height"] + extent) // SUB)
    return low, high


def bands(s):
    return ((0, s["first"]), (s["first"], s["last"]), (s["last"], s["tiles"]))


def place():
    return lax.axis_index("gy"), lax.axis_index("gx"), lax.axis_size("gy"), lax.axis_size("gx")


def weights_kernel(s, index_ref, profiles_ref, taps_ref, forward_ref, backward_ref, full):
    gy, gx, ny, nx = place()
    breadth, taps, radius = s["breadth"], s["taps"], s["radius"]
    ring = 2 * breadth
    lane = lax.broadcasted_iota(jnp.int32, (SUB, breadth), 1)
    chunk = 32

    def split(value):
        upper = value.astype(BF16)
        return upper, (value - upper.astype(F32)).astype(BF16)

    for band in range(3):
        row = gy + (band - 1)
        picked = []
        for side in range(3):
            col = gx + (side - 1)
            inside = (row >= 0) & (row < ny) & (col >= 0) & (col < nx)
            number = index_ref[jnp.clip(row, 0, ny - 1), jnp.clip(col, 0, nx - 1)]
            picked.append((inside, number))
        columns = []
        for dim in range(3):
            for tap in range(taps):
                left, centre, right = [
                    jnp.where(inside, profiles_ref[tap, dim, number], 0.0) for inside, number in picked
                ]
                main = jnp.full((SUB, breadth), centre, F32)
                side = jnp.where(lane < breadth // 2, right, left)
                if dim < 2:
                    taps_ref[band, dim, 0, tap] = main
                    taps_ref[band, dim, 1, tap] = side
                else:
                    columns.append(jnp.concatenate([main, side], axis=1)[:1])

        def build(piece, carry, band=band, columns=columns):
            start = pl.multiple_of(piece * chunk, chunk)
            source = lax.broadcasted_iota(jnp.int32, (chunk, ring), 0) + start
            target = lax.broadcasted_iota(jnp.int32, (chunk, ring), 1)
            distance = target - source + radius
            distance = jnp.where(distance < 0, distance + ring, distance)
            distance = jnp.where(distance >= ring, distance - ring, distance)
            total = jnp.zeros((chunk, ring), F32)
            for tap in range(taps):
                total = jnp.where(distance == tap, columns[tap], total)
            full[pl.ds(start, chunk), :] = total
            return carry

        lax.fori_loop(0, ring // chunk, build, 0)
        value = full[...]
        for ref, matrix in ((forward_ref, value), (backward_ref, value.T)):
            upper, lower = split(matrix)
            ref[band, :ring, :] = upper
            ref[band, ring:2 * ring, :] = lower
            ref[band, 2 * ring:, :] = upper


def strip_places(s, layer):
    group, lane = divmod(layer * s["halo"], s["breadth"])
    return group, lane, min(s["halo"], s["breadth"] - lane)


def pack_kernel(s, tile_ref, even_ref, odd_ref, first_ref, second_ref):
    gy, gx, _, _ = place()
    halo, height, breadth = s["halo"], s["height"], s["breadth"]
    row_even, col_even = lax.rem(gy, 2) == 0, lax.rem(gx, 2) == 0
    lane = lax.broadcasted_iota(jnp.int32, (1, breadth), 1)
    for start, count in ((0, halo), (halo, height), (halo + height, halo)):
        first = [jnp.zeros((count, breadth), F32)] * s["groups"]
        second = list(first)
        for layer in range(s["layers"]):
            if start == halo:
                value = tile_ref[layer]
            elif start == 0:
                value = jnp.where(row_even, odd_ref[layer], even_ref[layer])
            else:
                value = jnp.where(row_even, even_ref[layer], odd_ref[layer])
            group, begin, here = strip_places(s, layer)
            from_left, from_right = begin, (begin + halo) % breadth
            to_first = pltpu.roll(value, jnp.where(col_even, from_right, from_left), 1)
            to_second = pltpu.roll(value, jnp.where(col_even, from_left, from_right), 1)
            parts = [(group, (lane >= begin) & (lane < begin + here))]
            if here < halo:
                parts.append((group + 1, lane < halo - here))
            for number, mine in parts:
                first[number] = jnp.where(mine, to_first, first[number])
                second[number] = jnp.where(mine, to_second, second[number])
        for number in range(s["groups"]):
            first_ref[number, start:start + count, :] = first[number]
            second_ref[number, start:start + count, :] = second[number]


def unpack_layer(s, groups, layer, to):
    breadth = s["breadth"]
    lane = lax.broadcasted_iota(jnp.int32, (1, breadth), 1)
    group, begin, here = strip_places(s, layer)
    value = groups[group]
    if here < s["halo"]:
        value = jnp.where(lane >= begin, value, groups[group + 1])
    shift = (to - begin) % breadth
    return pltpu.roll(value, shift, 1) if shift else value


def row_depth(s, load, row_taps, depth_taps, transposed):
    layers, taps, radius = s["layers"], s["taps"], s["radius"]
    mixed = []
    for layer in range(layers):
        total = None
        for tap in range(taps):
            term = row_taps[tap] * load(layer, tap - radius if transposed else radius - tap)
            total = term if total is None else total + term
        mixed.append(total)
    outs = []
    for layer in range(layers):
        total = None
        for tap in range(taps):
            shift = tap - radius if transposed else radius - tap
            if 0 <= layer + shift < layers:
                term = depth_taps[tap] * mixed[layer + shift]
                total = term if total is None else total + term
        outs.append(total)
    return outs


def slope_tile(s, source, shift, tile, divergence, flux_rows, where):
    gy, gx, ny, nx = where
    layers, height, breadth = s["layers"], s["height"], s["breadth"]
    ring = 2 * breadth
    lane = lax.broadcasted_iota(jnp.int32, (SUB, ring), 1)
    col = gx * breadth + jnp.where(lane < breadth + breadth // 2, lane, lane - ring)
    col_mask = jnp.where((col >= 0) & (col < nx * breadth - 1), 1.0, 0.0).astype(F32)
    start = tile * SUB
    row = gy * height + start - s["off"] + shift + lax.broadcasted_iota(jnp.int32, (SUB, ring), 0)
    row_mask = jnp.where((row >= 0) & (row < ny * height - 1), 1.0, 0.0).astype(F32)

    def load(layer, begin):
        return jnp.concatenate([source[half, layer, begin:begin + SUB, :] for half in range(2)], axis=1)

    here = load(0, start)
    flux_before = None
    for layer in range(layers):
        below = load(layer, start + 1)
        step_rows = (below - here) * row_mask
        step_cols = (pltpu.roll(here, ring - 1, 1) - here) * col_mask
        square = step_rows * step_rows + step_cols * step_cols + SMOOTHING * SMOOTHING
        if layer + 1 < layers:
            after = load(layer + 1, start)
            step_depth = after - here
            square = square + step_depth * step_depth
        inverse = lax.rsqrt(square)
        f_rows, f_cols = step_rows * inverse, step_cols * inverse
        total = pltpu.roll(f_cols, 1, 1) - f_cols - f_rows
        if flux_before is not None:
            total = total + flux_before
        if layer + 1 < layers:
            flux_before = step_depth * inverse
            total = total - flux_before
            here = after
        for half in range(2):
            part = slice(half * breadth, (half + 1) * breadth)
            divergence[half, layer, start:start + SUB, :] = total[:, part]
            flux_rows[half, layer, start:start + SUB, :] = f_rows[:, part]


def main_kernel(s, tile_ref, even_ref, odd_ref, first_ref, second_ref, taps_ref, forward_ref, backward_ref,
                x1_ref, g1_ref, pull_ref, again_ref, part_ref,
                x0, x1, x2, g0, y0, y1, y2, r0, r1, r2, q0, q1, q2, acc, div, flux):
    where = place()
    gy, gx, ny, nx = where
    layers, height, breadth, off = s["layers"], s["height"], s["breadth"], s["off"]
    halo, radius, taps = s["halo"], s["radius"], s["taps"]
    begin, end = s["first"], s["last"]
    row_even, col_even = lax.rem(gy, 2) == 0, lax.rem(gx, 2) == 0
    lane = lax.broadcasted_iota(jnp.int32, (1, breadth), 1)
    xs, ys, rs, qs = (x0, x1, x2), (y0, y1, y2), (r0, r1, r2), (q0, q1, q2)
    span = bands(s)

    def rows(tile, stop=None):
        return slice(tile * SUB, (tile + 1 if stop is None else stop) * SUB)

    top = off - halo
    x0[0, :, top:off, :] = jnp.where(row_even, odd_ref[...], even_ref[...])
    x0[0, :, off:off + height, :] = tile_ref[...]
    x0[0, :, off + height:off + height + halo, :] = jnp.where(row_even, even_ref[...], odd_ref[...])
    firsts = [first_ref[g] for g in range(s["groups"])]
    seconds = [second_ref[g] for g in range(s["groups"])]
    rights = [jnp.where(col_even, a, b) for a, b in zip(firsts, seconds)]
    lefts = [jnp.where(col_even, b, a) for a, b in zip(firsts, seconds)]
    for layer in range(layers):
        value = jnp.where(lane < halo, unpack_layer(s, rights, layer, 0), 0.0)
        value = jnp.where(lane >= breadth - halo, unpack_layer(s, lefts, layer, breadth - halo), value)
        x0[1, layer, top:off + height + halo, :] = value
    zero = jnp.zeros((2, layers, SUB, breadth), F32)
    for ref, tiles in ((y0, (0,)), (y2, (s["tiles"] - 1,)), (r0, (begin, begin + 1)),
                       (r1, (begin - 2, begin - 1, end, end + 1)), (r2, (end - 2, end - 1))):
        for tile in tiles:
            ref[:, :, rows(tile), :] = zero

    def chunk(ref, low, high):
        value = jnp.concatenate(
            [ref[half, :, rows(low, high), :].reshape(layers * (high - low) * SUB, breadth) for half in range(2)], axis=1)
        upper = value.astype(BF16)
        lower = (value - upper.astype(F32)).astype(BF16)
        return jnp.concatenate([upper, upper, lower], axis=1)

    def halves(result, low, high):
        return [result[:, h * breadth:(h + 1) * breadth].reshape(layers, (high - low) * SUB, breadth) for h in range(2)]

    def taps_of(band, half):
        return [[taps_ref[band, dim, half, t] for t in range(taps)] for dim in (1, 0)]

    def one_pass(number):
        x = xs[number]
        low, high = reach(s, (5 - 2 * number) * radius)
        in_low, in_high = reach(s, (6 - 2 * number) * radius)
        back_low, back_high = reach(s, (4 - 2 * number) * radius)
        out = [(max(low, a), min(high, b)) for a, b in span]
        back = [(max(back_low, a - 1), min(back_high, b + 1)) for a, b in span]
        done = set()

        def columns(band):
            a, b = max(out[band][0] - 1, in_low), min(out[band][1] + 1, in_high)
            result = jnp.dot(chunk(x, a, b), forward_ref[band], preferred_element_type=F32)
            for half, piece in enumerate(halves(result, a, b)):
                ys[band][half, :, rows(a, b), :] = piece

        def blur_rows(band):
            for tile in range(*out[band]):
                for half in range(2):
                    load = lambda layer, shift: ys[band][half, layer, tile * SUB + shift:(tile + 1) * SUB + shift, :]
                    outs = row_depth(s, load, *taps_of(band, half), False)
                    for layer in range(layers):
                        value = outs[layer] if number == 2 else outs[layer] - x0[half, layer, rows(tile), :]
                        rs[band][half, layer, rows(tile), :] = value

        def back_rows(band):
            for tile in range(*back[band]):
                for half in range(2):
                    load = lambda layer, shift: rs[band][half, layer, tile * SUB + shift:(tile + 1) * SUB + shift, :]
                    outs = row_depth(s, load, *taps_of(band, half), True)
                    for layer in range(layers):
                        qs[band][half, layer, rows(tile), :] = outs[layer]

        def back_columns(band):
            a, b = back[band]
            result = jnp.dot(chunk(qs[band], a, b), backward_ref[band], preferred_element_type=F32)
            for half, piece in enumerate(halves(result, a, b)):
                for tile in range(a, b):
                    part = piece[:, (tile - a) * SUB:(tile - a + 1) * SUB, :]
                    acc[half, :, rows(tile), :] = acc[half, :, rows(tile), :] + part if tile in done else part
            done.update(range(a, b))

        def inside(tile, half):
            row = gy * height + tile * SUB - off + lax.broadcasted_iota(jnp.int32, (SUB, breadth), 0)
            here = lax.broadcasted_iota(jnp.int32, (SUB, breadth), 1)
            if half == 1:
                here = jnp.where(here < breadth // 2, here + breadth, here - breadth)
            col = gx * breadth + here
            return (row >= 0) & (row < ny * height) & (col >= 0) & (col < nx * breadth)

        def update(tile):
            for half in range(2):
                keep = inside(tile, half)
                for layer in range(layers):
                    here = x[half, layer, rows(tile), :]
                    total = acc[half, layer, rows(tile), :] + DAMPING * here
                    before = flux[half, layer, tile * SUB - 1:(tile + 1) * SUB - 1, :]
                    total = total + WEIGHT_TV * (div[half, layer, rows(tile), :] + before)
                    total = jnp.where(keep, total, 0.0)
                    if number == 0:
                        xs[1][half, layer, rows(tile), :] = here - START_STEP * total
                        if half == 0 and begin <= tile < end:
                            g0[layer, rows(tile), :] = total
                    else:
                        xs[2][half, layer, rows(tile), :] = total

        def slopes(a, b):
            if number < 2:
                for tile in range(a, b):
                    slope_tile(s, x, 0, tile, div, flux, where)

        middle = (begin + end) // 2
        columns(0)
        slopes(back_low - 1, middle)
        columns(1)
        blur_rows(0)
        columns(2)
        back_rows(0)
        blur_rows(1)
        back_columns(0)
        back_rows(1)
        back_columns(1)
        blur_rows(2)
        slopes(middle, back_high)
        back_rows(2)
        back_columns(2)
        if number == 1:
            pull_ref[...] = acc[0, :, rows(begin, end), :]
        if number < 2:
            for tile in range(back_low, back_high):
                update(tile)

    for number in range(3):
        one_pass(number)
    again_ref[...] = acc[0, :, rows(begin, end), :]
    low, high = reach(s, 2 * radius)
    x1_ref[...] = x1[:, :, rows(low, high), :]
    g1_ref[...] = x2[:, :, rows(low, high), :]

    zero_sq = cross = one_sq = jnp.zeros((SUB, breadth), F32)
    for tile in range(begin, end):
        for layer in range(layers):
            a, b = g0[layer, rows(tile), :], x2[0, layer, rows(tile), :]
            zero_sq, cross, one_sq = zero_sq + a * a, cross + a * (b - a), one_sq + b * b
    zero_sq, cross, one_sq = [jnp.sum(t, axis=(0, 1), keepdims=True) for t in (zero_sq, cross, one_sq)]
    row = jnp.where(lane == 0, zero_sq, jnp.where(lane == 1, cross, one_sq))
    part_ref[...] = jnp.broadcast_to(row, part_ref.shape)


def step_kernel(s, sums_ref, x1_ref, g1_ref, pull_ref, again_ref, x2_ref, g2_ref, part_ref, keep_ref, x2, div, flux):
    where = place()
    layers, height, breadth = s["layers"], s["height"], s["breadth"]
    low, high = reach(s, 2 * s["radius"])
    lane = lax.broadcasted_iota(jnp.int32, (1, breadth), 1)
    total = jnp.sum(sums_ref[...], axis=0, keepdims=True)
    zero_sq, cross, one_sq = [
        jnp.sum(jnp.where(lane == number, total, 0.0), axis=(0, 1), keepdims=True) for number in range(3)
    ]
    step = (START_STEP * START_STEP * zero_sq) / (-START_STEP * cross)
    count = (high - low) * SUB
    for half in range(2):
        for layer in range(layers):
            x2[half, layer, :count, :] = x1_ref[half, layer] - step * g1_ref[half, layer]
    begin = s["first"] - low
    total = jnp.zeros((SUB, breadth), F32)
    for tile in range(begin - 1, begin + height // SUB):
        slope_tile(s, x2, low * SUB, tile, div, flux, where)
        if tile < begin:
            continue
        at, out = slice(tile * SUB, (tile + 1) * SUB), slice((tile - begin) * SUB, (tile - begin + 1) * SUB)
        for layer in range(layers):
            here = x2[0, layer, at, :]
            slope = pull_ref[layer, out, :] - step * again_ref[layer, out, :] + DAMPING * here
            slope = slope + WEIGHT_TV * (div[0, layer, at, :] + flux[0, layer, tile * SUB - 1:(tile + 1) * SUB - 1, :])
            x2_ref[layer, out, :] = here
            g2_ref[layer, out, :] = slope
            old = g1_ref[0, layer, at, :]
            total = total + old * (slope - old)
    growth = -step * jnp.sum(total, axis=(0, 1), keepdims=True)
    part_ref[...] = jnp.broadcast_to(growth, part_ref.shape)
    keep_ref[...] = jnp.broadcast_to(step * step * one_sq, keep_ref.shape)


def final_kernel(sums_ref, keep_ref, x2_ref, g2_ref, out_ref):
    step = keep_ref[:1, :] / jnp.sum(sums_ref[...], axis=0, keepdims=True)
    for layer in range(x2_ref.shape[0]):
        out_ref[layer] = x2_ref[layer] - step * g2_ref[layer]


def pairings(count):
    def both(start):
        pairs = []
        for i in range(start, count - 1, 2):
            pairs += [(i, i + 1), (i + 1, i)]
        return pairs

    return both(0), both(1)


def call(kernel, outs, scratch=(), inputs=None):
    whole = pl.BlockSpec(memory_space=pltpu.VMEM)
    return pl.pallas_call(
        kernel,
        out_shape=outs,
        in_specs=inputs,
        out_specs=jax.tree.map(lambda _: whole, outs),
        scratch_shapes=list(scratch),
        compiler_params=pltpu.CompilerParams(vmem_limit_bytes=VMEM_BYTES),
    )


def per_device(observed, profiles, tile_index):
    layers, height, breadth = observed.shape
    s = plan(layers, height, breadth, profiles.shape[2])
    halo, rows, taps = s["halo"], s["rows"], s["taps"]
    ring = 2 * breadth
    gy = lax.axis_index("gy")
    n = lax.axis_size("gy") * lax.axis_size("gx")
    vmem, smem = pl.BlockSpec(memory_space=pltpu.VMEM), pl.BlockSpec(memory_space=pltpu.SMEM)
    sds = jax.ShapeDtypeStruct

    even = lax.rem(gy, 2) == 0
    bottom, top = jnp.int32(height - halo), jnp.int32(0)
    to_even = lax.dynamic_slice_in_dim(observed, jnp.where(even, bottom, top), halo, axis=1)
    to_odd = lax.dynamic_slice_in_dim(observed, jnp.where(even, top, bottom), halo, axis=1)
    first_pairs, second_pairs = pairings(lax.axis_size("gy"))
    from_even = lax.ppermute(to_even, "gy", first_pairs)
    from_odd = lax.ppermute(to_odd, "gy", second_pairs)

    taps_all, forward, backward = call(
        functools.partial(weights_kernel, s),
        (sds((3, 2, 2, taps, SUB, breadth), F32), sds((3, 3 * ring, ring), BF16), sds((3, 3 * ring, ring), BF16)),
        scratch=[pltpu.VMEM((ring, ring), F32)],
        inputs=[smem, smem],
    )(tile_index, profiles.transpose(2, 1, 0))

    packed = (s["groups"], height + 2 * halo, breadth)
    first, second = call(
        functools.partial(pack_kernel, s), (sds(packed, F32), sds(packed, F32)), inputs=[vmem] * 3
    )(observed, from_even, from_odd)
    first_pairs, second_pairs = pairings(lax.axis_size("gx"))
    got_first = lax.ppermute(first, "gx", first_pairs)
    got_second = lax.ppermute(second, "gx", second_pairs)

    big = (2, layers, rows, breadth)
    low, high = reach(s, 2 * s["radius"])
    wide = (2, layers, (high - low) * SUB, breadth)
    tile = sds((layers, height, breadth), F32)
    x1, g1, pull, again, part = call(
        functools.partial(main_kernel, s),
        (sds(wide, F32), sds(wide, F32), tile, tile, sds((n, breadth), F32)),
        scratch=[pltpu.VMEM(shape, F32) for shape in [big] * 3 + [big[1:]] + [big] * 12],
        inputs=[vmem] * 8,
    )(observed, from_even, from_odd, got_first, got_second, taps_all, forward, backward)
    sums = lax.all_to_all(part, ("gy", "gx"), 0, 0, tiled=True)
    work = pltpu.VMEM((2, layers, (high - low + 1) * SUB, breadth), F32)
    x2, g2, part, keep = call(
        functools.partial(step_kernel, s),
        (tile, tile, sds((n, breadth), F32), sds((SUB, breadth), F32)),
        scratch=[work] * 3,
        inputs=[vmem] * 5,
    )(sums, x1, g1, pull, again)
    sums = lax.all_to_all(part, ("gy", "gx"), 0, 0, tiled=True)
    return call(final_kernel, tile, inputs=[vmem] * 4)(sums, keep, x2, g2)


def solution(mesh):
    in_specs = (P(None, "gy", "gx"), P(), P())
    out_specs = P(None, "gy", "gx")
    return jax.shard_map(
        per_device, mesh=mesh, in_specs=in_specs, out_specs=out_specs, check_vma=False
    )
```

```python
import functools
import jax
import jax.numpy as jnp
from jax import lax
from jax.experimental import pallas as pl
from jax.experimental.pallas import tpu as pltpu
from jax.sharding import PartitionSpec as P

ITERS = 2
WEIGHT_TV = 0.02
SMOOTHING = 0.1
DAMPING = 0.05
START_STEP = 0.5
SUB = 8
F32 = jnp.float32
BF16 = jnp.bfloat16
VMEM_BYTES = 44 * 1024 * 1024


def plan(layers, height, breadth, taps):
    radius = (taps - 1) // 2
    halo = 6 * radius
    off = -(-halo // SUB) * SUB + SUB
    return dict(
        layers=layers, height=height, breadth=breadth, taps=taps, radius=radius, halo=halo, off=off,
        rows=height + 2 * off, groups=-(-layers * halo // breadth), first=off // SUB, last=(off + height) // SUB,
        tiles=(height + 2 * off) // SUB,
    )


def reach(s, extent):
    low = (s["off"] - extent) // SUB
    high = -(-(s["off"] + s["height"] + extent) // SUB)
    return low, high


def bands(s):
    return ((0, s["first"]), (s["first"], s["last"]), (s["last"], s["tiles"]))


def place():
    return lax.axis_index("gy"), lax.axis_index("gx"), lax.axis_size("gy"), lax.axis_size("gx")


def weights_kernel(s, index_ref, profiles_ref, after_ref, taps_ref, forward_ref, backward_ref, full):
    gy, gx, ny, nx = place()
    breadth, taps, radius = s["breadth"], s["taps"], s["radius"]
    ring = 2 * breadth
    lane = lax.broadcasted_iota(jnp.int32, (SUB, breadth), 1)
    chunk = 32

    def split(value):
        upper = value.astype(BF16)
        return upper, (value - upper.astype(F32)).astype(BF16)

    for band in range(3):
        row = gy + (band - 1)
        picked = []
        for side in range(3):
            col = gx + (side - 1)
            inside = (row >= 0) & (row < ny) & (col >= 0) & (col < nx)
            number = index_ref[jnp.clip(row, 0, ny - 1), jnp.clip(col, 0, nx - 1)]
            picked.append((inside, number))
        columns = []
        for dim in range(3):
            for tap in range(taps):
                left, centre, right = [
                    jnp.where(inside, profiles_ref[tap, dim, number], 0.0) for inside, number in picked
                ]
                main = jnp.full((SUB, breadth), centre, F32)
                side = jnp.where(lane < breadth // 2, right, left)
                if dim < 2:
                    taps_ref[band, dim, 0, tap] = main
                    taps_ref[band, dim, 1, tap] = side
                else:
                    columns.append(jnp.concatenate([main, side], axis=1)[:1])

        def build(piece, carry, band=band, columns=columns):
            start = pl.multiple_of(piece * chunk, chunk)
            source = lax.broadcasted_iota(jnp.int32, (chunk, ring), 0) + start
            target = lax.broadcasted_iota(jnp.int32, (chunk, ring), 1)
            distance = target - source + radius
            distance = jnp.where(distance < 0, distance + ring, distance)
            distance = jnp.where(distance >= ring, distance - ring, distance)
            total = jnp.zeros((chunk, ring), F32)
            for tap in range(taps):
                total = jnp.where(distance == tap, columns[tap], total)
            full[pl.ds(start, chunk), :] = total
            return carry

        lax.fori_loop(0, ring // chunk, build, 0)
        value = full[...]
        for ref, matrix in ((forward_ref, value), (backward_ref, value.T)):
            upper, lower = split(matrix)
            ref[band, :ring, :] = upper
            ref[band, ring:2 * ring, :] = lower
            ref[band, 2 * ring:, :] = upper


def strip_places(s, layer):
    group, lane = divmod(layer * s["halo"], s["breadth"])
    return group, lane, min(s["halo"], s["breadth"] - lane)


def copy_kernel(tile_ref, out_ref):
    out_ref[...] = tile_ref[...]


def pack_kernel(s, tile_ref, even_ref, odd_ref, first_ref, second_ref, centre_ref):
    gy, gx, _, _ = place()
    halo, height, breadth = s["halo"], s["height"], s["breadth"]
    row_even, col_even = lax.rem(gy, 2) == 0, lax.rem(gx, 2) == 0
    lane = lax.broadcasted_iota(jnp.int32, (1, breadth), 1)
    for start, count in ((0, halo), (halo, height), (halo + height, halo)):
        first = [jnp.zeros((count, breadth), F32)] * s["groups"]
        second = list(first)
        for layer in range(s["layers"]):
            if start == halo:
                value = tile_ref[layer]
            elif start == 0:
                value = jnp.where(row_even, odd_ref[layer], even_ref[layer])
            else:
                value = jnp.where(row_even, even_ref[layer], odd_ref[layer])
            centre_ref[layer, start:start + count, :] = value
            group, begin, here = strip_places(s, layer)
            from_left, from_right = begin, (begin + halo) % breadth
            to_first = pltpu.roll(value, jnp.where(col_even, from_right, from_left), 1)
            to_second = pltpu.roll(value, jnp.where(col_even, from_left, from_right), 1)
            parts = [(group, (lane >= begin) & (lane < begin + here))]
            if here < halo:
                parts.append((group + 1, lane < halo - here))
            for number, mine in parts:
                first[number] = jnp.where(mine, to_first, first[number])
                second[number] = jnp.where(mine, to_second, second[number])
        for number in range(s["groups"]):
            first_ref[number, start:start + count, :] = first[number]
            second_ref[number, start:start + count, :] = second[number]


def unpack_layer(s, groups, layer, to):
    breadth = s["breadth"]
    lane = lax.broadcasted_iota(jnp.int32, (1, breadth), 1)
    group, begin, here = strip_places(s, layer)
    value = groups[group]
    if here < s["halo"]:
        value = jnp.where(lane >= begin, value, groups[group + 1])
    shift = (to - begin) % breadth
    return pltpu.roll(value, shift, 1) if shift else value


def row_depth(s, load, row_taps, depth_taps, transposed):
    layers, taps, radius = s["layers"], s["taps"], s["radius"]
    mixed = []
    for layer in range(layers):
        total = None
        for tap in range(taps):
            term = row_taps[tap] * load(layer, tap - radius if transposed else radius - tap)
            total = term if total is None else total + term
        mixed.append(total)
    outs = []
    for layer in range(layers):
        total = None
        for tap in range(taps):
            shift = tap - radius if transposed else radius - tap
            if 0 <= layer + shift < layers:
                term = depth_taps[tap] * mixed[layer + shift]
                total = term if total is None else total + term
        outs.append(total)
    return outs


def slope_tile(s, source, shift, tile, divergence, flux_rows, where):
    gy, gx, ny, nx = where
    layers, height, breadth = s["layers"], s["height"], s["breadth"]
    ring = 2 * breadth
    lane = lax.broadcasted_iota(jnp.int32, (SUB, ring), 1)
    col = gx * breadth + jnp.where(lane < breadth + breadth // 2, lane, lane - ring)
    col_mask = jnp.where((col >= 0) & (col < nx * breadth - 1), 1.0, 0.0).astype(F32)
    start = tile * SUB
    row = gy * height + start - s["off"] + shift + lax.broadcasted_iota(jnp.int32, (SUB, ring), 0)
    row_mask = jnp.where((row >= 0) & (row < ny * height - 1), 1.0, 0.0).astype(F32)

    def load(layer, begin):
        return jnp.concatenate([source[half, layer, begin:begin + SUB, :] for half in range(2)], axis=1)

    here = load(0, start)
    flux_before = None
    for layer in range(layers):
        below = load(layer, start + 1)
        step_rows = (below - here) * row_mask
        step_cols = (pltpu.roll(here, ring - 1, 1) - here) * col_mask
        square = step_rows * step_rows + step_cols * step_cols + SMOOTHING * SMOOTHING
        if layer + 1 < layers:
            after = load(layer + 1, start)
            step_depth = after - here
            square = square + step_depth * step_depth
        inverse = lax.rsqrt(square)
        f_rows, f_cols = step_rows * inverse, step_cols * inverse
        total = pltpu.roll(f_cols, 1, 1) - f_cols - f_rows
        if flux_before is not None:
            total = total + flux_before
        if layer + 1 < layers:
            flux_before = step_depth * inverse
            total = total - flux_before
            here = after
        for half in range(2):
            part = slice(half * breadth, (half + 1) * breadth)
            divergence[half, layer, start:start + SUB, :] = total[:, part]
            flux_rows[half, layer, start:start + SUB, :] = f_rows[:, part]


def main_kernel(s, centre_ref, first_ref, second_ref, taps_ref, forward_ref, backward_ref,
                x1_ref, g1_ref, pull_ref, again_ref, part_ref,
                x0, x1, x2, g0, y0, y1, y2, r0, r1, r2, q0, q1, q2, acc, div, flux):
    where = place()
    gy, gx, ny, nx = where
    layers, height, breadth, off = s["layers"], s["height"], s["breadth"], s["off"]
    halo, radius, taps = s["halo"], s["radius"], s["taps"]
    begin, end = s["first"], s["last"]
    col_even = lax.rem(gx, 2) == 0
    lane = lax.broadcasted_iota(jnp.int32, (1, breadth), 1)
    xs, ys, rs, qs = (x0, x1, x2), (y0, y1, y2), (r0, r1, r2), (q0, q1, q2)
    span = bands(s)

    def rows(tile, stop=None):
        return slice(tile * SUB, (tile + 1 if stop is None else stop) * SUB)

    top = off - halo
    x0[0, :, top:off + height + halo, :] = centre_ref[...]
    firsts = [first_ref[g] for g in range(s["groups"])]
    seconds = [second_ref[g] for g in range(s["groups"])]
    rights = [jnp.where(col_even, a, b) for a, b in zip(firsts, seconds)]
    lefts = [jnp.where(col_even, b, a) for a, b in zip(firsts, seconds)]
    for layer in range(layers):
        value = jnp.where(lane < halo, unpack_layer(s, rights, layer, 0), 0.0)
        value = jnp.where(lane >= breadth - halo, unpack_layer(s, lefts, layer, breadth - halo), value)
        x0[1, layer, top:off + height + halo, :] = value
    zero = jnp.zeros((2, layers, SUB, breadth), F32)
    for ref, tiles in ((y0, (0,)), (y2, (s["tiles"] - 1,)), (r0, (begin, begin + 1)),
                       (r1, (begin - 2, begin - 1, end, end + 1)), (r2, (end - 2, end - 1))):
        for tile in tiles:
            ref[:, :, rows(tile), :] = zero

    def chunk(ref, low, high):
        value = jnp.concatenate(
            [ref[half, :, rows(low, high), :].reshape(layers * (high - low) * SUB, breadth) for half in range(2)], axis=1)
        upper = value.astype(BF16)
        lower = (value - upper.astype(F32)).astype(BF16)
        return jnp.concatenate([upper, upper, lower], axis=1)

    def halves(result, low, high):
        return [result[:, h * breadth:(h + 1) * breadth].reshape(layers, (high - low) * SUB, breadth) for h in range(2)]

    def taps_of(band, half):
        return [[taps_ref[band, dim, half, t] for t in range(taps)] for dim in (1, 0)]

    def one_pass(number):
        x = xs[number]
        low, high = reach(s, (5 - 2 * number) * radius)
        in_low, in_high = reach(s, (6 - 2 * number) * radius)
        back_low, back_high = reach(s, (4 - 2 * number) * radius)
        out = [(max(low, a), min(high, b)) for a, b in span]
        back = [(max(back_low, a - 1), min(back_high, b + 1)) for a, b in span]
        done = set()

        def columns(band):
            a, b = max(out[band][0] - 1, in_low), min(out[band][1] + 1, in_high)
            result = jnp.dot(chunk(x, a, b), forward_ref[band], preferred_element_type=F32)
            for half, piece in enumerate(halves(result, a, b)):
                ys[band][half, :, rows(a, b), :] = piece

        def blur_rows(band):
            for tile in range(*out[band]):
                for half in range(2):
                    load = lambda layer, shift: ys[band][half, layer, tile * SUB + shift:(tile + 1) * SUB + shift, :]
                    outs = row_depth(s, load, *taps_of(band, half), False)
                    for layer in range(layers):
                        value = outs[layer] if number == 2 else outs[layer] - x0[half, layer, rows(tile), :]
                        rs[band][half, layer, rows(tile), :] = value

        def back_rows(band):
            for tile in range(*back[band]):
                for half in range(2):
                    load = lambda layer, shift: rs[band][half, layer, tile * SUB + shift:(tile + 1) * SUB + shift, :]
                    outs = row_depth(s, load, *taps_of(band, half), True)
                    for layer in range(layers):
                        qs[band][half, layer, rows(tile), :] = outs[layer]

        def back_columns(band):
            a, b = back[band]
            result = jnp.dot(chunk(qs[band], a, b), backward_ref[band], preferred_element_type=F32)
            for half, piece in enumerate(halves(result, a, b)):
                for tile in range(a, b):
                    part = piece[:, (tile - a) * SUB:(tile - a + 1) * SUB, :]
                    acc[half, :, rows(tile), :] = acc[half, :, rows(tile), :] + part if tile in done else part
            done.update(range(a, b))

        def inside(tile, half):
            row = gy * height + tile * SUB - off + lax.broadcasted_iota(jnp.int32, (SUB, breadth), 0)
            here = lax.broadcasted_iota(jnp.int32, (SUB, breadth), 1)
            if half == 1:
                here = jnp.where(here < breadth // 2, here + breadth, here - breadth)
            col = gx * breadth + here
            return (row >= 0) & (row < ny * height) & (col >= 0) & (col < nx * breadth)

        def update(tile):
            for half in range(2):
                keep = inside(tile, half)
                for layer in range(layers):
                    here = x[half, layer, rows(tile), :]
                    total = acc[half, layer, rows(tile), :] + DAMPING * here
                    before = flux[half, layer, tile * SUB - 1:(tile + 1) * SUB - 1, :]
                    total = total + WEIGHT_TV * (div[half, layer, rows(tile), :] + before)
                    total = jnp.where(keep, total, 0.0)
                    if number == 0:
                        xs[1][half, layer, rows(tile), :] = here - START_STEP * total
                        if half == 0 and begin <= tile < end:
                            g0[layer, rows(tile), :] = total
                    else:
                        xs[2][half, layer, rows(tile), :] = total

        def slopes(a, b):
            if number < 2:
                for tile in range(a, b):
                    slope_tile(s, x, 0, tile, div, flux, where)

        middle = (begin + end) // 2
        columns(0)
        slopes(back_low - 1, middle)
        columns(1)
        blur_rows(0)
        columns(2)
        back_rows(0)
        blur_rows(1)
        back_columns(0)
        back_rows(1)
        back_columns(1)
        blur_rows(2)
        slopes(middle, back_high)
        back_rows(2)
        back_columns(2)
        if number == 1:
            pull_ref[...] = acc[0, :, rows(begin, end), :]
        if number < 2:
            for tile in range(back_low, back_high):
                update(tile)

    for number in range(3):
        one_pass(number)
    again_ref[...] = acc[0, :, rows(begin, end), :]
    low, high = reach(s, 2 * radius)
    x1_ref[...] = x1[:, :, rows(low, high), :]
    g1_ref[...] = x2[:, :, rows(low, high), :]

    zero_sq = cross = one_sq = jnp.zeros((SUB, breadth), F32)
    for tile in range(begin, end):
        for layer in range(layers):
            a, b = g0[layer, rows(tile), :], x2[0, layer, rows(tile), :]
            zero_sq, cross, one_sq = zero_sq + a * a, cross + a * (b - a), one_sq + b * b
    zero_sq, cross, one_sq = [jnp.sum(t, axis=(0, 1), keepdims=True) for t in (zero_sq, cross, one_sq)]
    row = jnp.where(lane == 0, zero_sq, jnp.where(lane == 1, cross, one_sq))
    part_ref[...] = jnp.broadcast_to(row, part_ref.shape)


def step_kernel(s, sums_ref, x1_ref, g1_ref, pull_ref, again_ref, x2_ref, g2_ref, part_ref, keep_ref, x2, div, flux):
    where = place()
    layers, height, breadth = s["layers"], s["height"], s["breadth"]
    low, high = reach(s, 2 * s["radius"])
    lane = lax.broadcasted_iota(jnp.int32, (1, breadth), 1)
    total = jnp.sum(sums_ref[...], axis=0, keepdims=True)
    zero_sq, cross, one_sq = [
        jnp.sum(jnp.where(lane == number, total, 0.0), axis=(0, 1), keepdims=True) for number in range(3)
    ]
    step = (START_STEP * START_STEP * zero_sq) / (-START_STEP * cross)
    count = (high - low) * SUB
    for half in range(2):
        for layer in range(layers):
            x2[half, layer, :count, :] = x1_ref[half, layer] - step * g1_ref[half, layer]
    begin = s["first"] - low
    total = jnp.zeros((SUB, breadth), F32)
    for tile in range(begin - 1, begin + height // SUB):
        slope_tile(s, x2, low * SUB, tile, div, flux, where)
        if tile < begin:
            continue
        at, out = slice(tile * SUB, (tile + 1) * SUB), slice((tile - begin) * SUB, (tile - begin + 1) * SUB)
        for layer in range(layers):
            here = x2[0, layer, at, :]
            slope = pull_ref[layer, out, :] - step * again_ref[layer, out, :] + DAMPING * here
            slope = slope + WEIGHT_TV * (div[0, layer, at, :] + flux[0, layer, tile * SUB - 1:(tile + 1) * SUB - 1, :])
            x2_ref[layer, out, :] = here
            g2_ref[layer, out, :] = slope
            old = g1_ref[0, layer, at, :]
            total = total + old * (slope - old)
    growth = -step * jnp.sum(total, axis=(0, 1), keepdims=True)
    part_ref[...] = jnp.broadcast_to(growth, part_ref.shape)
    keep_ref[...] = jnp.broadcast_to(step * step * one_sq, keep_ref.shape)


def final_kernel(sums_ref, keep_ref, x2_ref, g2_ref, out_ref):
    step = keep_ref[:1, :] / jnp.sum(sums_ref[...], axis=0, keepdims=True)
    for layer in range(x2_ref.shape[0]):
        out_ref[layer] = x2_ref[layer] - step * g2_ref[layer]


def pairings(count):
    def both(start):
        pairs = []
        for i in range(start, count - 1, 2):
            pairs += [(i, i + 1), (i + 1, i)]
        return pairs

    return both(0), both(1)


def call(kernel, outs, scratch=(), inputs=None):
    whole = pl.BlockSpec(memory_space=pltpu.VMEM)
    return pl.pallas_call(
        kernel,
        out_shape=outs,
        in_specs=inputs,
        out_specs=jax.tree.map(lambda _: whole, outs),
        scratch_shapes=list(scratch),
        compiler_params=pltpu.CompilerParams(vmem_limit_bytes=VMEM_BYTES),
    )


def per_device(observed, profiles, tile_index):
    layers, height, breadth = observed.shape
    s = plan(layers, height, breadth, profiles.shape[2])
    halo, rows, taps = s["halo"], s["rows"], s["taps"]
    ring = 2 * breadth
    gy = lax.axis_index("gy")
    n = lax.axis_size("gy") * lax.axis_size("gx")
    vmem, smem = pl.BlockSpec(memory_space=pltpu.VMEM), pl.BlockSpec(memory_space=pltpu.SMEM)
    sds = jax.ShapeDtypeStruct

    even = lax.rem(gy, 2) == 0
    bottom, top = jnp.int32(height - halo), jnp.int32(0)
    to_even = lax.dynamic_slice_in_dim(observed, jnp.where(even, bottom, top), halo, axis=1)
    to_odd = lax.dynamic_slice_in_dim(observed, jnp.where(even, top, bottom), halo, axis=1)
    first_pairs, second_pairs = pairings(lax.axis_size("gy"))
    from_even = lax.ppermute(to_even, "gy", first_pairs)
    from_odd = lax.ppermute(to_odd, "gy", second_pairs)

    packed = (s["groups"], height + 2 * halo, breadth)
    tile_here = call(copy_kernel, sds(observed.shape, F32), inputs=[vmem])(observed)
    first, second, centre = call(
        functools.partial(pack_kernel, s),
        (sds(packed, F32), sds(packed, F32), sds((layers, height + 2 * halo, breadth), F32)),
        inputs=[vmem] * 3,
    )(tile_here, from_even, from_odd)
    taps_all, forward, backward = call(
        functools.partial(weights_kernel, s),
        (sds((3, 2, 2, taps, SUB, breadth), F32), sds((3, 3 * ring, ring), BF16), sds((3, 3 * ring, ring), BF16)),
        scratch=[pltpu.VMEM((ring, ring), F32)],
        inputs=[smem, smem, pl.BlockSpec(memory_space=pl.ANY)],
    )(tile_index, profiles.transpose(2, 1, 0), second)
    first, taps_all = lax.optimization_barrier((first, taps_all))
    first_pairs, second_pairs = pairings(lax.axis_size("gx"))
    got_first = lax.ppermute(first, "gx", first_pairs)
    got_second = lax.ppermute(second, "gx", second_pairs)

    big = (2, layers, rows, breadth)
    low, high = reach(s, 2 * s["radius"])
    wide = (2, layers, (high - low) * SUB, breadth)
    tile = sds((layers, height, breadth), F32)
    x1, g1, pull, again, part = call(
        functools.partial(main_kernel, s),
        (sds(wide, F32), sds(wide, F32), tile, tile, sds((n, breadth), F32)),
        scratch=[pltpu.VMEM(shape, F32) for shape in [big] * 3 + [big[1:]] + [big] * 12],
        inputs=[vmem] * 6,
    )(centre, got_first, got_second, taps_all, forward, backward)
    sums = lax.all_to_all(part, ("gy", "gx"), 0, 0, tiled=True)
    work = pltpu.VMEM((2, layers, (high - low + 1) * SUB, breadth), F32)
    x2, g2, part, keep = call(
        functools.partial(step_kernel, s),
        (tile, tile, sds((n, breadth), F32), sds((SUB, breadth), F32)),
        scratch=[work] * 3,
        inputs=[vmem] * 5,
    )(sums, x1, g1, pull, again)
    sums = lax.all_to_all(part, ("gy", "gx"), 0, 0, tiled=True)
    return call(final_kernel, tile, inputs=[vmem] * 4)(sums, keep, x2, g2)


def solution(mesh):
    in_specs = (P(None, "gy", "gx"), P(), P())
    out_specs = P(None, "gy", "gx")
    return jax.shard_map(
        per_device, mesh=mesh, in_specs=in_specs, out_specs=out_specs, check_vma=False
    )
```

```python
import functools
import jax
import jax.numpy as jnp
from jax import lax
from jax.experimental import pallas as pl
from jax.experimental.pallas import tpu as pltpu
from jax.sharding import PartitionSpec as P

ITERS = 2
WEIGHT_TV = 0.02
SMOOTHING = 0.1
DAMPING = 0.05
START_STEP = 0.5
SUB = 8
F32 = jnp.float32
BF16 = jnp.bfloat16
VMEM_BYTES = 36 * 1024 * 1024


def plan(layers, height, breadth, taps):
    radius = (taps - 1) // 2
    halo = 6 * radius
    off = -(-halo // SUB) * SUB + SUB
    return dict(
        layers=layers, height=height, breadth=breadth, taps=taps, radius=radius, halo=halo, off=off,
        rows=height + 2 * off, groups=-(-layers * halo // breadth), pairs=layers // 2, planes=layers + layers // 2, quarter=breadth // 4, first=off // SUB, last=(off + height) // SUB,
        tiles=(height + 2 * off) // SUB,
    )


def reach(s, extent):
    low = (s["off"] - extent) // SUB
    high = -(-(s["off"] + s["height"] + extent) // SUB)
    return low, high


def bands(s):
    return ((0, s["first"]), (s["first"], s["last"]), (s["last"], s["tiles"]))


def place():
    return lax.axis_index("gy"), lax.axis_index("gx"), lax.axis_size("gy"), lax.axis_size("gx")


def column_of(s, place, member):
    breadth, quarter = s["breadth"], s["quarter"]
    side = place - breadth
    right, left = (0, 3 * quarter) if member == 0 else (2 * quarter, quarter)
    column = jnp.where((side >= right) & (side < right + quarter), breadth + side - right, 1 << 20)
    column = jnp.where((side >= left) & (side < left + quarter), side - left - quarter, column)
    return jnp.where(place < breadth, place, column)


def weights_kernel(s, index_ref, profiles_ref, taps_ref, columns_ref):
    gy, gx, ny, nx = place()
    breadth, taps = s["breadth"], s["taps"]
    lane = lax.broadcasted_iota(jnp.int32, (SUB, breadth), 1)
    is_right = lax.rem(lane // s["quarter"], 2) == 0
    for band in range(3):
        row = gy + (band - 1)
        picked = []
        for side in range(3):
            col = gx + (side - 1)
            inside = (row >= 0) & (row < ny) & (col >= 0) & (col < nx)
            number = index_ref[jnp.clip(row, 0, ny - 1), jnp.clip(col, 0, nx - 1)]
            picked.append((inside, number))
        for dim in range(3):
            for tap in range(taps):
                left, centre, right = [
                    jnp.where(inside, profiles_ref[tap, dim, number], 0.0) for inside, number in picked
                ]
                own, side = jnp.full((SUB, breadth), centre, F32), jnp.where(is_right, right, left)
                if dim < 2:
                    taps_ref[band, dim, 0, tap] = own
                    taps_ref[band, dim, 1, tap] = side
                else:
                    columns_ref[band, tap] = jnp.concatenate([own, side], axis=1)


def matrices_kernel(s, columns_ref, after_ref, forward_ref, backward_ref, full):
    breadth, taps, radius = s["breadth"], s["taps"], s["radius"]
    ring = 2 * breadth
    chunk = 32
    target = lax.broadcasted_iota(jnp.int32, (1, ring), 1)
    for number in range(6):
        band, member = divmod(number, 2)
        columns = [columns_ref[band, t, :1, :] for t in range(taps)]
        reached = column_of(s, target, member)
        reached = jnp.where(reached < 1 << 19, reached + radius, -(1 << 20))
        for start in range(0, ring, chunk):
            source = lax.broadcasted_iota(jnp.int32, (chunk, 1), 0) + start
            distance = reached - column_of(s, source, member)
            total = jnp.zeros((chunk, ring), F32)
            for tap in range(taps):
                total = jnp.where(distance == tap, columns[tap], total)
            full[start:start + chunk, :] = total
        matrix = full[...]
        for ref, value in ((forward_ref, matrix), (backward_ref, matrix.T)):
            upper = value.astype(BF16)
            ref[number, :ring, :] = upper
            ref[number, ring:2 * ring, :] = (value - upper.astype(F32)).astype(BF16)
            ref[number, 2 * ring:, :] = upper


def strip_places(s, layer):
    group, lane = divmod(layer * s["halo"], s["breadth"])
    return group, lane, min(s["halo"], s["breadth"] - lane)


def copy_kernel(tile_ref, out_ref):
    out_ref[...] = tile_ref[...]


def pack_kernel(s, tile_ref, even_ref, odd_ref, after_ref, first_ref, second_ref, centre_ref):
    gy, gx, _, _ = place()
    halo, height, breadth = s["halo"], s["height"], s["breadth"]
    row_even, col_even = lax.rem(gy, 2) == 0, lax.rem(gx, 2) == 0
    lane = lax.broadcasted_iota(jnp.int32, (1, breadth), 1)
    for start, count in ((0, halo), (halo, height), (halo + height, halo)):
        first = [jnp.zeros((count, breadth), F32)] * s["groups"]
        second = list(first)
        for layer in range(s["layers"]):
            if start == halo:
                value = tile_ref[layer]
            elif start == 0:
                value = jnp.where(row_even, odd_ref[layer], even_ref[layer])
            else:
                value = jnp.where(row_even, even_ref[layer], odd_ref[layer])
            centre_ref[layer, start:start + count, :] = value
            group, begin, here = strip_places(s, layer)
            from_left, from_right = begin, (begin + halo) % breadth
            to_first = pltpu.roll(value, jnp.where(col_even, from_right, from_left), 1)
            to_second = pltpu.roll(value, jnp.where(col_even, from_left, from_right), 1)
            parts = [(group, (lane >= begin) & (lane < begin + here))]
            if here < halo:
                parts.append((group + 1, lane < halo - here))
            for number, mine in parts:
                first[number] = jnp.where(mine, to_first, first[number])
                second[number] = jnp.where(mine, to_second, second[number])
        for number in range(s["groups"]):
            first_ref[number, start:start + count, :] = first[number]
            second_ref[number, start:start + count, :] = second[number]


def unpack_layer(s, groups, layer, to):
    breadth = s["breadth"]
    lane = lax.broadcasted_iota(jnp.int32, (1, breadth), 1)
    group, begin, here = strip_places(s, layer)
    value = groups[group]
    if here < s["halo"]:
        value = jnp.where(lane >= begin, value, groups[group + 1])
    shift = (to - begin) % breadth
    return pltpu.roll(value, shift, 1) if shift else value


def first_lanes(s):
    lane = lax.broadcasted_iota(jnp.int32, (1, s["breadth"]), 1)
    return (lane < s["quarter"]) | (lane >= 3 * s["quarter"])


def swap_layers(s, value):
    return pltpu.roll(value, 2 * s["quarter"], 1)


def weighted(taps, values):
    total = None
    for tap, value in zip(taps, values):
        if value is not None:
            total = tap * value if total is None else total + tap * value
    return total


def row_depth(s, load, side, row_taps, depth_taps, transposed):
    layers, taps, radius, pairs = s["layers"], s["taps"], s["radius"], s["pairs"]
    shifts = [t - radius if transposed else radius - t for t in range(taps)]
    base, count = (layers, pairs) if side else (0, layers)
    mixed = [weighted(row_taps, [load(base + p, shift) for shift in shifts]) for p in range(count)]
    beyond = {}
    if side:
        first = first_lanes(s)
        for step in range(1, radius + 1):
            beyond[-step] = jnp.where(first, 0.0, swap_layers(s, mixed[pairs - step]))
            beyond[pairs - 1 + step] = jnp.where(first, swap_layers(s, mixed[step - 1]), 0.0)
    at = lambda p: mixed[p] if 0 <= p < count else beyond.get(p)
    return [weighted(depth_taps, [at(p + shift) for shift in shifts]) for p in range(count)]


def slope_tile(s, source, shift, tile, divergence, flux_rows, where):
    gy, gx, ny, nx = where
    layers, height, breadth, pairs, quarter = s["layers"], s["height"], s["breadth"], s["pairs"], s["quarter"]
    lane = lax.broadcasted_iota(jnp.int32, (SUB, breadth), 1)
    side_col = jnp.where(lax.rem(lane // quarter, 2) == 0, breadth + lax.rem(lane, quarter), lax.rem(lane, quarter) - quarter)
    masks = []
    for col in (lane, side_col):
        col = gx * breadth + col
        masks.append(jnp.where((col >= 0) & (col < nx * breadth - 1), 1.0, 0.0).astype(F32))
    start = tile * SUB
    row = gy * height + start - s["off"] + shift + lax.broadcasted_iota(jnp.int32, (SUB, breadth), 0)
    row_mask = jnp.where((row >= 0) & (row < ny * height - 1), 1.0, 0.0).astype(F32)
    last, first = breadth - 1, first_lanes(s)
    rows = slice(start, start + SUB)

    def swap(value):
        return swap_layers(s, value)

    before = [None, None, None]
    heres = [source[plane, rows, :] for plane in (0, pairs, layers)]
    for p in range(pairs):
        planes = (p, p + pairs, layers + p)
        afters = [source[plane + 1, rows, :] if p + 1 < pairs else None for plane in planes]
        if p + 1 == pairs:
            afters[0] = source[pairs, rows, :]
            afters[2] = jnp.where(first, swap(source[layers, rows, :]), heres[2])
        rolled = [pltpu.roll(value, breadth - 1, 1) for value in heres]
        nexts = [
            jnp.where(lane == last, rolled[2], rolled[0]),
            jnp.where(lane == last, swap(rolled[2]), rolled[1]),
            jnp.where(lane == last, rolled[0], jnp.where(lane == 2 * quarter - 1, swap(rolled[1]), rolled[2])),
        ]
        f_cols, totals = [], []
        for k, plane in enumerate(planes):
            here = heres[k]
            step_rows = (source[plane, start + 1:start + 1 + SUB, :] - here) * row_mask
            step_cols = (nexts[k] - here) * masks[k // 2]
            square = step_rows * step_rows + step_cols * step_cols + SMOOTHING * SMOOTHING
            if afters[k] is not None:
                step_depth = afters[k] - here
                square = square + step_depth * step_depth
            inverse = lax.rsqrt(square)
            f_rows = step_rows * inverse
            flux_rows[plane, rows, :] = f_rows
            f_cols.append(step_cols * inverse)
            total = -f_cols[k] - f_rows
            if before[k] is not None:
                total = total + before[k]
            before[k] = None
            if afters[k] is not None:
                before[k] = step_depth * inverse
                total = total - before[k]
            totals.append(total)
        rolled = [pltpu.roll(value, 1, 1) for value in f_cols]
        totals[0] = totals[0] + jnp.where(lane == 0, rolled[2], rolled[0])
        totals[1] = totals[1] + jnp.where(lane == 0, swap(rolled[2]), rolled[1])
        totals[2] = totals[2] + jnp.where(lane == 0, rolled[0], jnp.where(lane == 2 * quarter, swap(rolled[1]), rolled[2]))
        for plane, total in zip(planes, totals):
            divergence[plane, rows, :] = total
        heres = afters
    divergence[pairs, rows, :] = divergence[pairs, rows, :] + before[0]
    divergence[layers, rows, :] = divergence[layers, rows, :] + jnp.where(first, 0.0, swap(before[2]))


def main_kernel(s, centre_ref, first_ref, second_ref, taps_ref, forward_ref, backward_ref,
                x1_ref, g1_ref, pull_ref, again_ref, part_ref,
                x0, x1, x2, g0, y0, y1, y2, r0, r1, r2, q0, q1, q2, acc, div, flux):
    where = place()
    gy, gx, ny, nx = where
    layers, height, breadth, off = s["layers"], s["height"], s["breadth"], s["off"]
    halo, radius, taps, pairs, planes, quarter = [s[k] for k in ("halo", "radius", "taps", "pairs", "planes", "quarter")]
    begin, end = s["first"], s["last"]
    col_even = lax.rem(gx, 2) == 0
    lane = lax.broadcasted_iota(jnp.int32, (1, breadth), 1)
    xs, ys, rs, qs = (x0, x1, x2), (y0, y1, y2), (r0, r1, r2), (q0, q1, q2)
    span = bands(s)

    def rows(tile, stop=None):
        return slice(tile * SUB, (tile + 1 if stop is None else stop) * SUB)

    top = off - halo
    x0[:layers, top:off + height + halo, :] = centre_ref[...]
    firsts = [first_ref[g] for g in range(s["groups"])]
    seconds = [second_ref[g] for g in range(s["groups"])]
    rights = [jnp.where(col_even, a, b) for a, b in zip(firsts, seconds)]
    lefts = [jnp.where(col_even, b, a) for a, b in zip(firsts, seconds)]
    for p in range(pairs):
        value = jnp.zeros((height + 2 * halo, breadth), F32)
        for groups, layer, to in ((rights, p, 0), (lefts, p + pairs, 2 * quarter - halo),
                                  (rights, p + pairs, 2 * quarter), (lefts, p, breadth - halo)):
            value = jnp.where((lane >= to) & (lane < to + halo), unpack_layer(s, groups, layer, to), value)
        x0[layers + p, top:off + height + halo, :] = value
    zero = jnp.zeros((planes, SUB, breadth), F32)
    for ref, tiles in ((y0, (0,)), (y2, (s["tiles"] - 1,)), (r0, (begin, begin + 1)),
                       (r1, (begin - 2, begin - 1, end, end + 1)), (r2, (end - 2, end - 1))):
        for tile in tiles:
            ref[:, rows(tile), :] = zero

    def product(ref, low, high, band, matrices):
        count = (high - low) * SUB

        def split(a, b):
            value = ref[a:b, rows(low, high), :].reshape((b - a) * count, breadth)
            upper = value.astype(BF16)
            return upper, (value - upper.astype(F32)).astype(BF16)

        side_high, side_low = split(layers, planes)
        own, side = [], None
        for member in range(2):
            high_part, low_part = split(member * pairs, (member + 1) * pairs)
            parts = [high_part, side_high] * 2 + [low_part, side_low]
            result = jnp.dot(jnp.concatenate(parts, axis=1), matrices[2 * band + member], preferred_element_type=F32)
            own.append(result[:, :breadth].reshape(pairs, count, breadth))
            rest = result[:, breadth:]
            side = rest if side is None else side + rest
        return [(0, own[0]), (pairs, own[1]), (layers, side.reshape(pairs, count, breadth))]

    def taps_of(band, half):
        return [[taps_ref[band, dim, half, t] for t in range(taps)] for dim in (1, 0)]

    def one_pass(number):
        x = xs[number]
        low, high = reach(s, (5 - 2 * number) * radius)
        in_low, in_high = reach(s, (6 - 2 * number) * radius)
        back_low, back_high = reach(s, (4 - 2 * number) * radius)
        out = [(max(low, a), min(high, b)) for a, b in span]
        back = [(max(back_low, a - 1), min(back_high, b + 1)) for a, b in span]
        done = set()

        def columns(band):
            a, b = max(out[band][0] - 1, in_low), min(out[band][1] + 1, in_high)
            for plane, piece in product(x, a, b, band, forward_ref):
                ys[band][plane:plane + pairs, rows(a, b), :] = piece

        def blur_rows(band):
            for tile in range(*out[band]):
                for side in range(2):
                    load = lambda plane, shift: ys[band][plane, tile * SUB + shift:(tile + 1) * SUB + shift, :]
                    for plane, value in enumerate(row_depth(s, load, side, *taps_of(band, side), False), side * layers):
                        if number < 2:
                            value = value - x0[plane, rows(tile), :]
                        rs[band][plane, rows(tile), :] = value

        def back_rows(band):
            for tile in range(*back[band]):
                for side in range(2):
                    load = lambda plane, shift: rs[band][plane, tile * SUB + shift:(tile + 1) * SUB + shift, :]
                    for plane, value in enumerate(row_depth(s, load, side, *taps_of(band, side), True), side * layers):
                        qs[band][plane, rows(tile), :] = value

        def back_columns(band):
            a, b = back[band]
            for plane, piece in product(qs[band], a, b, band, backward_ref):
                for tile in range(a, b):
                    part = piece[:, (tile - a) * SUB:(tile - a + 1) * SUB, :]
                    at = slice(plane, plane + pairs)
                    acc[at, rows(tile), :] = acc[at, rows(tile), :] + part if tile in done else part
            done.update(range(a, b))

        def inside(tile, side):
            row = gy * height + tile * SUB - off + lax.broadcasted_iota(jnp.int32, (SUB, breadth), 0)
            here = lax.broadcasted_iota(jnp.int32, (SUB, breadth), 1)
            if side:
                part = lax.rem(here, quarter)
                here = jnp.where(lax.rem(here // quarter, 2) == 0, breadth + part, part - quarter)
            col = gx * breadth + here
            return (row >= 0) & (row < ny * height) & (col >= 0) & (col < nx * breadth)

        def update(tile):
            keep = [inside(tile, side) for side in range(2)]
            for plane in range(planes):
                here = x[plane, rows(tile), :]
                total = acc[plane, rows(tile), :] + DAMPING * here
                before = flux[plane, tile * SUB - 1:(tile + 1) * SUB - 1, :]
                total = total + WEIGHT_TV * (div[plane, rows(tile), :] + before)
                total = jnp.where(keep[plane // layers], total, 0.0)
                if number == 0:
                    xs[1][plane, rows(tile), :] = here - START_STEP * total
                    if plane < layers and begin <= tile < end:
                        g0[plane, rows(tile), :] = total
                else:
                    xs[2][plane, rows(tile), :] = total

        def slopes(a, b):
            if number < 2:
                for tile in range(a, b):
                    slope_tile(s, x, 0, tile, div, flux, where)

        middle = (begin + end) // 2
        columns(0)
        slopes(back_low - 1, middle)
        columns(1)
        blur_rows(0)
        columns(2)
        back_rows(0)
        blur_rows(1)
        back_columns(0)
        back_rows(1)
        back_columns(1)
        blur_rows(2)
        slopes(middle, back_high)
        back_rows(2)
        back_columns(2)
        if number == 1:
            pull_ref[...] = acc[:layers, rows(begin, end), :]
        if number < 2:
            for tile in range(back_low, back_high):
                update(tile)

    for number in range(3):
        one_pass(number)
    again_ref[...] = acc[:layers, rows(begin, end), :]
    low, high = reach(s, 2 * radius)
    x1_ref[...] = x1[:, rows(low, high), :]
    g1_ref[...] = x2[:, rows(low, high), :]

    zero_sq = cross = one_sq = jnp.zeros((SUB, breadth), F32)
    for tile in range(begin, end):
        for layer in range(layers):
            a, b = g0[layer, rows(tile), :], x2[layer, rows(tile), :]
            zero_sq, cross, one_sq = zero_sq + a * a, cross + a * (b - a), one_sq + b * b
    zero_sq, cross, one_sq = [jnp.sum(t, axis=(0, 1), keepdims=True) for t in (zero_sq, cross, one_sq)]
    row = jnp.where(lane == 0, zero_sq, jnp.where(lane == 1, cross, one_sq))
    part_ref[...] = jnp.broadcast_to(row, part_ref.shape)


def step_kernel(s, sums_ref, x1_ref, g1_ref, pull_ref, again_ref, x2_ref, g2_ref, part_ref, keep_ref, x2, div, flux):
    where = place()
    layers, height, breadth = s["layers"], s["height"], s["breadth"]
    low, high = reach(s, 2 * s["radius"])
    lane = lax.broadcasted_iota(jnp.int32, (1, breadth), 1)
    total = jnp.sum(sums_ref[...], axis=0, keepdims=True)
    zero_sq, cross, one_sq = [
        jnp.sum(jnp.where(lane == number, total, 0.0), axis=(0, 1), keepdims=True) for number in range(3)
    ]
    step = (START_STEP * START_STEP * zero_sq) / (-START_STEP * cross)
    count = (high - low) * SUB
    for plane in range(s["planes"]):
        x2[plane, :count, :] = x1_ref[plane] - step * g1_ref[plane]
    begin = s["first"] - low
    total = jnp.zeros((SUB, breadth), F32)
    for tile in range(begin - 1, begin + height // SUB):
        slope_tile(s, x2, low * SUB, tile, div, flux, where)
        if tile < begin:
            continue
        at, out = slice(tile * SUB, (tile + 1) * SUB), slice((tile - begin) * SUB, (tile - begin + 1) * SUB)
        for layer in range(layers):
            here = x2[layer, at, :]
            slope = pull_ref[layer, out, :] - step * again_ref[layer, out, :] + DAMPING * here
            slope = slope + WEIGHT_TV * (div[layer, at, :] + flux[layer, tile * SUB - 1:(tile + 1) * SUB - 1, :])
            x2_ref[layer, out, :] = here
            g2_ref[layer, out, :] = slope
            old = g1_ref[layer, at, :]
            total = total + old * (slope - old)
    growth = -step * jnp.sum(total, axis=(0, 1), keepdims=True)
    part_ref[...] = jnp.broadcast_to(growth, part_ref.shape)
    keep_ref[...] = jnp.broadcast_to(step * step * one_sq, keep_ref.shape)


def final_kernel(sums_ref, keep_ref, x2_ref, g2_ref, out_ref):
    step = keep_ref[:1, :] / jnp.sum(sums_ref[...], axis=0, keepdims=True)
    for layer in range(x2_ref.shape[0]):
        out_ref[layer] = x2_ref[layer] - step * g2_ref[layer]


def pairings(count):
    def both(start):
        pairs = []
        for i in range(start, count - 1, 2):
            pairs += [(i, i + 1), (i + 1, i)]
        return pairs

    return both(0), both(1)


def call(kernel, outs, scratch=(), inputs=None):
    whole = pl.BlockSpec(memory_space=pltpu.VMEM)
    return pl.pallas_call(
        kernel,
        out_shape=outs,
        in_specs=inputs,
        out_specs=jax.tree.map(lambda _: whole, outs),
        scratch_shapes=list(scratch),
        compiler_params=pltpu.CompilerParams(vmem_limit_bytes=VMEM_BYTES),
    )


def per_device(observed, profiles, tile_index):
    layers, height, breadth = observed.shape
    s = plan(layers, height, breadth, profiles.shape[2])
    halo, rows, taps = s["halo"], s["rows"], s["taps"]
    ring = 2 * breadth
    gy = lax.axis_index("gy")
    n = lax.axis_size("gy") * lax.axis_size("gx")
    vmem, smem = pl.BlockSpec(memory_space=pltpu.VMEM), pl.BlockSpec(memory_space=pltpu.SMEM)
    sds = jax.ShapeDtypeStruct

    even = lax.rem(gy, 2) == 0
    bottom, top = jnp.int32(height - halo), jnp.int32(0)
    to_even = lax.dynamic_slice_in_dim(observed, jnp.where(even, bottom, top), halo, axis=1)
    to_odd = lax.dynamic_slice_in_dim(observed, jnp.where(even, top, bottom), halo, axis=1)
    first_pairs, second_pairs = pairings(lax.axis_size("gy"))
    from_even = lax.ppermute(to_even, "gy", first_pairs)
    from_odd = lax.ppermute(to_odd, "gy", second_pairs)

    packed = (s["groups"], height + 2 * halo, breadth)
    anywhere = pl.BlockSpec(memory_space=pl.ANY)
    taps_all, columns = call(
        functools.partial(weights_kernel, s),
        (sds((3, 2, 2, taps, SUB, breadth), F32), sds((3, taps, SUB, ring), F32)), inputs=[smem, smem],
    )(tile_index, profiles.transpose(2, 1, 0))
    tile_here = call(copy_kernel, sds(observed.shape, F32), inputs=[vmem])(observed)
    first, second, centre = call(
        functools.partial(pack_kernel, s),
        (sds(packed, F32), sds(packed, F32), sds((layers, height + 2 * halo, breadth), F32)),
        inputs=[vmem] * 3 + [anywhere],
    )(tile_here, from_even, from_odd, taps_all)
    matrices = sds((6, 3 * ring, ring), BF16)
    forward, backward = call(
        functools.partial(matrices_kernel, s), (matrices, matrices),
        scratch=[pltpu.VMEM((ring, ring), F32)], inputs=[vmem, anywhere],
    )(columns, second)
    first, backward = lax.optimization_barrier((first, backward))
    first_pairs, second_pairs = pairings(lax.axis_size("gx"))
    got_first = lax.ppermute(first, "gx", first_pairs)
    got_second = lax.ppermute(second, "gx", second_pairs)

    big = (s["planes"], rows, breadth)
    low, high = reach(s, 2 * s["radius"])
    wide = (s["planes"], (high - low) * SUB, breadth)
    tile = sds((layers, height, breadth), F32)
    x1, g1, pull, again, part = call(
        functools.partial(main_kernel, s),
        (sds(wide, F32), sds(wide, F32), tile, tile, sds((n, breadth), F32)),
        scratch=[pltpu.VMEM(shape, F32) for shape in [big] * 3 + [(layers, rows, breadth)] + [big] * 12],
        inputs=[vmem] * 6,
    )(centre, got_first, got_second, taps_all, forward, backward)
    sums = lax.all_to_all(part, ("gy", "gx"), 0, 0, tiled=True)
    work = pltpu.VMEM((s["planes"], (high - low + 1) * SUB, breadth), F32)
    x2, g2, part, keep = call(
        functools.partial(step_kernel, s),
        (tile, tile, sds((n, breadth), F32), sds((SUB, breadth), F32)),
        scratch=[work] * 3,
        inputs=[vmem] * 5,
    )(sums, x1, g1, pull, again)
    sums = lax.all_to_all(part, ("gy", "gx"), 0, 0, tiled=True)
    return call(final_kernel, tile, inputs=[vmem] * 4)(sums, keep, x2, g2)


def solution(mesh):
    in_specs = (P(None, "gy", "gx"), P(), P())
    out_specs = P(None, "gy", "gx")
    return jax.shard_map(
        per_device, mesh=mesh, in_specs=in_specs, out_specs=out_specs, check_vma=False
    )
```

```python
import functools
import jax
import jax.numpy as jnp
from jax import lax
from jax.experimental import pallas as pl
from jax.experimental.pallas import tpu as pltpu
from jax.sharding import PartitionSpec as P

ITERS = 2
WEIGHT_TV = 0.02
SMOOTHING = 0.1
DAMPING = 0.05
START_STEP = 0.5
SUB = 8
F32 = jnp.float32
BF16 = jnp.bfloat16
VMEM_BYTES = 36 * 1024 * 1024


def plan(layers, height, breadth, taps):
    radius = (taps - 1) // 2
    halo = 6 * radius
    off = -(-halo // SUB) * SUB + SUB
    return dict(
        layers=layers, height=height, breadth=breadth, taps=taps, radius=radius, halo=halo, off=off,
        rows=height + 2 * off, groups=-(-layers * halo // breadth), pairs=layers // 2, planes=layers + layers // 2, quarter=breadth // 4, first=off // SUB, last=(off + height) // SUB,
        tiles=(height + 2 * off) // SUB,
    )


def reach(s, extent):
    low = (s["off"] - extent) // SUB
    high = -(-(s["off"] + s["height"] + extent) // SUB)
    return low, high


def bands(s):
    return ((0, s["first"]), (s["first"], s["last"]), (s["last"], s["tiles"]))


def place():
    return lax.axis_index("gy"), lax.axis_index("gx"), lax.axis_size("gy"), lax.axis_size("gx")


def column_of(s, place, member):
    breadth, quarter = s["breadth"], s["quarter"]
    side = place - breadth
    right, left = (0, 3 * quarter) if member == 0 else (2 * quarter, quarter)
    column = jnp.where((side >= right) & (side < right + quarter), breadth + side - right, 1 << 20)
    column = jnp.where((side >= left) & (side < left + quarter), side - left - quarter, column)
    return jnp.where(place < breadth, place, column)


def weights_kernel(s, index_ref, profiles_ref, taps_ref, columns_ref):
    gy, gx, ny, nx = place()
    breadth, taps = s["breadth"], s["taps"]
    lane = lax.broadcasted_iota(jnp.int32, (SUB, breadth), 1)
    is_right = lax.rem(lane // s["quarter"], 2) == 0
    for band in range(3):
        row = gy + (band - 1)
        picked = []
        for side in range(3):
            col = gx + (side - 1)
            inside = (row >= 0) & (row < ny) & (col >= 0) & (col < nx)
            number = index_ref[jnp.clip(row, 0, ny - 1), jnp.clip(col, 0, nx - 1)]
            picked.append((inside, number))
        for dim in range(3):
            for tap in range(taps):
                left, centre, right = [
                    jnp.where(inside, profiles_ref[tap, dim, number], 0.0) for inside, number in picked
                ]
                own, side = jnp.full((SUB, breadth), centre, F32), jnp.where(is_right, right, left)
                if dim < 2:
                    taps_ref[band, dim, 0, tap] = own
                    taps_ref[band, dim, 1, tap] = side
                else:
                    columns_ref[band, tap] = jnp.concatenate([own, side], axis=1)


def matrices_kernel(s, columns_ref, taps_ref, after_ref, forward_ref, backward_ref, depth_ref, full):
    breadth, taps, radius = s["breadth"], s["taps"], s["radius"]
    ring = 2 * breadth
    chunk = 32
    target = lax.broadcasted_iota(jnp.int32, (1, ring), 1)
    for number in range(6):
        band, member = divmod(number, 2)
        columns = [columns_ref[band, t, :1, :] for t in range(taps)]
        reached = column_of(s, target, member)
        reached = jnp.where(reached < 1 << 19, reached + radius, -(1 << 20))
        for start in range(0, ring, chunk):
            source = lax.broadcasted_iota(jnp.int32, (chunk, 1), 0) + start
            distance = reached - column_of(s, source, member)
            total = jnp.zeros((chunk, ring), F32)
            for tap in range(taps):
                total = jnp.where(distance == tap, columns[tap], total)
            full[start:start + chunk, :] = total
        matrix = full[...]
        for ref, value in ((forward_ref, matrix), (backward_ref, matrix.T)):
            upper = value.astype(BF16)
            ref[number, :ring, :] = upper
            ref[number, ring:2 * ring, :] = (value - upper.astype(F32)).astype(BF16)
            ref[number, 2 * ring:, :] = upper
    size = s["layers"] * SUB
    row = lax.broadcasted_iota(jnp.int32, (size, 1), 0)
    col = lax.broadcasted_iota(jnp.int32, (1, size), 1)
    same = lax.rem(row, SUB) == lax.rem(col, SUB)
    apart = jnp.where(same, row // SUB - col // SUB + radius, -1)
    for band in range(3):
        total = jnp.zeros((size, size), F32)
        for tap in range(taps):
            total = jnp.where(apart == tap, jnp.broadcast_to(taps_ref[band, 0, 0, tap][:1, :size], (1, size)), total)
        for number, value in enumerate((total, total.T)):
            upper = value.astype(BF16)
            depth_ref[2 * band + number, :, :size] = upper
            depth_ref[2 * band + number, :, size:2 * size] = upper
            depth_ref[2 * band + number, :, 2 * size:] = (value - upper.astype(F32)).astype(BF16)


def strip_places(s, layer):
    group, lane = divmod(layer * s["halo"], s["breadth"])
    return group, lane, min(s["halo"], s["breadth"] - lane)


def copy_kernel(tile_ref, out_ref):
    out_ref[...] = tile_ref[...]


def pack_kernel(s, tile_ref, even_ref, odd_ref, after_ref, first_ref, second_ref, centre_ref):
    gy, gx, _, _ = place()
    halo, height, breadth = s["halo"], s["height"], s["breadth"]
    row_even, col_even = lax.rem(gy, 2) == 0, lax.rem(gx, 2) == 0
    lane = lax.broadcasted_iota(jnp.int32, (1, breadth), 1)
    for start, count in ((0, halo), (halo, height), (halo + height, halo)):
        first = [jnp.zeros((count, breadth), F32)] * s["groups"]
        second = list(first)
        for layer in range(s["layers"]):
            if start == halo:
                value = tile_ref[layer]
            elif start == 0:
                value = jnp.where(row_even, odd_ref[layer], even_ref[layer])
            else:
                value = jnp.where(row_even, even_ref[layer], odd_ref[layer])
            centre_ref[layer, start:start + count, :] = value
            group, begin, here = strip_places(s, layer)
            from_left, from_right = begin, (begin + halo) % breadth
            to_first = pltpu.roll(value, jnp.where(col_even, from_right, from_left), 1)
            to_second = pltpu.roll(value, jnp.where(col_even, from_left, from_right), 1)
            parts = [(group, (lane >= begin) & (lane < begin + here))]
            if here < halo:
                parts.append((group + 1, lane < halo - here))
            for number, mine in parts:
                first[number] = jnp.where(mine, to_first, first[number])
                second[number] = jnp.where(mine, to_second, second[number])
        for number in range(s["groups"]):
            first_ref[number, start:start + count, :] = first[number]
            second_ref[number, start:start + count, :] = second[number]


def unpack_layer(s, groups, layer, to):
    breadth = s["breadth"]
    lane = lax.broadcasted_iota(jnp.int32, (1, breadth), 1)
    group, begin, here = strip_places(s, layer)
    value = groups[group]
    if here < s["halo"]:
        value = jnp.where(lane >= begin, value, groups[group + 1])
    shift = (to - begin) % breadth
    return pltpu.roll(value, shift, 1) if shift else value


def first_lanes(s):
    lane = lax.broadcasted_iota(jnp.int32, (1, s["breadth"]), 1)
    return (lane < s["quarter"]) | (lane >= 3 * s["quarter"])


def swap_layers(s, value):
    return pltpu.roll(value, 2 * s["quarter"], 1)


def weighted(taps, values):
    total = None
    for tap, value in zip(taps, values):
        if value is not None:
            total = tap * value if total is None else total + tap * value
    return total


def shifts_of(s, transposed):
    return [t - s["radius"] if transposed else s["radius"] - t for t in range(s["taps"])]


def own_sums(s, loads, row_taps, depth_matrix, transposed):
    layers, breadth = s["layers"], s["breadth"]
    mixed = [
        jnp.concatenate(
            [weighted(row_taps, [load(p, shift) for shift in shifts_of(s, transposed)]) for p in range(layers)], axis=0)
        for load in loads
    ]
    value = jnp.concatenate(mixed, axis=1)
    upper = value.astype(BF16)
    lower = (value - upper.astype(F32)).astype(BF16)
    result = jnp.dot(depth_matrix, jnp.concatenate([upper, lower, upper], axis=0), preferred_element_type=F32)
    return [
        [result[p * SUB:(p + 1) * SUB, k * breadth:(k + 1) * breadth] for p in range(layers)] for k in range(len(loads))
    ]


def side_sums(s, load, row_taps, depth_taps, transposed):
    layers, radius, pairs = s["layers"], s["radius"], s["pairs"]
    shifts = shifts_of(s, transposed)
    mixed = [weighted(row_taps, [load(layers + p, shift) for shift in shifts]) for p in range(pairs)]
    beyond = {}
    first = first_lanes(s)
    for step in range(1, radius + 1):
        beyond[-step] = jnp.where(first, 0.0, swap_layers(s, mixed[pairs - step]))
        beyond[pairs - 1 + step] = jnp.where(first, swap_layers(s, mixed[step - 1]), 0.0)
    at = lambda p: mixed[p] if 0 <= p < pairs else beyond.get(p)
    return [weighted(depth_taps, [at(p + shift) for shift in shifts]) for p in range(pairs)]


def slope_tile(s, source, shift, tile, divergence, flux_rows, where, rows_only=False):
    gy, gx, ny, nx = where
    layers, height, breadth, pairs, quarter = s["layers"], s["height"], s["breadth"], s["pairs"], s["quarter"]
    lane = lax.broadcasted_iota(jnp.int32, (SUB, breadth), 1)
    side_col = jnp.where(lax.rem(lane // quarter, 2) == 0, breadth + lax.rem(lane, quarter), lax.rem(lane, quarter) - quarter)
    masks = []
    for col in (lane, side_col):
        col = gx * breadth + col
        masks.append(jnp.where((col >= 0) & (col < nx * breadth - 1), 1.0, 0.0).astype(F32))
    start = tile * SUB
    row = gy * height + start - s["off"] + shift + lax.broadcasted_iota(jnp.int32, (SUB, breadth), 0)
    row_mask = jnp.where((row >= 0) & (row < ny * height - 1), 1.0, 0.0).astype(F32)
    at_edge = tile * SUB + shift - s["off"] in (-SUB, height - SUB)
    last, first = breadth - 1, first_lanes(s)
    rows = slice(start, start + SUB)

    def swap(value):
        return swap_layers(s, value)

    before = [None, None, None]
    heres = [source[plane, rows, :] for plane in (0, pairs, layers)]
    for p in range(pairs):
        planes = (p, p + pairs, layers + p)
        afters = [source[plane + 1, rows, :] if p + 1 < pairs else None for plane in planes]
        if p + 1 == pairs:
            afters[0] = source[pairs, rows, :]
            afters[2] = jnp.where(first, swap(source[layers, rows, :]), heres[2])
        rolled = [pltpu.roll(value, breadth - 1, 1) for value in heres]
        nexts = [
            jnp.where(lane == last, rolled[2], rolled[0]),
            jnp.where(lane == last, swap(rolled[2]), rolled[1]),
            jnp.where(lane == last, rolled[0], jnp.where(lane == 2 * quarter - 1, swap(rolled[1]), rolled[2])),
        ]
        f_cols, totals = [], []
        for k, plane in enumerate(planes):
            here = heres[k]
            step_rows = source[plane, start + 1:start + 1 + SUB, :] - here
            if at_edge:
                step_rows = step_rows * row_mask
            step_cols = (nexts[k] - here) * masks[k // 2]
            square = step_rows * step_rows + step_cols * step_cols + SMOOTHING * SMOOTHING
            if afters[k] is not None:
                step_depth = afters[k] - here
                square = square + step_depth * step_depth
            inverse = lax.rsqrt(square)
            f_rows = step_rows * inverse
            flux_rows[plane, rows, :] = f_rows
            if rows_only:
                continue
            f_cols.append(step_cols * inverse)
            total = -f_cols[k] - f_rows
            if before[k] is not None:
                total = total + before[k]
            before[k] = None
            if afters[k] is not None:
                before[k] = step_depth * inverse
                total = total - before[k]
            totals.append(total)
        heres = afters
        if rows_only:
            continue
        rolled = [pltpu.roll(value, 1, 1) for value in f_cols]
        totals[0] = totals[0] + jnp.where(lane == 0, rolled[2], rolled[0])
        totals[1] = totals[1] + jnp.where(lane == 0, swap(rolled[2]), rolled[1])
        totals[2] = totals[2] + jnp.where(lane == 0, rolled[0], jnp.where(lane == 2 * quarter, swap(rolled[1]), rolled[2]))
        for plane, total in zip(planes, totals):
            divergence[plane, rows, :] = total
    if rows_only:
        return
    divergence[pairs, rows, :] = divergence[pairs, rows, :] + before[0]
    divergence[layers, rows, :] = divergence[layers, rows, :] + jnp.where(first, 0.0, swap(before[2]))


def main_kernel(s, centre_ref, first_ref, second_ref, taps_ref, forward_ref, backward_ref, depth_ref,
                x1_ref, g1_ref, pull_ref, again_ref, part_ref,
                x0, x1, x2, g0, y0, y1, y2, r0, r1, r2, q0, q1, q2, acc, div, flux):
    where = place()
    gy, gx, ny, nx = where
    layers, height, breadth, off = s["layers"], s["height"], s["breadth"], s["off"]
    halo, radius, taps, pairs, planes, quarter = [s[k] for k in ("halo", "radius", "taps", "pairs", "planes", "quarter")]
    begin, end = s["first"], s["last"]
    col_even = lax.rem(gx, 2) == 0
    lane = lax.broadcasted_iota(jnp.int32, (1, breadth), 1)
    xs, ys, rs, qs = (x0, x1, x2), (y0, y1, y2), (r0, r1, r2), (q0, q1, q2)
    span = bands(s)

    def rows(tile, stop=None):
        return slice(tile * SUB, (tile + 1 if stop is None else stop) * SUB)

    top = off - halo
    x0[:layers, top:off + height + halo, :] = centre_ref[...]
    firsts = [first_ref[g] for g in range(s["groups"])]
    seconds = [second_ref[g] for g in range(s["groups"])]
    rights = [jnp.where(col_even, a, b) for a, b in zip(firsts, seconds)]
    lefts = [jnp.where(col_even, b, a) for a, b in zip(firsts, seconds)]
    for p in range(pairs):
        value = jnp.zeros((height + 2 * halo, breadth), F32)
        for groups, layer, to in ((rights, p, 0), (lefts, p + pairs, 2 * quarter - halo),
                                  (rights, p + pairs, 2 * quarter), (lefts, p, breadth - halo)):
            value = jnp.where((lane >= to) & (lane < to + halo), unpack_layer(s, groups, layer, to), value)
        x0[layers + p, top:off + height + halo, :] = value
    zero = jnp.zeros((planes, SUB, breadth), F32)
    for ref, tiles in ((y0, (0,)), (y2, (s["tiles"] - 1,)), (r0, (begin, begin + 1)),
                       (r1, (begin - 2, begin - 1, end, end + 1)), (r2, (end - 2, end - 1))):
        for tile in tiles:
            ref[:, rows(tile), :] = zero

    def product(ref, low, high, band, matrices, own_only=False):
        width = breadth if own_only else 2 * breadth
        count = (high - low) * SUB

        def split(a, b):
            value = ref[a:b, rows(low, high), :].reshape((b - a) * count, breadth)
            upper = value.astype(BF16)
            return upper, (value - upper.astype(F32)).astype(BF16)

        side_high, side_low = split(layers, planes)
        own, side = [], None
        for member in range(2):
            high_part, low_part = split(member * pairs, (member + 1) * pairs)
            parts = [high_part, side_high] * 2 + [low_part, side_low]
            result = jnp.dot(jnp.concatenate(parts, axis=1), matrices[2 * band + member, :, :width], preferred_element_type=F32)
            own.append(result[:, :breadth].reshape(pairs, count, breadth))
            if not own_only:
                rest = result[:, breadth:]
                side = rest if side is None else side + rest
        pieces = [(0, own[0]), (pairs, own[1])]
        return pieces if own_only else pieces + [(layers, side.reshape(pairs, count, breadth))]

    def taps_of(band, half):
        return [[taps_ref[band, dim, half, t] for t in range(taps)] for dim in (1, 0)]

    def one_pass(number):
        x = xs[number]
        low, high = reach(s, (5 - 2 * number) * radius)
        in_low, in_high = reach(s, (6 - 2 * number) * radius)
        back_low, back_high = reach(s, (4 - 2 * number) * radius)
        out = [(max(low, a), min(high, b)) for a, b in span]
        back = [(max(back_low, a - 1), min(back_high, b + 1)) for a, b in span]
        done = set()

        def columns(band):
            a, b = max(out[band][0] - 1, in_low), min(out[band][1] + 1, in_high)
            for plane, piece in product(x, a, b, band, forward_ref):
                ys[band][plane:plane + pairs, rows(a, b), :] = piece

        def sums(band, source, low, high, transposed, emit):
            own_taps, (row_taps, depth_taps) = taps_of(band, 0)[0], taps_of(band, 1)

            def load_at(tile):
                def load(plane, shift):
                    if transposed and ((tile < span[band][0] and shift <= 0) or (tile >= span[band][1] and shift >= 0)):
                        return None
                    return source[plane, tile * SUB + shift:(tile + 1) * SUB + shift, :]

                return load

            for at in range(low, high, 2):
                group = range(at, min(at + 2, high))
                matrix = depth_ref[2 * band + (1 if transposed else 0)]
                results = own_sums(s, [load_at(tile) for tile in group], own_taps, matrix, transposed)
                for tile, result in zip(group, results):
                    side = side_sums(s, load_at(tile), row_taps, depth_taps, transposed)
                    for plane, value in enumerate(result + side):
                        emit(plane, tile, value)

        def blur_rows(band):
            def emit(plane, tile, value):
                rs[band][plane, rows(tile), :] = value if number == 2 else value - x0[plane, rows(tile), :]

            sums(band, ys[band], *out[band], False, emit)

        def back_rows(band):
            def emit(plane, tile, value):
                qs[band][plane, rows(tile), :] = value

            sums(band, rs[band], *back[band], True, emit)

        def back_columns(band):
            a, b = back[band]
            for plane, piece in product(qs[band], a, b, band, backward_ref, number == 2):
                for tile in range(a, b):
                    part = piece[:, (tile - a) * SUB:(tile - a + 1) * SUB, :]
                    at = slice(plane, plane + pairs)
                    acc[at, rows(tile), :] = acc[at, rows(tile), :] + part if tile in done else part
            done.update(range(a, b))

        def inside(tile, side):
            row = gy * height + tile * SUB - off + lax.broadcasted_iota(jnp.int32, (SUB, breadth), 0)
            here = lax.broadcasted_iota(jnp.int32, (SUB, breadth), 1)
            if side:
                part = lax.rem(here, quarter)
                here = jnp.where(lax.rem(here // quarter, 2) == 0, breadth + part, part - quarter)
            col = gx * breadth + here
            return (row >= 0) & (row < ny * height) & (col >= 0) & (col < nx * breadth)

        def update(tile):
            keep = [inside(tile, side) for side in range(2)]
            for plane in range(planes):
                here = x[plane, rows(tile), :]
                total = acc[plane, rows(tile), :] + DAMPING * here
                before = flux[plane, tile * SUB - 1:(tile + 1) * SUB - 1, :]
                total = total + WEIGHT_TV * (div[plane, rows(tile), :] + before)
                total = jnp.where(keep[plane // layers], total, 0.0)
                if number == 0:
                    xs[1][plane, rows(tile), :] = here - START_STEP * total
                    if plane < layers and begin <= tile < end:
                        g0[plane, rows(tile), :] = total
                else:
                    xs[2][plane, rows(tile), :] = total

        def slopes(a, b):
            if number < 2:
                for tile in range(a, b):
                    slope_tile(s, x, 0, tile, div, flux, where, tile < back_low)

        middle = (begin + end) // 2
        columns(0)
        slopes(back_low - 1, middle)
        columns(1)
        blur_rows(0)
        columns(2)
        back_rows(0)
        blur_rows(1)
        back_columns(0)
        back_rows(1)
        back_columns(1)
        blur_rows(2)
        slopes(middle, back_high)
        back_rows(2)
        back_columns(2)
        if number == 1:
            pull_ref[...] = acc[:layers, rows(begin, end), :]
        if number < 2:
            for tile in range(back_low, back_high):
                update(tile)

    for number in range(3):
        one_pass(number)
    again_ref[...] = acc[:layers, rows(begin, end), :]
    low, high = reach(s, 2 * radius)
    x1_ref[...] = x1[:, rows(low, high), :]
    g1_ref[...] = x2[:, rows(low, high), :]

    zero_sq = cross = one_sq = jnp.zeros((SUB, breadth), F32)
    for tile in range(begin, end):
        for layer in range(layers):
            a, b = g0[layer, rows(tile), :], x2[layer, rows(tile), :]
            zero_sq, cross, one_sq = zero_sq + a * a, cross + a * (b - a), one_sq + b * b
    zero_sq, cross, one_sq = [jnp.sum(t, axis=(0, 1), keepdims=True) for t in (zero_sq, cross, one_sq)]
    row = jnp.where(lane == 0, zero_sq, jnp.where(lane == 1, cross, one_sq))
    part_ref[...] = jnp.broadcast_to(row, part_ref.shape)


def step_kernel(s, sums_ref, x1_ref, g1_ref, pull_ref, again_ref, x2_ref, g2_ref, part_ref, keep_ref, x2, div, flux):
    where = place()
    layers, height, breadth = s["layers"], s["height"], s["breadth"]
    low, high = reach(s, 2 * s["radius"])
    lane = lax.broadcasted_iota(jnp.int32, (1, breadth), 1)
    total = jnp.sum(sums_ref[...], axis=0, keepdims=True)
    zero_sq, cross, one_sq = [
        jnp.sum(jnp.where(lane == number, total, 0.0), axis=(0, 1), keepdims=True) for number in range(3)
    ]
    step = (START_STEP * START_STEP * zero_sq) / (-START_STEP * cross)
    count = (high - low) * SUB
    for plane in range(s["planes"]):
        x2[plane, :count, :] = x1_ref[plane] - step * g1_ref[plane]
    begin = s["first"] - low
    total = jnp.zeros((SUB, breadth), F32)
    for tile in range(begin - 1, begin + height // SUB):
        slope_tile(s, x2, low * SUB, tile, div, flux, where, tile < begin)
        if tile < begin:
            continue
        at, out = slice(tile * SUB, (tile + 1) * SUB), slice((tile - begin) * SUB, (tile - begin + 1) * SUB)
        for layer in range(layers):
            here = x2[layer, at, :]
            slope = pull_ref[layer, out, :] - step * again_ref[layer, out, :] + DAMPING * here
            slope = slope + WEIGHT_TV * (div[layer, at, :] + flux[layer, tile * SUB - 1:(tile + 1) * SUB - 1, :])
            x2_ref[layer, out, :] = here
            g2_ref[layer, out, :] = slope
            old = g1_ref[layer, at, :]
            total = total + old * (slope - old)
    growth = -step * jnp.sum(total, axis=(0, 1), keepdims=True)
    part_ref[...] = jnp.broadcast_to(growth, part_ref.shape)
    keep_ref[...] = jnp.broadcast_to(step * step * one_sq, keep_ref.shape)


def final_kernel(sums_ref, keep_ref, x2_ref, g2_ref, out_ref):
    step = keep_ref[:1, :] / jnp.sum(sums_ref[...], axis=0, keepdims=True)
    for layer in range(x2_ref.shape[0]):
        out_ref[layer] = x2_ref[layer] - step * g2_ref[layer]


def pairings(count):
    def both(start):
        pairs = []
        for i in range(start, count - 1, 2):
            pairs += [(i, i + 1), (i + 1, i)]
        return pairs

    return both(0), both(1)


def call(kernel, outs, scratch=(), inputs=None):
    whole = pl.BlockSpec(memory_space=pltpu.VMEM)
    return pl.pallas_call(
        kernel,
        out_shape=outs,
        in_specs=inputs,
        out_specs=jax.tree.map(lambda _: whole, outs),
        scratch_shapes=list(scratch),
        compiler_params=pltpu.CompilerParams(vmem_limit_bytes=VMEM_BYTES),
    )


def per_device(observed, profiles, tile_index):
    layers, height, breadth = observed.shape
    s = plan(layers, height, breadth, profiles.shape[2])
    halo, rows, taps = s["halo"], s["rows"], s["taps"]
    ring = 2 * breadth
    gy = lax.axis_index("gy")
    n = lax.axis_size("gy") * lax.axis_size("gx")
    vmem, smem = pl.BlockSpec(memory_space=pltpu.VMEM), pl.BlockSpec(memory_space=pltpu.SMEM)
    sds = jax.ShapeDtypeStruct

    even = lax.rem(gy, 2) == 0
    bottom, top = jnp.int32(height - halo), jnp.int32(0)
    to_even = lax.dynamic_slice_in_dim(observed, jnp.where(even, bottom, top), halo, axis=1)
    to_odd = lax.dynamic_slice_in_dim(observed, jnp.where(even, top, bottom), halo, axis=1)
    first_pairs, second_pairs = pairings(lax.axis_size("gy"))
    from_even = lax.ppermute(to_even, "gy", first_pairs)
    from_odd = lax.ppermute(to_odd, "gy", second_pairs)

    packed = (s["groups"], height + 2 * halo, breadth)
    anywhere = pl.BlockSpec(memory_space=pl.ANY)
    taps_all, columns = call(
        functools.partial(weights_kernel, s),
        (sds((3, 2, 2, taps, SUB, breadth), F32), sds((3, taps, SUB, ring), F32)), inputs=[smem, smem],
    )(tile_index, profiles.transpose(2, 1, 0))
    tile_here = call(copy_kernel, sds(observed.shape, F32), inputs=[vmem])(observed)
    first, second, centre = call(
        functools.partial(pack_kernel, s),
        (sds(packed, F32), sds(packed, F32), sds((layers, height + 2 * halo, breadth), F32)),
        inputs=[vmem] * 3 + [anywhere],
    )(tile_here, from_even, from_odd, taps_all)
    matrices = sds((6, 3 * ring, ring), BF16)
    size = layers * SUB
    forward, backward, depth = call(
        functools.partial(matrices_kernel, s), (matrices, matrices, sds((6, size, 3 * size), BF16)),
        scratch=[pltpu.VMEM((ring, ring), F32)], inputs=[vmem, vmem, anywhere],
    )(columns, taps_all, second)
    first, backward = lax.optimization_barrier((first, backward))
    first_pairs, second_pairs = pairings(lax.axis_size("gx"))
    got_first = lax.ppermute(first, "gx", first_pairs)
    got_second = lax.ppermute(second, "gx", second_pairs)

    big = (s["planes"], rows, breadth)
    low, high = reach(s, 2 * s["radius"])
    wide = (s["planes"], (high - low) * SUB, breadth)
    tile = sds((layers, height, breadth), F32)
    x1, g1, pull, again, part = call(
        functools.partial(main_kernel, s),
        (sds(wide, F32), sds(wide, F32), tile, tile, sds((n, breadth), F32)),
        scratch=[pltpu.VMEM(shape, F32) for shape in [big] * 3 + [(layers, rows, breadth)] + [big] * 12],
        inputs=[vmem] * 7,
    )(centre, got_first, got_second, taps_all, forward, backward, depth)
    sums = lax.all_to_all(part, ("gy", "gx"), 0, 0, tiled=True)
    work = pltpu.VMEM((s["planes"], (high - low + 1) * SUB, breadth), F32)
    x2, g2, part, keep = call(
        functools.partial(step_kernel, s),
        (tile, tile, sds((n, breadth), F32), sds((SUB, breadth), F32)),
        scratch=[work] * 3,
        inputs=[vmem] * 5,
    )(sums, x1, g1, pull, again)
    sums = lax.all_to_all(part, ("gy", "gx"), 0, 0, tiled=True)
    return call(final_kernel, tile, inputs=[vmem] * 4)(sums, keep, x2, g2)


def solution(mesh):
    in_specs = (P(None, "gy", "gx"), P(), P())
    out_specs = P(None, "gy", "gx")
    return jax.shard_map(
        per_device, mesh=mesh, in_specs=in_specs, out_specs=out_specs, check_vma=False
    )
```

```python
import functools
import jax
import jax.numpy as jnp
from jax import lax
from jax.experimental import pallas as pl
from jax.experimental.pallas import tpu as pltpu
from jax.sharding import PartitionSpec as P

ITERS = 2
WEIGHT_TV = 0.02
SMOOTHING = 0.1
DAMPING = 0.05
START_STEP = 0.5
SUB = 8
F32 = jnp.float32
BF16 = jnp.bfloat16
VMEM_BYTES = 36 * 1024 * 1024


def plan(layers, height, breadth, taps):
    radius = (taps - 1) // 2
    halo = 6 * radius
    off = -(-halo // SUB) * SUB + SUB
    return dict(
        layers=layers, height=height, breadth=breadth, taps=taps, radius=radius, halo=halo, off=off,
        rows=height + 2 * off, groups=-(-layers * halo // breadth), pairs=layers // 2, planes=layers + layers // 2, quarter=breadth // 4, first=off // SUB, last=(off + height) // SUB,
        tiles=(height + 2 * off) // SUB,
    )


def reach(s, extent):
    low = (s["off"] - extent) // SUB
    high = -(-(s["off"] + s["height"] + extent) // SUB)
    return low, high


def bands(s):
    return ((0, s["first"]), (s["first"], s["last"]), (s["last"], s["tiles"]))


def place():
    return lax.axis_index("gy"), lax.axis_index("gx"), lax.axis_size("gy"), lax.axis_size("gx")


def column_of(s, place, member):
    breadth, quarter = s["breadth"], s["quarter"]
    side = place - breadth
    right, left = (0, 3 * quarter) if member == 0 else (2 * quarter, quarter)
    column = jnp.where((side >= right) & (side < right + quarter), breadth + side - right, 1 << 20)
    column = jnp.where((side >= left) & (side < left + quarter), side - left - quarter, column)
    return jnp.where(place < breadth, place, column)


def weights_kernel(s, index_ref, profiles_ref, taps_ref, columns_ref):
    gy, gx, ny, nx = place()
    breadth, taps = s["breadth"], s["taps"]
    lane = lax.broadcasted_iota(jnp.int32, (SUB, breadth), 1)
    is_right = lax.rem(lane // s["quarter"], 2) == 0
    for band in range(3):
        row = gy + (band - 1)
        picked = []
        for side in range(3):
            col = gx + (side - 1)
            inside = (row >= 0) & (row < ny) & (col >= 0) & (col < nx)
            number = index_ref[jnp.clip(row, 0, ny - 1), jnp.clip(col, 0, nx - 1)]
            picked.append((inside, number))
        for dim in range(3):
            for tap in range(taps):
                left, centre, right = [
                    jnp.where(inside, profiles_ref[tap, dim, number], 0.0) for inside, number in picked
                ]
                own, side = jnp.full((SUB, breadth), centre, F32), jnp.where(is_right, right, left)
                if dim < 2:
                    taps_ref[band, dim, 0, tap] = own
                    taps_ref[band, dim, 1, tap] = side
                else:
                    columns_ref[band, tap] = jnp.concatenate([own, side], axis=1)


def matrices_kernel(s, columns_ref, taps_ref, after_ref, forward_ref, backward_ref, depth_ref, full):
    breadth, taps, radius = s["breadth"], s["taps"], s["radius"]
    ring = 2 * breadth
    chunk = 32
    target = lax.broadcasted_iota(jnp.int32, (1, ring), 1)
    for number in range(6):
        band, member = divmod(number, 2)
        columns = [columns_ref[band, t, :1, :] for t in range(taps)]
        reached = column_of(s, target, member)
        reached = jnp.where(reached < 1 << 19, reached + radius, -(1 << 20))
        for start in range(0, ring, chunk):
            source = lax.broadcasted_iota(jnp.int32, (chunk, 1), 0) + start
            distance = reached - column_of(s, source, member)
            total = jnp.zeros((chunk, ring), F32)
            for tap in range(taps):
                total = jnp.where(distance == tap, columns[tap], total)
            full[start:start + chunk, :] = total
        matrix = full[...]
        for ref, value in ((forward_ref, matrix), (backward_ref, matrix.T)):
            upper = value.astype(BF16)
            ref[number, :ring, :] = upper
            ref[number, ring:2 * ring, :] = (value - upper.astype(F32)).astype(BF16)
            ref[number, 2 * ring:, :] = upper
    window = SUB + 2 * radius
    size = s["layers"] * window
    place_in = lax.broadcasted_iota(jnp.int32, (SUB, size), 1)
    layer_in, row_in = place_in // window, lax.rem(place_in, window)
    row_out = lax.broadcasted_iota(jnp.int32, (SUB, size), 0)

    def wide(band, dim, tap):
        return jnp.broadcast_to(taps_ref[band, dim, 0, tap][:1, :1], (SUB, size))

    for band in range(3):
        for transposed in range(2):
            number = 2 * band + transposed
            apart = row_in - row_out if transposed else row_out + 2 * radius - row_in
            by_row = jnp.zeros((SUB, size), F32)
            for tap in range(taps):
                by_row = jnp.where(apart == tap, wide(band, 1, tap), by_row)
            depth_taps = [wide(band, 0, tap) for tap in range(taps)]
            for layer in range(s["layers"]):
                apart = layer_in - layer + radius if transposed else layer - layer_in + radius
                value = jnp.zeros((SUB, size), F32)
                for tap in range(taps):
                    value = jnp.where(apart == tap, depth_taps[tap], value)
                full[layer * SUB:(layer + 1) * SUB, :size] = value * by_row
            value = full[:s["layers"] * SUB, :size]
            upper = value.astype(BF16)
            depth_ref[number, :, :size] = upper
            depth_ref[number, :, size:2 * size] = upper
            depth_ref[number, :, 2 * size:] = (value - upper.astype(F32)).astype(BF16)


def strip_places(s, layer):
    group, lane = divmod(layer * s["halo"], s["breadth"])
    return group, lane, min(s["halo"], s["breadth"] - lane)


def copy_kernel(tile_ref, out_ref):
    out_ref[...] = tile_ref[...]


def pack_kernel(s, tile_ref, even_ref, odd_ref, after_ref, first_ref, second_ref, centre_ref):
    gy, gx, _, _ = place()
    halo, height, breadth = s["halo"], s["height"], s["breadth"]
    row_even, col_even = lax.rem(gy, 2) == 0, lax.rem(gx, 2) == 0
    lane = lax.broadcasted_iota(jnp.int32, (1, breadth), 1)
    for start, count in ((0, halo), (halo, height), (halo + height, halo)):
        first = [jnp.zeros((count, breadth), F32)] * s["groups"]
        second = list(first)
        for layer in range(s["layers"]):
            if start == halo:
                value = tile_ref[layer]
            elif start == 0:
                value = jnp.where(row_even, odd_ref[layer], even_ref[layer])
            else:
                value = jnp.where(row_even, even_ref[layer], odd_ref[layer])
            centre_ref[layer, start:start + count, :] = value
            group, begin, here = strip_places(s, layer)
            from_left, from_right = begin, (begin + halo) % breadth
            to_first = pltpu.roll(value, jnp.where(col_even, from_right, from_left), 1)
            to_second = pltpu.roll(value, jnp.where(col_even, from_left, from_right), 1)
            parts = [(group, (lane >= begin) & (lane < begin + here))]
            if here < halo:
                parts.append((group + 1, lane < halo - here))
            for number, mine in parts:
                first[number] = jnp.where(mine, to_first, first[number])
                second[number] = jnp.where(mine, to_second, second[number])
        for number in range(s["groups"]):
            first_ref[number, start:start + count, :] = first[number]
            second_ref[number, start:start + count, :] = second[number]


def unpack_layer(s, groups, layer, to):
    breadth = s["breadth"]
    lane = lax.broadcasted_iota(jnp.int32, (1, breadth), 1)
    group, begin, here = strip_places(s, layer)
    value = groups[group]
    if here < s["halo"]:
        value = jnp.where(lane >= begin, value, groups[group + 1])
    shift = (to - begin) % breadth
    return pltpu.roll(value, shift, 1) if shift else value


def first_lanes(s):
    lane = lax.broadcasted_iota(jnp.int32, (1, s["breadth"]), 1)
    return (lane < s["quarter"]) | (lane >= 3 * s["quarter"])


def swap_layers(s, value):
    return pltpu.roll(value, 2 * s["quarter"], 1)


def weighted(taps, values):
    total = None
    for tap, value in zip(taps, values):
        if value is not None:
            total = tap * value if total is None else total + tap * value
    return total


def shifts_of(s, transposed):
    return [t - s["radius"] if transposed else s["radius"] - t for t in range(s["taps"])]


def own_sums(s, windows, matrix):
    layers, breadth = s["layers"], s["breadth"]
    value = jnp.concatenate([w.reshape(layers * w.shape[1], breadth) for w in windows], axis=1)
    upper = value.astype(BF16)
    lower = (value - upper.astype(F32)).astype(BF16)
    result = jnp.dot(matrix, jnp.concatenate([upper, lower, upper], axis=0), preferred_element_type=F32)
    return [
        [result[p * SUB:(p + 1) * SUB, k * breadth:(k + 1) * breadth] for p in range(layers)] for k in range(len(windows))
    ]


def side_sums(s, load, row_taps, depth_taps, transposed):
    layers, radius, pairs = s["layers"], s["radius"], s["pairs"]
    shifts = shifts_of(s, transposed)
    mixed = [weighted(row_taps, [load(layers + p, shift) for shift in shifts]) for p in range(pairs)]
    beyond = {}
    first = first_lanes(s)
    for step in range(1, radius + 1):
        beyond[-step] = jnp.where(first, 0.0, swap_layers(s, mixed[pairs - step]))
        beyond[pairs - 1 + step] = jnp.where(first, swap_layers(s, mixed[step - 1]), 0.0)
    at = lambda p: mixed[p] if 0 <= p < pairs else beyond.get(p)
    return [weighted(depth_taps, [at(p + shift) for shift in shifts]) for p in range(pairs)]


def slope_tile(s, source, shift, tile, divergence, flux_rows, where, rows_only=False):
    gy, gx, ny, nx = where
    layers, height, breadth, pairs, quarter = s["layers"], s["height"], s["breadth"], s["pairs"], s["quarter"]
    lane = lax.broadcasted_iota(jnp.int32, (SUB, breadth), 1)
    side_col = jnp.where(lax.rem(lane // quarter, 2) == 0, breadth + lax.rem(lane, quarter), lax.rem(lane, quarter) - quarter)
    masks = []
    for col in (lane, side_col):
        col = gx * breadth + col
        masks.append(jnp.where((col >= 0) & (col < nx * breadth - 1), 1.0, 0.0).astype(F32))
    start = tile * SUB
    row = gy * height + start - s["off"] + shift + lax.broadcasted_iota(jnp.int32, (SUB, breadth), 0)
    row_mask = jnp.where((row >= 0) & (row < ny * height - 1), 1.0, 0.0).astype(F32)
    at_edge = tile * SUB + shift - s["off"] in (-SUB, height - SUB)
    last, first = breadth - 1, first_lanes(s)
    rows = slice(start, start + SUB)

    def swap(value):
        return swap_layers(s, value)

    before = [None, None, None]
    heres = [source[plane, rows, :] for plane in (0, pairs, layers)]
    for p in range(pairs):
        planes = (p, p + pairs, layers + p)
        afters = [source[plane + 1, rows, :] if p + 1 < pairs else None for plane in planes]
        if p + 1 == pairs:
            afters[0] = source[pairs, rows, :]
            afters[2] = jnp.where(first, swap(source[layers, rows, :]), heres[2])
        rolled = [pltpu.roll(value, breadth - 1, 1) for value in heres]
        nexts = [
            jnp.where(lane == last, rolled[2], rolled[0]),
            jnp.where(lane == last, swap(rolled[2]), rolled[1]),
            jnp.where(lane == last, rolled[0], jnp.where(lane == 2 * quarter - 1, swap(rolled[1]), rolled[2])),
        ]
        f_cols, totals = [], []
        for k, plane in enumerate(planes):
            here = heres[k]
            step_rows = source[plane, start + 1:start + 1 + SUB, :] - here
            if at_edge:
                step_rows = step_rows * row_mask
            step_cols = (nexts[k] - here) * masks[k // 2]
            square = step_rows * step_rows + step_cols * step_cols + SMOOTHING * SMOOTHING
            if afters[k] is not None:
                step_depth = afters[k] - here
                square = square + step_depth * step_depth
            inverse = lax.rsqrt(square)
            f_rows = step_rows * inverse
            flux_rows[plane, rows, :] = f_rows
            if rows_only:
                continue
            f_cols.append(step_cols * inverse)
            total = -f_cols[k] - f_rows
            if before[k] is not None:
                total = total + before[k]
            before[k] = None
            if afters[k] is not None:
                before[k] = step_depth * inverse
                total = total - before[k]
            totals.append(total)
        heres = afters
        if rows_only:
            continue
        rolled = [pltpu.roll(value, 1, 1) for value in f_cols]
        totals[0] = totals[0] + jnp.where(lane == 0, rolled[2], rolled[0])
        totals[1] = totals[1] + jnp.where(lane == 0, swap(rolled[2]), rolled[1])
        totals[2] = totals[2] + jnp.where(lane == 0, rolled[0], jnp.where(lane == 2 * quarter, swap(rolled[1]), rolled[2]))
        for plane, total in zip(planes, totals):
            divergence[plane, rows, :] = total
    if rows_only:
        return
    divergence[pairs, rows, :] = divergence[pairs, rows, :] + before[0]
    divergence[layers, rows, :] = divergence[layers, rows, :] + jnp.where(first, 0.0, swap(before[2]))


def main_kernel(s, centre_ref, first_ref, second_ref, taps_ref, forward_ref, backward_ref, depth_ref,
                x1_ref, g1_ref, pull_ref, again_ref, part_ref,
                x0, x1, x2, g0, y0, y1, y2, r0, r1, r2, q0, q1, q2, acc, div, flux):
    where = place()
    gy, gx, ny, nx = where
    layers, height, breadth, off = s["layers"], s["height"], s["breadth"], s["off"]
    halo, radius, taps, pairs, planes, quarter = [s[k] for k in ("halo", "radius", "taps", "pairs", "planes", "quarter")]
    begin, end = s["first"], s["last"]
    col_even = lax.rem(gx, 2) == 0
    lane = lax.broadcasted_iota(jnp.int32, (1, breadth), 1)
    xs, ys, rs, qs = (x0, x1, x2), (y0, y1, y2), (r0, r1, r2), (q0, q1, q2)
    span = bands(s)

    def rows(tile, stop=None):
        return slice(tile * SUB, (tile + 1 if stop is None else stop) * SUB)

    top = off - halo
    x0[:layers, top:off + height + halo, :] = centre_ref[...]
    firsts = [first_ref[g] for g in range(s["groups"])]
    seconds = [second_ref[g] for g in range(s["groups"])]
    rights = [jnp.where(col_even, a, b) for a, b in zip(firsts, seconds)]
    lefts = [jnp.where(col_even, b, a) for a, b in zip(firsts, seconds)]
    for p in range(pairs):
        value = jnp.zeros((height + 2 * halo, breadth), F32)
        for groups, layer, to in ((rights, p, 0), (lefts, p + pairs, 2 * quarter - halo),
                                  (rights, p + pairs, 2 * quarter), (lefts, p, breadth - halo)):
            value = jnp.where((lane >= to) & (lane < to + halo), unpack_layer(s, groups, layer, to), value)
        x0[layers + p, top:off + height + halo, :] = value
    zero = jnp.zeros((planes, SUB, breadth), F32)
    for ref, tiles in ((y0, (0,)), (y2, (s["tiles"] - 1,)), (r0, (begin, begin + 1)),
                       (r1, (begin - 2, begin - 1, end, end + 1)), (r2, (end - 2, end - 1))):
        for tile in tiles:
            ref[:, rows(tile), :] = zero

    def product(ref, low, high, band, matrices, own_only=False):
        width = breadth if own_only else 2 * breadth
        count = (high - low) * SUB

        def split(a, b):
            value = ref[a:b, rows(low, high), :].reshape((b - a) * count, breadth)
            upper = value.astype(BF16)
            return upper, (value - upper.astype(F32)).astype(BF16)

        side_high, side_low = split(layers, planes)
        own, side = [], None
        for member in range(2):
            high_part, low_part = split(member * pairs, (member + 1) * pairs)
            parts = [high_part, side_high] * 2 + [low_part, side_low]
            result = jnp.dot(jnp.concatenate(parts, axis=1), matrices[2 * band + member, :, :width], preferred_element_type=F32)
            own.append(result[:, :breadth].reshape(pairs, count, breadth))
            if not own_only:
                rest = result[:, breadth:]
                side = rest if side is None else side + rest
        pieces = [(0, own[0]), (pairs, own[1])]
        return pieces if own_only else pieces + [(layers, side.reshape(pairs, count, breadth))]

    def taps_of(band, half):
        return [[taps_ref[band, dim, half, t] for t in range(taps)] for dim in (1, 0)]

    def one_pass(number):
        x = xs[number]
        low, high = reach(s, (5 - 2 * number) * radius)
        in_low, in_high = reach(s, (6 - 2 * number) * radius)
        back_low, back_high = reach(s, (4 - 2 * number) * radius)
        out = [(max(low, a), min(high, b)) for a, b in span]
        back = [(max(back_low, a - 1), min(back_high, b + 1)) for a, b in span]
        done = set()

        def columns(band):
            a, b = max(out[band][0] - 1, in_low), min(out[band][1] + 1, in_high)
            for plane, piece in product(x, a, b, band, forward_ref):
                ys[band][plane:plane + pairs, rows(a, b), :] = piece

        def sums(band, source, low, high, transposed, emit):
            row_taps, depth_taps = taps_of(band, 1)

            def load_at(tile):
                def load(plane, shift):
                    if transposed and ((tile < span[band][0] and shift <= 0) or (tile >= span[band][1] and shift >= 0)):
                        return None
                    return source[plane, tile * SUB + shift:(tile + 1) * SUB + shift, :]

                return load

            for at in range(low, high, 2):
                group = range(at, min(at + 2, high))
                matrix = depth_ref[2 * band + (1 if transposed else 0)]
                windows = [source[:layers, tile * SUB - radius:(tile + 1) * SUB + radius, :] for tile in group]
                results = own_sums(s, windows, matrix)
                for tile, result in zip(group, results):
                    side = side_sums(s, load_at(tile), row_taps, depth_taps, transposed)
                    for plane, value in enumerate(result + side):
                        emit(plane, tile, value)

        def blur_rows(band):
            def emit(plane, tile, value):
                rs[band][plane, rows(tile), :] = value if number == 2 else value - x0[plane, rows(tile), :]

            sums(band, ys[band], *out[band], False, emit)

        def back_rows(band):
            def emit(plane, tile, value):
                qs[band][plane, rows(tile), :] = value

            sums(band, rs[band], *back[band], True, emit)

        def back_columns(band):
            a, b = back[band]
            for plane, piece in product(qs[band], a, b, band, backward_ref, number == 2):
                for tile in range(a, b):
                    part = piece[:, (tile - a) * SUB:(tile - a + 1) * SUB, :]
                    at = slice(plane, plane + pairs)
                    acc[at, rows(tile), :] = acc[at, rows(tile), :] + part if tile in done else part
            done.update(range(a, b))

        def inside(tile, side):
            row = gy * height + tile * SUB - off + lax.broadcasted_iota(jnp.int32, (SUB, breadth), 0)
            here = lax.broadcasted_iota(jnp.int32, (SUB, breadth), 1)
            if side:
                part = lax.rem(here, quarter)
                here = jnp.where(lax.rem(here // quarter, 2) == 0, breadth + part, part - quarter)
            col = gx * breadth + here
            return (row >= 0) & (row < ny * height) & (col >= 0) & (col < nx * breadth)

        def update(tile):
            keep = [inside(tile, side) for side in range(2)]
            for plane in range(planes):
                here = x[plane, rows(tile), :]
                total = acc[plane, rows(tile), :] + DAMPING * here
                before = flux[plane, tile * SUB - 1:(tile + 1) * SUB - 1, :]
                total = total + WEIGHT_TV * (div[plane, rows(tile), :] + before)
                total = jnp.where(keep[plane // layers], total, 0.0)
                if number == 0:
                    xs[1][plane, rows(tile), :] = here - START_STEP * total
                    if plane < layers and begin <= tile < end:
                        g0[plane, rows(tile), :] = total
                else:
                    xs[2][plane, rows(tile), :] = total

        def slopes(a, b):
            if number < 2:
                for tile in range(a, b):
                    slope_tile(s, x, 0, tile, div, flux, where, tile < back_low)

        middle = (begin + end) // 2
        columns(0)
        slopes(back_low - 1, middle)
        columns(1)
        blur_rows(0)
        columns(2)
        back_rows(0)
        blur_rows(1)
        back_columns(0)
        back_rows(1)
        back_columns(1)
        blur_rows(2)
        slopes(middle, back_high)
        back_rows(2)
        back_columns(2)
        if number == 1:
            pull_ref[...] = acc[:layers, rows(begin, end), :]
        if number < 2:
            for tile in range(back_low, back_high):
                update(tile)

    for number in range(3):
        one_pass(number)
    again_ref[...] = acc[:layers, rows(begin, end), :]
    low, high = reach(s, 2 * radius)
    x1_ref[...] = x1[:, rows(low, high), :]
    g1_ref[...] = x2[:, rows(low, high), :]

    zero_sq = cross = one_sq = jnp.zeros((SUB, breadth), F32)
    for tile in range(begin, end):
        for layer in range(layers):
            a, b = g0[layer, rows(tile), :], x2[layer, rows(tile), :]
            zero_sq, cross, one_sq = zero_sq + a * a, cross + a * (b - a), one_sq + b * b
    zero_sq, cross, one_sq = [jnp.sum(t, axis=(0, 1), keepdims=True) for t in (zero_sq, cross, one_sq)]
    row = jnp.where(lane == 0, zero_sq, jnp.where(lane == 1, cross, one_sq))
    part_ref[...] = jnp.broadcast_to(row, part_ref.shape)


def step_kernel(s, sums_ref, x1_ref, g1_ref, pull_ref, again_ref, x2_ref, g2_ref, part_ref, keep_ref, x2, div, flux):
    where = place()
    layers, height, breadth = s["layers"], s["height"], s["breadth"]
    low, high = reach(s, 2 * s["radius"])
    lane = lax.broadcasted_iota(jnp.int32, (1, breadth), 1)
    total = jnp.sum(sums_ref[...], axis=0, keepdims=True)
    zero_sq, cross, one_sq = [
        jnp.sum(jnp.where(lane == number, total, 0.0), axis=(0, 1), keepdims=True) for number in range(3)
    ]
    step = (START_STEP * START_STEP * zero_sq) / (-START_STEP * cross)
    count = (high - low) * SUB
    for plane in range(s["planes"]):
        x2[plane, :count, :] = x1_ref[plane] - step * g1_ref[plane]
    begin = s["first"] - low
    total = jnp.zeros((SUB, breadth), F32)
    for tile in range(begin - 1, begin + height // SUB):
        slope_tile(s, x2, low * SUB, tile, div, flux, where, tile < begin)
        if tile < begin:
            continue
        at, out = slice(tile * SUB, (tile + 1) * SUB), slice((tile - begin) * SUB, (tile - begin + 1) * SUB)
        for layer in range(layers):
            here = x2[layer, at, :]
            slope = pull_ref[layer, out, :] - step * again_ref[layer, out, :] + DAMPING * here
            slope = slope + WEIGHT_TV * (div[layer, at, :] + flux[layer, tile * SUB - 1:(tile + 1) * SUB - 1, :])
            x2_ref[layer, out, :] = here
            g2_ref[layer, out, :] = slope
            old = g1_ref[layer, at, :]
            total = total + old * (slope - old)
    growth = -step * jnp.sum(total, axis=(0, 1), keepdims=True)
    part_ref[...] = jnp.broadcast_to(growth, part_ref.shape)
    keep_ref[...] = jnp.broadcast_to(step * step * one_sq, keep_ref.shape)


def final_kernel(sums_ref, keep_ref, x2_ref, g2_ref, out_ref):
    step = keep_ref[:1, :] / jnp.sum(sums_ref[...], axis=0, keepdims=True)
    for layer in range(x2_ref.shape[0]):
        out_ref[layer] = x2_ref[layer] - step * g2_ref[layer]


def pairings(count):
    def both(start):
        pairs = []
        for i in range(start, count - 1, 2):
            pairs += [(i, i + 1), (i + 1, i)]
        return pairs

    return both(0), both(1)


def call(kernel, outs, scratch=(), inputs=None):
    whole = pl.BlockSpec(memory_space=pltpu.VMEM)
    return pl.pallas_call(
        kernel,
        out_shape=outs,
        in_specs=inputs,
        out_specs=jax.tree.map(lambda _: whole, outs),
        scratch_shapes=list(scratch),
        compiler_params=pltpu.CompilerParams(vmem_limit_bytes=VMEM_BYTES),
    )


def per_device(observed, profiles, tile_index):
    layers, height, breadth = observed.shape
    s = plan(layers, height, breadth, profiles.shape[2])
    halo, rows, taps = s["halo"], s["rows"], s["taps"]
    ring = 2 * breadth
    gy = lax.axis_index("gy")
    n = lax.axis_size("gy") * lax.axis_size("gx")
    vmem, smem = pl.BlockSpec(memory_space=pltpu.VMEM), pl.BlockSpec(memory_space=pltpu.SMEM)
    sds = jax.ShapeDtypeStruct

    even = lax.rem(gy, 2) == 0
    bottom, top = jnp.int32(height - halo), jnp.int32(0)
    to_even = lax.dynamic_slice_in_dim(observed, jnp.where(even, bottom, top), halo, axis=1)
    to_odd = lax.dynamic_slice_in_dim(observed, jnp.where(even, top, bottom), halo, axis=1)
    first_pairs, second_pairs = pairings(lax.axis_size("gy"))
    from_even = lax.ppermute(to_even, "gy", first_pairs)
    from_odd = lax.ppermute(to_odd, "gy", second_pairs)

    packed = (s["groups"], height + 2 * halo, breadth)
    anywhere = pl.BlockSpec(memory_space=pl.ANY)
    taps_all, columns = call(
        functools.partial(weights_kernel, s),
        (sds((3, 2, 2, taps, SUB, breadth), F32), sds((3, taps, SUB, ring), F32)), inputs=[smem, smem],
    )(tile_index, profiles.transpose(2, 1, 0))
    tile_here = call(copy_kernel, sds(observed.shape, F32), inputs=[vmem])(observed)
    first, second, centre = call(
        functools.partial(pack_kernel, s),
        (sds(packed, F32), sds(packed, F32), sds((layers, height + 2 * halo, breadth), F32)),
        inputs=[vmem] * 3 + [anywhere],
    )(tile_here, from_even, from_odd, taps_all)
    matrices = sds((6, 3 * ring, ring), BF16)
    size = layers * (SUB + 2 * s["radius"])
    forward, backward, depth = call(
        functools.partial(matrices_kernel, s), (matrices, matrices, sds((6, layers * SUB, 3 * size), BF16)),
        scratch=[pltpu.VMEM((ring, ring), F32)], inputs=[vmem, vmem, anywhere],
    )(columns, taps_all, second)
    first, backward = lax.optimization_barrier((first, backward))
    first_pairs, second_pairs = pairings(lax.axis_size("gx"))
    got_first = lax.ppermute(first, "gx", first_pairs)
    got_second = lax.ppermute(second, "gx", second_pairs)

    big = (s["planes"], rows, breadth)
    low, high = reach(s, 2 * s["radius"])
    wide = (s["planes"], (high - low) * SUB, breadth)
    tile = sds((layers, height, breadth), F32)
    x1, g1, pull, again, part = call(
        functools.partial(main_kernel, s),
        (sds(wide, F32), sds(wide, F32), tile, tile, sds((n, breadth), F32)),
        scratch=[pltpu.VMEM(shape, F32) for shape in [big] * 3 + [(layers, rows, breadth)] + [big] * 12],
        inputs=[vmem] * 7,
    )(centre, got_first, got_second, taps_all, forward, backward, depth)
    sums = lax.all_to_all(part, ("gy", "gx"), 0, 0, tiled=True)
    work = pltpu.VMEM((s["planes"], (high - low + 1) * SUB, breadth), F32)
    x2, g2, part, keep = call(
        functools.partial(step_kernel, s),
        (tile, tile, sds((n, breadth), F32), sds((SUB, breadth), F32)),
        scratch=[work] * 3,
        inputs=[vmem] * 5,
    )(sums, x1, g1, pull, again)
    sums = lax.all_to_all(part, ("gy", "gx"), 0, 0, tiled=True)
    return call(final_kernel, tile, inputs=[vmem] * 4)(sums, keep, x2, g2)


def solution(mesh):
    in_specs = (P(None, "gy", "gx"), P(), P())
    out_specs = P(None, "gy", "gx")
    return jax.shard_map(
        per_device, mesh=mesh, in_specs=in_specs, out_specs=out_specs, check_vma=False
    )
```

```python
import functools
import jax
import jax.numpy as jnp
from jax import lax
from jax.experimental import pallas as pl
from jax.experimental.pallas import tpu as pltpu
from jax.sharding import PartitionSpec as P

ITERS = 2
WEIGHT_TV = 0.02
SMOOTHING = 0.1
DAMPING = 0.05
START_STEP = 0.5
SUB = 8
F32 = jnp.float32
BF16 = jnp.bfloat16
VMEM_BYTES = 36 * 1024 * 1024


def plan(layers, height, breadth, taps):
    radius = (taps - 1) // 2
    halo = 6 * radius
    off = -(-halo // SUB) * SUB + SUB
    return dict(
        layers=layers, height=height, breadth=breadth, taps=taps, radius=radius, halo=halo, off=off,
        rows=height + 2 * off, groups=-(-layers * halo // breadth), pairs=layers // 2, planes=layers + layers // 2, quarter=breadth // 4, first=off // SUB, last=(off + height) // SUB,
        tiles=(height + 2 * off) // SUB,
    )


def reach(s, extent):
    low = (s["off"] - extent) // SUB
    high = -(-(s["off"] + s["height"] + extent) // SUB)
    return low, high


def bands(s):
    return ((0, s["first"]), (s["first"], s["last"]), (s["last"], s["tiles"]))


def place():
    return lax.axis_index("gy"), lax.axis_index("gx"), lax.axis_size("gy"), lax.axis_size("gx")


def column_of(s, place, member):
    breadth, quarter = s["breadth"], s["quarter"]
    side = place - breadth
    right, left = (0, 3 * quarter) if member == 0 else (2 * quarter, quarter)
    column = jnp.where((side >= right) & (side < right + quarter), breadth + side - right, 1 << 20)
    column = jnp.where((side >= left) & (side < left + quarter), side - left - quarter, column)
    return jnp.where(place < breadth, place, column)


def weights_kernel(s, index_ref, profiles_ref, taps_ref, columns_ref):
    gy, gx, ny, nx = place()
    breadth, taps = s["breadth"], s["taps"]
    lane = lax.broadcasted_iota(jnp.int32, (SUB, breadth), 1)
    is_right = lax.rem(lane // s["quarter"], 2) == 0
    for band in range(3):
        row = gy + (band - 1)
        picked = []
        for side in range(3):
            col = gx + (side - 1)
            inside = (row >= 0) & (row < ny) & (col >= 0) & (col < nx)
            number = index_ref[jnp.clip(row, 0, ny - 1), jnp.clip(col, 0, nx - 1)]
            picked.append((inside, number))
        for dim in range(3):
            for tap in range(taps):
                left, centre, right = [
                    jnp.where(inside, profiles_ref[tap, dim, number], 0.0) for inside, number in picked
                ]
                own, side = jnp.full((SUB, breadth), centre, F32), jnp.where(is_right, right, left)
                if dim < 2:
                    taps_ref[band, dim, 0, tap] = own
                    taps_ref[band, dim, 1, tap] = side
                else:
                    columns_ref[band, tap] = jnp.concatenate([own, side], axis=1)


def matrices_kernel(s, columns_ref, taps_ref, after_ref, centre_ref, forward_ref, backward_ref, depth_ref, first_ref, full):
    _, gx, _, _ = place()
    for start in range(0, centre_ref.shape[1], 2 * SUB):
        values = [centre_ref[layer, start:start + 2 * SUB, :] for layer in range(s["layers"])]
        pack_strips(s, values, lax.rem(gx, 2) == 0, first_ref, start)
    breadth, taps, radius = s["breadth"], s["taps"], s["radius"]
    ring = 2 * breadth
    chunk = 32
    target = lax.broadcasted_iota(jnp.int32, (1, ring), 1)
    for number in range(6):
        band, member = divmod(number, 2)
        columns = [columns_ref[band, t, :1, :] for t in range(taps)]
        reached = column_of(s, target, member)
        reached = jnp.where(reached < 1 << 19, reached + radius, -(1 << 20))
        for start in range(0, ring, chunk):
            source = lax.broadcasted_iota(jnp.int32, (chunk, 1), 0) + start
            distance = reached - column_of(s, source, member)
            total = jnp.zeros((chunk, ring), F32)
            for tap in range(taps):
                total = jnp.where(distance == tap, columns[tap], total)
            full[start:start + chunk, :] = total
        matrix = full[...]
        for ref, value in ((forward_ref, matrix), (backward_ref, matrix.T)):
            upper = value.astype(BF16)
            ref[number, :ring, :] = upper
            ref[number, ring:2 * ring, :] = (value - upper.astype(F32)).astype(BF16)
            ref[number, 2 * ring:, :] = upper
    window = SUB + 2 * radius
    size = s["layers"] * window
    place_in = lax.broadcasted_iota(jnp.int32, (SUB, size), 1)
    layer_in, row_in = place_in // window, lax.rem(place_in, window)
    row_out = lax.broadcasted_iota(jnp.int32, (SUB, size), 0)

    def wide(band, dim, tap):
        return jnp.broadcast_to(taps_ref[band, dim, 0, tap][:1, :1], (SUB, size))

    for band in range(3):
        for transposed in range(2):
            number = 2 * band + transposed
            apart = row_in - row_out if transposed else row_out + 2 * radius - row_in
            by_row = jnp.zeros((SUB, size), F32)
            for tap in range(taps):
                by_row = jnp.where(apart == tap, wide(band, 1, tap), by_row)
            depth_taps = [wide(band, 0, tap) for tap in range(taps)]
            for layer in range(s["layers"]):
                apart = layer_in - layer + radius if transposed else layer - layer_in + radius
                value = jnp.zeros((SUB, size), F32)
                for tap in range(taps):
                    value = jnp.where(apart == tap, depth_taps[tap], value)
                full[layer * SUB:(layer + 1) * SUB, :size] = value * by_row
            value = full[:s["layers"] * SUB, :size]
            upper = value.astype(BF16)
            depth_ref[number, :, :size] = upper
            depth_ref[number, :, size:2 * size] = upper
            depth_ref[number, :, 2 * size:] = (value - upper.astype(F32)).astype(BF16)


def strip_places(s, layer):
    group, lane = divmod(layer * s["halo"], s["breadth"])
    return group, lane, min(s["halo"], s["breadth"] - lane)


def copy_kernel(tile_ref, out_ref):
    out_ref[...] = tile_ref[...]


def pack_strips(s, values, right, out_ref, start):
    halo, breadth = s["halo"], s["breadth"]
    lane = lax.broadcasted_iota(jnp.int32, (1, breadth), 1)
    count = values[0].shape[0]
    total = [jnp.zeros((count, breadth), F32)] * s["groups"]
    for layer, value in enumerate(values):
        group, begin, here = strip_places(s, layer)
        moved = pltpu.roll(value, jnp.where(right, (begin + halo) % breadth, begin), 1)
        total[group] = jnp.where((lane >= begin) & (lane < begin + here), moved, total[group])
        if here < halo:
            total[group + 1] = jnp.where(lane < halo - here, moved, total[group + 1])
    for number in range(s["groups"]):
        out_ref[number, start:start + count, :] = total[number]


def pack_kernel(s, tile_ref, even_ref, odd_ref, after_ref, second_ref, centre_ref):
    gy, gx, _, _ = place()
    halo, height = s["halo"], s["height"]
    row_even = lax.rem(gy, 2) == 0
    for start, count in ((0, halo), (halo, height), (halo + height, halo)):
        values = []
        for layer in range(s["layers"]):
            if start == halo:
                value = tile_ref[layer]
            elif start == 0:
                value = jnp.where(row_even, odd_ref[layer], even_ref[layer])
            else:
                value = jnp.where(row_even, even_ref[layer], odd_ref[layer])
            centre_ref[layer, start:start + count, :] = value
            values.append(value)
        pack_strips(s, values, lax.rem(gx, 2) == 1, second_ref, start)


def unpack_layer(s, groups, layer, to):
    breadth = s["breadth"]
    lane = lax.broadcasted_iota(jnp.int32, (1, breadth), 1)
    group, begin, here = strip_places(s, layer)
    value = groups[group]
    if here < s["halo"]:
        value = jnp.where(lane >= begin, value, groups[group + 1])
    shift = (to - begin) % breadth
    return pltpu.roll(value, shift, 1) if shift else value


def first_lanes(s):
    lane = lax.broadcasted_iota(jnp.int32, (1, s["breadth"]), 1)
    return (lane < s["quarter"]) | (lane >= 3 * s["quarter"])


def swap_layers(s, value):
    return pltpu.roll(value, 2 * s["quarter"], 1)


def weighted(taps, values):
    total = None
    for tap, value in zip(taps, values):
        if value is not None:
            total = tap * value if total is None else total + tap * value
    return total


def shifts_of(s, transposed):
    return [t - s["radius"] if transposed else s["radius"] - t for t in range(s["taps"])]


def own_sums(s, windows, matrix):
    layers, breadth = s["layers"], s["breadth"]
    value = jnp.concatenate([w.reshape(layers * w.shape[1], breadth) for w in windows], axis=1)
    upper = value.astype(BF16)
    lower = (value - upper.astype(F32)).astype(BF16)
    result = jnp.dot(matrix, jnp.concatenate([upper, lower, upper], axis=0), preferred_element_type=F32)
    return [
        [result[p * SUB:(p + 1) * SUB, k * breadth:(k + 1) * breadth] for p in range(layers)] for k in range(len(windows))
    ]


def side_sums(s, load, row_taps, depth_taps, transposed):
    layers, radius, pairs = s["layers"], s["radius"], s["pairs"]
    shifts = shifts_of(s, transposed)
    mixed = [weighted(row_taps, [load(layers + p, shift) for shift in shifts]) for p in range(pairs)]
    beyond = {}
    first = first_lanes(s)
    for step in range(1, radius + 1):
        beyond[-step] = jnp.where(first, 0.0, swap_layers(s, mixed[pairs - step]))
        beyond[pairs - 1 + step] = jnp.where(first, swap_layers(s, mixed[step - 1]), 0.0)
    at = lambda p: mixed[p] if 0 <= p < pairs else beyond.get(p)
    return [weighted(depth_taps, [at(p + shift) for shift in shifts]) for p in range(pairs)]


def slope_tile(s, source, shift, tile, divergence, flux_rows, where, rows_only=False):
    gy, gx, ny, nx = where
    layers, height, breadth, pairs, quarter = s["layers"], s["height"], s["breadth"], s["pairs"], s["quarter"]
    lane = lax.broadcasted_iota(jnp.int32, (SUB, breadth), 1)
    side_col = jnp.where(lax.rem(lane // quarter, 2) == 0, breadth + lax.rem(lane, quarter), lax.rem(lane, quarter) - quarter)
    masks = []
    for col in (lane, side_col):
        col = gx * breadth + col
        masks.append(jnp.where((col >= 0) & (col < nx * breadth - 1), 1.0, 0.0).astype(F32))
    start = tile * SUB
    row = gy * height + start - s["off"] + shift + lax.broadcasted_iota(jnp.int32, (SUB, breadth), 0)
    row_mask = jnp.where((row >= 0) & (row < ny * height - 1), 1.0, 0.0).astype(F32)
    at_edge = tile * SUB + shift - s["off"] in (-SUB, height - SUB)
    last, first = breadth - 1, first_lanes(s)
    rows = slice(start, start + SUB)

    def swap(value):
        return swap_layers(s, value)

    before = [None, None, None]
    heres = [source[plane, rows, :] for plane in (0, pairs, layers)]
    for p in range(pairs):
        planes = (p, p + pairs, layers + p)
        afters = [source[plane + 1, rows, :] if p + 1 < pairs else None for plane in planes]
        if p + 1 == pairs:
            afters[0] = source[pairs, rows, :]
            afters[2] = jnp.where(first, swap(source[layers, rows, :]), heres[2])
        rolled = [pltpu.roll(value, breadth - 1, 1) for value in heres]
        nexts = [
            jnp.where(lane == last, rolled[2], rolled[0]),
            jnp.where(lane == last, swap(rolled[2]), rolled[1]),
            jnp.where(lane == last, rolled[0], jnp.where(lane == 2 * quarter - 1, swap(rolled[1]), rolled[2])),
        ]
        f_cols, totals = [], []
        for k, plane in enumerate(planes):
            here = heres[k]
            step_rows = source[plane, start + 1:start + 1 + SUB, :] - here
            if at_edge:
                step_rows = step_rows * row_mask
            step_cols = (nexts[k] - here) * masks[k // 2]
            square = step_rows * step_rows + step_cols * step_cols + SMOOTHING * SMOOTHING
            if afters[k] is not None:
                step_depth = afters[k] - here
                square = square + step_depth * step_depth
            inverse = lax.rsqrt(square)
            f_rows = step_rows * inverse
            flux_rows[plane, rows, :] = f_rows
            if rows_only:
                continue
            f_cols.append(step_cols * inverse)
            total = -f_cols[k] - f_rows
            if before[k] is not None:
                total = total + before[k]
            before[k] = None
            if afters[k] is not None:
                before[k] = step_depth * inverse
                total = total - before[k]
            totals.append(total)
        heres = afters
        if rows_only:
            continue
        rolled = [pltpu.roll(value, 1, 1) for value in f_cols]
        totals[0] = totals[0] + jnp.where(lane == 0, rolled[2], rolled[0])
        totals[1] = totals[1] + jnp.where(lane == 0, swap(rolled[2]), rolled[1])
        totals[2] = totals[2] + jnp.where(lane == 0, rolled[0], jnp.where(lane == 2 * quarter, swap(rolled[1]), rolled[2]))
        for plane, total in zip(planes, totals):
            divergence[plane, rows, :] = total
    if rows_only:
        return
    divergence[pairs, rows, :] = divergence[pairs, rows, :] + before[0]
    divergence[layers, rows, :] = divergence[layers, rows, :] + jnp.where(first, 0.0, swap(before[2]))


def main_kernel(s, centre_ref, first_ref, second_ref, taps_ref, forward_ref, backward_ref, depth_ref,
                x1_ref, g1_ref, pull_ref, again_ref, part_ref,
                x0, x1, x2, g0, y0, y1, y2, r0, r1, r2, q0, q1, q2, acc, div, flux):
    where = place()
    gy, gx, ny, nx = where
    layers, height, breadth, off = s["layers"], s["height"], s["breadth"], s["off"]
    halo, radius, taps, pairs, planes, quarter = [s[k] for k in ("halo", "radius", "taps", "pairs", "planes", "quarter")]
    begin, end = s["first"], s["last"]
    col_even = lax.rem(gx, 2) == 0
    lane = lax.broadcasted_iota(jnp.int32, (1, breadth), 1)
    xs, ys, rs, qs = (x0, x1, x2), (y0, y1, y2), (r0, r1, r2), (q0, q1, q2)
    span = bands(s)

    def rows(tile, stop=None):
        return slice(tile * SUB, (tile + 1 if stop is None else stop) * SUB)

    top = off - halo
    x0[:layers, top:off + height + halo, :] = centre_ref[...]
    firsts = [first_ref[g] for g in range(s["groups"])]
    seconds = [second_ref[g] for g in range(s["groups"])]
    rights = [jnp.where(col_even, a, b) for a, b in zip(firsts, seconds)]
    lefts = [jnp.where(col_even, b, a) for a, b in zip(firsts, seconds)]
    for p in range(pairs):
        value = jnp.zeros((height + 2 * halo, breadth), F32)
        for groups, layer, to in ((rights, p, 0), (lefts, p + pairs, 2 * quarter - halo),
                                  (rights, p + pairs, 2 * quarter), (lefts, p, breadth - halo)):
            value = jnp.where((lane >= to) & (lane < to + halo), unpack_layer(s, groups, layer, to), value)
        x0[layers + p, top:off + height + halo, :] = value
    zero = jnp.zeros((planes, SUB, breadth), F32)
    for ref, tiles in ((y0, (0,)), (y2, (s["tiles"] - 1,)), (r0, (begin, begin + 1)),
                       (r1, (begin - 2, begin - 1, end, end + 1)), (r2, (end - 2, end - 1))):
        for tile in tiles:
            ref[:, rows(tile), :] = zero

    def product(ref, low, high, band, matrices, own_only=False):
        width = breadth if own_only else 2 * breadth
        count = (high - low) * SUB

        def split(a, b):
            value = ref[a:b, rows(low, high), :].reshape((b - a) * count, breadth)
            upper = value.astype(BF16)
            return upper, (value - upper.astype(F32)).astype(BF16)

        side_high, side_low = split(layers, planes)
        own, side = [], None
        for member in range(2):
            high_part, low_part = split(member * pairs, (member + 1) * pairs)
            parts = [high_part, side_high] * 2 + [low_part, side_low]
            result = jnp.dot(jnp.concatenate(parts, axis=1), matrices[2 * band + member, :, :width], preferred_element_type=F32)
            own.append(result[:, :breadth].reshape(pairs, count, breadth))
            if not own_only:
                rest = result[:, breadth:]
                side = rest if side is None else side + rest
        pieces = [(0, own[0]), (pairs, own[1])]
        return pieces if own_only else pieces + [(layers, side.reshape(pairs, count, breadth))]

    def taps_of(band, half):
        return [[taps_ref[band, dim, half, t] for t in range(taps)] for dim in (1, 0)]

    def one_pass(number):
        x = xs[number]
        low, high = reach(s, (5 - 2 * number) * radius)
        in_low, in_high = reach(s, (6 - 2 * number) * radius)
        back_low, back_high = reach(s, (4 - 2 * number) * radius)
        out = [(max(low, a), min(high, b)) for a, b in span]
        back = [(max(back_low, a - 1), min(back_high, b + 1)) for a, b in span]
        done = set()

        def columns(band):
            a, b = max(out[band][0] - 1, in_low), min(out[band][1] + 1, in_high)
            for plane, piece in product(x, a, b, band, forward_ref):
                ys[band][plane:plane + pairs, rows(a, b), :] = piece

        def sums(band, source, low, high, transposed, emit):
            row_taps, depth_taps = taps_of(band, 1)

            def load_at(tile):
                def load(plane, shift):
                    if transposed and ((tile < span[band][0] and shift <= 0) or (tile >= span[band][1] and shift >= 0)):
                        return None
                    return source[plane, tile * SUB + shift:(tile + 1) * SUB + shift, :]

                return load

            for at in range(low, high, 2):
                group = range(at, min(at + 2, high))
                matrix = depth_ref[2 * band + (1 if transposed else 0)]
                windows = [source[:layers, tile * SUB - radius:(tile + 1) * SUB + radius, :] for tile in group]
                results = own_sums(s, windows, matrix)
                for tile, result in zip(group, results):
                    side = side_sums(s, load_at(tile), row_taps, depth_taps, transposed)
                    for plane, value in enumerate(result + side):
                        emit(plane, tile, value)

        def blur_rows(band):
            def emit(plane, tile, value):
                rs[band][plane, rows(tile), :] = value if number == 2 else value - x0[plane, rows(tile), :]

            sums(band, ys[band], *out[band], False, emit)

        def back_rows(band):
            def emit(plane, tile, value):
                qs[band][plane, rows(tile), :] = value

            sums(band, rs[band], *back[band], True, emit)

        def back_columns(band):
            a, b = back[band]
            for plane, piece in product(qs[band], a, b, band, backward_ref, number == 2):
                for tile in range(a, b):
                    part = piece[:, (tile - a) * SUB:(tile - a + 1) * SUB, :]
                    at = slice(plane, plane + pairs)
                    acc[at, rows(tile), :] = acc[at, rows(tile), :] + part if tile in done else part
            done.update(range(a, b))

        def inside(tile, side):
            row = gy * height + tile * SUB - off + lax.broadcasted_iota(jnp.int32, (SUB, breadth), 0)
            here = lax.broadcasted_iota(jnp.int32, (SUB, breadth), 1)
            if side:
                part = lax.rem(here, quarter)
                here = jnp.where(lax.rem(here // quarter, 2) == 0, breadth + part, part - quarter)
            col = gx * breadth + here
            return (row >= 0) & (row < ny * height) & (col >= 0) & (col < nx * breadth)

        def update(tile):
            keep = [inside(tile, side) for side in range(2)]
            for plane in range(planes):
                here = x[plane, rows(tile), :]
                total = acc[plane, rows(tile), :] + DAMPING * here
                before = flux[plane, tile * SUB - 1:(tile + 1) * SUB - 1, :]
                total = total + WEIGHT_TV * (div[plane, rows(tile), :] + before)
                total = jnp.where(keep[plane // layers], total, 0.0)
                if number == 0:
                    xs[1][plane, rows(tile), :] = here - START_STEP * total
                    if plane < layers and begin <= tile < end:
                        g0[plane, rows(tile), :] = total
                else:
                    xs[2][plane, rows(tile), :] = total

        def slopes(a, b):
            if number < 2:
                for tile in range(a, b):
                    slope_tile(s, x, 0, tile, div, flux, where, tile < back_low)

        middle = (begin + end) // 2
        columns(0)
        slopes(back_low - 1, middle)
        columns(1)
        blur_rows(0)
        columns(2)
        back_rows(0)
        blur_rows(1)
        back_columns(0)
        back_rows(1)
        back_columns(1)
        blur_rows(2)
        slopes(middle, back_high)
        back_rows(2)
        back_columns(2)
        if number == 1:
            pull_ref[...] = acc[:layers, rows(begin, end), :]
        if number < 2:
            for tile in range(back_low, back_high):
                update(tile)

    for number in range(3):
        one_pass(number)
    again_ref[...] = acc[:layers, rows(begin, end), :]
    low, high = reach(s, 2 * radius)
    x1_ref[...] = x1[:, rows(low, high), :]
    g1_ref[...] = x2[:, rows(low, high), :]

    zero_sq = cross = one_sq = jnp.zeros((SUB, breadth), F32)
    for tile in range(begin, end):
        for layer in range(layers):
            a, b = g0[layer, rows(tile), :], x2[layer, rows(tile), :]
            zero_sq, cross, one_sq = zero_sq + a * a, cross + a * (b - a), one_sq + b * b
    zero_sq, cross, one_sq = [jnp.sum(t, axis=(0, 1), keepdims=True) for t in (zero_sq, cross, one_sq)]
    row = jnp.where(lane == 0, zero_sq, jnp.where(lane == 1, cross, one_sq))
    part_ref[...] = jnp.broadcast_to(row, part_ref.shape)


def step_kernel(s, sums_ref, x1_ref, g1_ref, pull_ref, again_ref, x2_ref, g2_ref, part_ref, keep_ref, x2, div, flux):
    where = place()
    layers, height, breadth = s["layers"], s["height"], s["breadth"]
    low, high = reach(s, 2 * s["radius"])
    lane = lax.broadcasted_iota(jnp.int32, (1, breadth), 1)
    total = jnp.sum(sums_ref[...], axis=0, keepdims=True)
    zero_sq, cross, one_sq = [
        jnp.sum(jnp.where(lane == number, total, 0.0), axis=(0, 1), keepdims=True) for number in range(3)
    ]
    step = (START_STEP * START_STEP * zero_sq) / (-START_STEP * cross)
    count = (high - low) * SUB
    for plane in range(s["planes"]):
        x2[plane, :count, :] = x1_ref[plane] - step * g1_ref[plane]
    begin = s["first"] - low
    total = jnp.zeros((SUB, breadth), F32)
    for tile in range(begin - 1, begin + height // SUB):
        slope_tile(s, x2, low * SUB, tile, div, flux, where, tile < begin)
        if tile < begin:
            continue
        at, out = slice(tile * SUB, (tile + 1) * SUB), slice((tile - begin) * SUB, (tile - begin + 1) * SUB)
        for layer in range(layers):
            here = x2[layer, at, :]
            slope = pull_ref[layer, out, :] - step * again_ref[layer, out, :] + DAMPING * here
            slope = slope + WEIGHT_TV * (div[layer, at, :] + flux[layer, tile * SUB - 1:(tile + 1) * SUB - 1, :])
            x2_ref[layer, out, :] = here
            g2_ref[layer, out, :] = slope
            old = g1_ref[layer, at, :]
            total = total + old * (slope - old)
    growth = -step * jnp.sum(total, axis=(0, 1), keepdims=True)
    part_ref[...] = jnp.broadcast_to(growth, part_ref.shape)
    keep_ref[...] = jnp.broadcast_to(step * step * one_sq, keep_ref.shape)


def final_kernel(sums_ref, keep_ref, x2_ref, g2_ref, out_ref):
    step = keep_ref[:1, :] / jnp.sum(sums_ref[...], axis=0, keepdims=True)
    for layer in range(x2_ref.shape[0]):
        out_ref[layer] = x2_ref[layer] - step * g2_ref[layer]


def pairings(count):
    def both(start):
        pairs = []
        for i in range(start, count - 1, 2):
            pairs += [(i, i + 1), (i + 1, i)]
        return pairs

    return both(0), both(1)


def call(kernel, outs, scratch=(), inputs=None):
    whole = pl.BlockSpec(memory_space=pltpu.VMEM)
    return pl.pallas_call(
        kernel,
        out_shape=outs,
        in_specs=inputs,
        out_specs=jax.tree.map(lambda _: whole, outs),
        scratch_shapes=list(scratch),
        compiler_params=pltpu.CompilerParams(vmem_limit_bytes=VMEM_BYTES),
    )


def per_device(observed, profiles, tile_index):
    layers, height, breadth = observed.shape
    s = plan(layers, height, breadth, profiles.shape[2])
    halo, rows, taps = s["halo"], s["rows"], s["taps"]
    ring = 2 * breadth
    gy = lax.axis_index("gy")
    n = lax.axis_size("gy") * lax.axis_size("gx")
    vmem, smem = pl.BlockSpec(memory_space=pltpu.VMEM), pl.BlockSpec(memory_space=pltpu.SMEM)
    sds = jax.ShapeDtypeStruct

    even = lax.rem(gy, 2) == 0
    bottom, top = jnp.int32(height - halo), jnp.int32(0)
    to_even = lax.dynamic_slice_in_dim(observed, jnp.where(even, bottom, top), halo, axis=1)
    to_odd = lax.dynamic_slice_in_dim(observed, jnp.where(even, top, bottom), halo, axis=1)
    first_pairs, second_pairs = pairings(lax.axis_size("gy"))
    from_even = lax.ppermute(to_even, "gy", first_pairs)
    from_odd = lax.ppermute(to_odd, "gy", second_pairs)

    packed = (s["groups"], height + 2 * halo, breadth)
    anywhere = pl.BlockSpec(memory_space=pl.ANY)
    taps_all, columns = call(
        functools.partial(weights_kernel, s),
        (sds((3, 2, 2, taps, SUB, breadth), F32), sds((3, taps, SUB, ring), F32)), inputs=[smem, smem],
    )(tile_index, profiles.transpose(2, 1, 0))
    tile_here = call(copy_kernel, sds(observed.shape, F32), inputs=[vmem])(observed)
    second, centre = call(
        functools.partial(pack_kernel, s),
        (sds(packed, F32), sds((layers, height + 2 * halo, breadth), F32)),
        inputs=[vmem] * 3 + [anywhere],
    )(tile_here, from_even, from_odd, taps_all)
    matrices = sds((6, 3 * ring, ring), BF16)
    size = layers * (SUB + 2 * s["radius"])
    forward, backward, depth, first = call(
        functools.partial(matrices_kernel, s), (matrices, matrices, sds((6, layers * SUB, 3 * size), BF16), sds(packed, F32)),
        scratch=[pltpu.VMEM((ring, ring), F32)], inputs=[vmem, vmem, anywhere, vmem],
    )(columns, taps_all, second, centre)
    first_pairs, second_pairs = pairings(lax.axis_size("gx"))
    got_first = lax.ppermute(first, "gx", first_pairs)
    got_second = lax.ppermute(second, "gx", second_pairs)

    big = (s["planes"], rows, breadth)
    low, high = reach(s, 2 * s["radius"])
    wide = (s["planes"], (high - low) * SUB, breadth)
    tile = sds((layers, height, breadth), F32)
    x1, g1, pull, again, part = call(
        functools.partial(main_kernel, s),
        (sds(wide, F32), sds(wide, F32), tile, tile, sds((n, breadth), F32)),
        scratch=[pltpu.VMEM(shape, F32) for shape in [big] * 3 + [(layers, rows, breadth)] + [big] * 12],
        inputs=[vmem] * 7,
    )(centre, got_first, got_second, taps_all, forward, backward, depth)
    sums = lax.all_to_all(part, ("gy", "gx"), 0, 0, tiled=True)
    work = pltpu.VMEM((s["planes"], (high - low + 1) * SUB, breadth), F32)
    x2, g2, part, keep = call(
        functools.partial(step_kernel, s),
        (tile, tile, sds((n, breadth), F32), sds((SUB, breadth), F32)),
        scratch=[work] * 3,
        inputs=[vmem] * 5,
    )(sums, x1, g1, pull, again)
    sums = lax.all_to_all(part, ("gy", "gx"), 0, 0, tiled=True)
    return call(final_kernel, tile, inputs=[vmem] * 4)(sums, keep, x2, g2)


def solution(mesh):
    in_specs = (P(None, "gy", "gx"), P(), P())
    out_specs = P(None, "gy", "gx")
    return jax.shard_map(
        per_device, mesh=mesh, in_specs=in_specs, out_specs=out_specs, check_vma=False
    )
```

```python
import functools
import jax
import jax.numpy as jnp
from jax import lax
from jax.experimental import pallas as pl
from jax.experimental.pallas import tpu as pltpu
from jax.sharding import PartitionSpec as P

ITERS = 2
WEIGHT_TV = 0.02
SMOOTHING = 0.1
DAMPING = 0.05
START_STEP = 0.5
SUB = 8
F32 = jnp.float32
BF16 = jnp.bfloat16
VMEM_BYTES = 36 * 1024 * 1024


def plan(layers, height, breadth, taps):
    radius = (taps - 1) // 2
    halo = 6 * radius
    off = -(-halo // SUB) * SUB + SUB
    return dict(
        layers=layers, height=height, breadth=breadth, taps=taps, radius=radius, halo=halo, off=off,
        rows=height + 2 * off, groups=-(-layers * halo // breadth), pairs=layers // 2, planes=layers + layers // 2, quarter=breadth // 4, first=off // SUB, last=(off + height) // SUB,
        tiles=(height + 2 * off) // SUB,
    )


def reach(s, extent):
    low = (s["off"] - extent) // SUB
    high = -(-(s["off"] + s["height"] + extent) // SUB)
    return low, high


def bands(s):
    return ((0, s["first"]), (s["first"], s["last"]), (s["last"], s["tiles"]))


def place():
    return lax.axis_index("gy"), lax.axis_index("gx"), lax.axis_size("gy"), lax.axis_size("gx")


def column_of(s, place, member):
    breadth, quarter = s["breadth"], s["quarter"]
    side = place - breadth
    right, left = (0, 3 * quarter) if member == 0 else (2 * quarter, quarter)
    column = jnp.where((side >= right) & (side < right + quarter), breadth + side - right, 1 << 20)
    column = jnp.where((side >= left) & (side < left + quarter), side - left - quarter, column)
    return jnp.where(place < breadth, place, column)


def weights_kernel(s, index_ref, profiles_ref, taps_ref, columns_ref):
    gy, gx, ny, nx = place()
    breadth, taps = s["breadth"], s["taps"]
    lane = lax.broadcasted_iota(jnp.int32, (SUB, breadth), 1)
    is_right = lax.rem(lane // s["quarter"], 2) == 0
    for band in range(3):
        row = gy + (band - 1)
        picked = []
        for side in range(3):
            col = gx + (side - 1)
            inside = (row >= 0) & (row < ny) & (col >= 0) & (col < nx)
            number = index_ref[jnp.clip(row, 0, ny - 1), jnp.clip(col, 0, nx - 1)]
            picked.append((inside, number))
        for dim in range(3):
            for tap in range(taps):
                left, centre, right = [
                    jnp.where(inside, profiles_ref[tap, dim, number], 0.0) for inside, number in picked
                ]
                own, side = jnp.full((SUB, breadth), centre, F32), jnp.where(is_right, right, left)
                if dim < 2:
                    taps_ref[band, dim, 0, tap] = own
                    taps_ref[band, dim, 1, tap] = side
                else:
                    columns_ref[band, tap] = jnp.concatenate([own, side], axis=1)


def matrices_kernel(s, columns_ref, taps_ref, after_ref, centre_ref, forward_ref, backward_ref, depth_ref, first_ref, full):
    _, gx, _, _ = place()
    for start in range(0, centre_ref.shape[1], 2 * SUB):
        values = [centre_ref[layer, start:start + 2 * SUB, :] for layer in range(s["layers"])]
        pack_strips(s, values, lax.rem(gx, 2) == 0, first_ref, start)
    breadth, taps, radius = s["breadth"], s["taps"], s["radius"]
    ring = 2 * breadth
    chunk = 32
    target = lax.broadcasted_iota(jnp.int32, (1, ring), 1)
    for number in range(6):
        band, member = divmod(number, 2)
        columns = [columns_ref[band, t, :1, :] for t in range(taps)]
        reached = column_of(s, target, member)
        reached = jnp.where(reached < 1 << 19, reached + radius, -(1 << 20))
        for start in range(0, ring, chunk):
            source = lax.broadcasted_iota(jnp.int32, (chunk, 1), 0) + start
            distance = reached - column_of(s, source, member)
            total = jnp.zeros((chunk, ring), F32)
            for tap in range(taps):
                total = jnp.where(distance == tap, columns[tap], total)
            full[start:start + chunk, :] = total
        matrix = full[...]
        for ref, value in ((forward_ref, matrix), (backward_ref, matrix.T)):
            upper = value.astype(BF16)
            ref[number, :ring, :] = upper
            ref[number, ring:2 * ring, :] = (value - upper.astype(F32)).astype(BF16)
            ref[number, 2 * ring:, :] = upper
    window = SUB + 2 * radius
    size = s["layers"] * window
    place_in = lax.broadcasted_iota(jnp.int32, (SUB, size), 1)
    layer_in, row_in = place_in // window, lax.rem(place_in, window)
    row_out = lax.broadcasted_iota(jnp.int32, (SUB, size), 0)

    def wide(band, dim, tap):
        return jnp.broadcast_to(taps_ref[band, dim, 0, tap][:1, :1], (SUB, size))

    for band in range(3):
        for transposed in range(2):
            number = 2 * band + transposed
            apart = row_in - row_out if transposed else row_out + 2 * radius - row_in
            by_row = jnp.zeros((SUB, size), F32)
            for tap in range(taps):
                by_row = jnp.where(apart == tap, wide(band, 1, tap), by_row)
            depth_taps = [wide(band, 0, tap) for tap in range(taps)]
            for layer in range(s["layers"]):
                apart = layer_in - layer + radius if transposed else layer - layer_in + radius
                value = jnp.zeros((SUB, size), F32)
                for tap in range(taps):
                    value = jnp.where(apart == tap, depth_taps[tap], value)
                full[layer * SUB:(layer + 1) * SUB, :size] = value * by_row
            value = full[:s["layers"] * SUB, :size]
            upper = value.astype(BF16)
            depth_ref[number, :, :size] = upper
            depth_ref[number, :, size:2 * size] = upper
            depth_ref[number, :, 2 * size:] = (value - upper.astype(F32)).astype(BF16)


def strip_places(s, layer):
    group, lane = divmod(layer * s["halo"], s["breadth"])
    return group, lane, min(s["halo"], s["breadth"] - lane)


def copy_kernel(tile_ref, out_ref):
    out_ref[...] = tile_ref[...]


def pack_strips(s, values, right, out_ref, start):
    halo, breadth = s["halo"], s["breadth"]
    lane = lax.broadcasted_iota(jnp.int32, (1, breadth), 1)
    count = values[0].shape[0]
    total = [jnp.zeros((count, breadth), F32)] * s["groups"]
    for layer, value in enumerate(values):
        group, begin, here = strip_places(s, layer)
        moved = pltpu.roll(value, jnp.where(right, (begin + halo) % breadth, begin), 1)
        total[group] = jnp.where((lane >= begin) & (lane < begin + here), moved, total[group])
        if here < halo:
            total[group + 1] = jnp.where(lane < halo - here, moved, total[group + 1])
    for number in range(s["groups"]):
        out_ref[number, start:start + count, :] = total[number]


def pack_kernel(s, tile_ref, even_ref, odd_ref, after_ref, second_ref, centre_ref):
    gy, gx, _, _ = place()
    halo, height = s["halo"], s["height"]
    row_even = lax.rem(gy, 2) == 0
    for start, count in ((0, halo), (halo, height), (halo + height, halo)):
        values = []
        for layer in range(s["layers"]):
            if start == halo:
                value = tile_ref[layer]
            elif start == 0:
                value = jnp.where(row_even, odd_ref[layer], even_ref[layer])
            else:
                value = jnp.where(row_even, even_ref[layer], odd_ref[layer])
            centre_ref[layer, start:start + count, :] = value
            values.append(value)
        pack_strips(s, values, lax.rem(gx, 2) == 1, second_ref, start)


def unpack_layer(s, groups, layer, to):
    breadth = s["breadth"]
    lane = lax.broadcasted_iota(jnp.int32, (1, breadth), 1)
    group, begin, here = strip_places(s, layer)
    value = groups[group]
    if here < s["halo"]:
        value = jnp.where(lane >= begin, value, groups[group + 1])
    shift = (to - begin) % breadth
    return pltpu.roll(value, shift, 1) if shift else value


def first_lanes(s):
    lane = lax.broadcasted_iota(jnp.int32, (1, s["breadth"]), 1)
    return (lane < s["quarter"]) | (lane >= 3 * s["quarter"])


def swap_layers(s, value):
    return pltpu.roll(value, 2 * s["quarter"], 1)


def weighted(taps, values):
    total = None
    for tap, value in zip(taps, values):
        if value is not None:
            total = tap * value if total is None else total + tap * value
    return total


def shifts_of(s, transposed):
    return [t - s["radius"] if transposed else s["radius"] - t for t in range(s["taps"])]


def own_sums(s, windows, matrix):
    layers, breadth = s["layers"], s["breadth"]
    value = jnp.concatenate([w.reshape(layers * w.shape[1], breadth) for w in windows], axis=1)
    upper = value.astype(BF16)
    lower = (value - upper.astype(F32)).astype(BF16)
    result = jnp.dot(matrix, jnp.concatenate([upper, lower, upper], axis=0), preferred_element_type=F32)
    return [
        [result[p * SUB:(p + 1) * SUB, k * breadth:(k + 1) * breadth] for p in range(layers)] for k in range(len(windows))
    ]


def side_sums(s, load, row_taps, depth_taps, transposed):
    layers, radius, pairs = s["layers"], s["radius"], s["pairs"]
    shifts = shifts_of(s, transposed)
    mixed = [weighted(row_taps, [load(layers + p, shift) for shift in shifts]) for p in range(pairs)]
    beyond = {}
    first = first_lanes(s)
    for step in range(1, radius + 1):
        beyond[-step] = jnp.where(first, 0.0, swap_layers(s, mixed[pairs - step]))
        beyond[pairs - 1 + step] = jnp.where(first, swap_layers(s, mixed[step - 1]), 0.0)
    at = lambda p: mixed[p] if 0 <= p < pairs else beyond.get(p)
    return [weighted(depth_taps, [at(p + shift) for shift in shifts]) for p in range(pairs)]


def slope_tile(s, source, shift, tile, divergence, flux_rows, where, rows_only=False, own_only=False):
    gy, gx, ny, nx = where
    layers, height, breadth, pairs, quarter = s["layers"], s["height"], s["breadth"], s["pairs"], s["quarter"]
    lane = lax.broadcasted_iota(jnp.int32, (SUB, breadth), 1)
    side_col = jnp.where(lax.rem(lane // quarter, 2) == 0, breadth + lax.rem(lane, quarter), lax.rem(lane, quarter) - quarter)
    masks = []
    for col in (lane, side_col):
        col = gx * breadth + col
        masks.append(jnp.where((col >= 0) & (col < nx * breadth - 1), 1.0, 0.0).astype(F32))
    start = tile * SUB
    row = gy * height + start - s["off"] + shift + lax.broadcasted_iota(jnp.int32, (SUB, breadth), 0)
    row_mask = jnp.where((row >= 0) & (row < ny * height - 1), 1.0, 0.0).astype(F32)
    at_edge = tile * SUB + shift - s["off"] in (-SUB, height - SUB)
    last, first = breadth - 1, first_lanes(s)
    rows = slice(start, start + SUB)

    def swap(value):
        return swap_layers(s, value)

    before = [None, None, None]
    heres = [source[plane, rows, :] for plane in (0, pairs, layers)]
    for p in range(pairs):
        planes = (p, p + pairs, layers + p)
        afters = [source[plane + 1, rows, :] if p + 1 < pairs else None for plane in planes]
        if p + 1 == pairs:
            afters[0] = source[pairs, rows, :]
            afters[2] = jnp.where(first, swap(source[layers, rows, :]), heres[2])
        rolled = [pltpu.roll(value, breadth - 1, 1) for value in heres]
        nexts = [
            jnp.where(lane == last, rolled[2], rolled[0]),
            jnp.where(lane == last, swap(rolled[2]), rolled[1]),
            jnp.where(lane == last, rolled[0], jnp.where(lane == 2 * quarter - 1, swap(rolled[1]), rolled[2])),
        ]
        f_cols, totals = [], []
        for k, plane in enumerate(planes):
            here = heres[k]
            step_rows = source[plane, start + 1:start + 1 + SUB, :] - here
            if at_edge:
                step_rows = step_rows * row_mask
            step_cols = (nexts[k] - here) * masks[k // 2]
            square = step_rows * step_rows + step_cols * step_cols + SMOOTHING * SMOOTHING
            if afters[k] is not None:
                step_depth = afters[k] - here
                square = square + step_depth * step_depth
            inverse = lax.rsqrt(square)
            if own_only and k == 2:
                f_cols.append(step_cols * inverse)
                continue
            f_rows = step_rows * inverse
            flux_rows[plane, rows, :] = f_rows
            if rows_only:
                continue
            f_cols.append(step_cols * inverse)
            total = -f_cols[k] - f_rows
            if before[k] is not None:
                total = total + before[k]
            before[k] = None
            if afters[k] is not None:
                before[k] = step_depth * inverse
                total = total - before[k]
            totals.append(total)
        heres = afters
        if rows_only:
            continue
        rolled = [pltpu.roll(value, 1, 1) for value in f_cols]
        totals[0] = totals[0] + jnp.where(lane == 0, rolled[2], rolled[0])
        totals[1] = totals[1] + jnp.where(lane == 0, swap(rolled[2]), rolled[1])
        if not own_only:
            totals[2] = totals[2] + jnp.where(lane == 0, rolled[0], jnp.where(lane == 2 * quarter, swap(rolled[1]), rolled[2]))
        for plane, total in zip(planes, totals):
            divergence[plane, rows, :] = total
    if rows_only:
        return
    divergence[pairs, rows, :] = divergence[pairs, rows, :] + before[0]
    if own_only:
        return
    divergence[layers, rows, :] = divergence[layers, rows, :] + jnp.where(first, 0.0, swap(before[2]))


def main_kernel(s, centre_ref, first_ref, second_ref, taps_ref, forward_ref, backward_ref, depth_ref,
                x1_ref, g1_ref, pull_ref, again_ref, part_ref,
                x0, x1, x2, g0, y0, y1, y2, r0, r1, r2, q0, q1, q2, acc, div, flux):
    where = place()
    gy, gx, ny, nx = where
    layers, height, breadth, off = s["layers"], s["height"], s["breadth"], s["off"]
    halo, radius, taps, pairs, planes, quarter = [s[k] for k in ("halo", "radius", "taps", "pairs", "planes", "quarter")]
    begin, end = s["first"], s["last"]
    col_even = lax.rem(gx, 2) == 0
    lane = lax.broadcasted_iota(jnp.int32, (1, breadth), 1)
    xs, ys, rs, qs = (x0, x1, x2), (y0, y1, y2), (r0, r1, r2), (q0, q1, q2)
    span = bands(s)

    def rows(tile, stop=None):
        return slice(tile * SUB, (tile + 1 if stop is None else stop) * SUB)

    top = off - halo
    x0[:layers, top:off + height + halo, :] = centre_ref[...]
    firsts = [first_ref[g] for g in range(s["groups"])]
    seconds = [second_ref[g] for g in range(s["groups"])]
    rights = [jnp.where(col_even, a, b) for a, b in zip(firsts, seconds)]
    lefts = [jnp.where(col_even, b, a) for a, b in zip(firsts, seconds)]
    for p in range(pairs):
        value = jnp.zeros((height + 2 * halo, breadth), F32)
        for groups, layer, to in ((rights, p, 0), (lefts, p + pairs, 2 * quarter - halo),
                                  (rights, p + pairs, 2 * quarter), (lefts, p, breadth - halo)):
            value = jnp.where((lane >= to) & (lane < to + halo), unpack_layer(s, groups, layer, to), value)
        x0[layers + p, top:off + height + halo, :] = value
    zero = jnp.zeros((planes, SUB, breadth), F32)
    for ref, tiles in ((y0, (0,)), (y2, (s["tiles"] - 1,)), (r0, (begin, begin + 1)),
                       (r1, (begin - 2, begin - 1, end, end + 1)), (r2, (end - 2, end - 1))):
        for tile in tiles:
            ref[:, rows(tile), :] = zero

    def product(ref, low, high, band, matrices, own_only=False):
        width = breadth if own_only else 2 * breadth
        count = (high - low) * SUB

        def split(a, b):
            value = ref[a:b, rows(low, high), :].reshape((b - a) * count, breadth)
            upper = value.astype(BF16)
            return upper, (value - upper.astype(F32)).astype(BF16)

        side_high, side_low = split(layers, planes)
        own, side = [], None
        for member in range(2):
            high_part, low_part = split(member * pairs, (member + 1) * pairs)
            parts = [high_part, side_high] * 2 + [low_part, side_low]
            result = jnp.dot(jnp.concatenate(parts, axis=1), matrices[2 * band + member, :, :width], preferred_element_type=F32)
            own.append(result[:, :breadth].reshape(pairs, count, breadth))
            if not own_only:
                rest = result[:, breadth:]
                side = rest if side is None else side + rest
        pieces = [(0, own[0]), (pairs, own[1])]
        return pieces if own_only else pieces + [(layers, side.reshape(pairs, count, breadth))]

    def taps_of(band, half):
        return [[taps_ref[band, dim, half, t] for t in range(taps)] for dim in (1, 0)]

    def one_pass(number):
        x = xs[number]
        low, high = reach(s, (5 - 2 * number) * radius)
        in_low, in_high = reach(s, (6 - 2 * number) * radius)
        back_low, back_high = reach(s, (4 - 2 * number) * radius)
        out = [(max(low, a), min(high, b)) for a, b in span]
        back = [(max(back_low, a - 1), min(back_high, b + 1)) for a, b in span]
        done = set()

        def columns(band):
            a, b = max(out[band][0] - 1, in_low), min(out[band][1] + 1, in_high)
            for plane, piece in product(x, a, b, band, forward_ref):
                ys[band][plane:plane + pairs, rows(a, b), :] = piece

        def sums(band, source, low, high, transposed, emit):
            row_taps, depth_taps = taps_of(band, 1)

            def load_at(tile):
                def load(plane, shift):
                    if transposed and ((tile < span[band][0] and shift <= 0) or (tile >= span[band][1] and shift >= 0)):
                        return None
                    return source[plane, tile * SUB + shift:(tile + 1) * SUB + shift, :]

                return load

            for at in range(low, high, 2):
                group = range(at, min(at + 2, high))
                matrix = depth_ref[2 * band + (1 if transposed else 0)]
                windows = [source[:layers, tile * SUB - radius:(tile + 1) * SUB + radius, :] for tile in group]
                results = own_sums(s, windows, matrix)
                for tile, result in zip(group, results):
                    side = side_sums(s, load_at(tile), row_taps, depth_taps, transposed)
                    for plane, value in enumerate(result + side):
                        emit(plane, tile, value)

        def blur_rows(band):
            def emit(plane, tile, value):
                rs[band][plane, rows(tile), :] = value if number == 2 else value - x0[plane, rows(tile), :]

            sums(band, ys[band], *out[band], False, emit)

        def back_rows(band):
            def emit(plane, tile, value):
                qs[band][plane, rows(tile), :] = value

            sums(band, rs[band], *back[band], True, emit)

        def back_columns(band):
            a, b = back[band]
            for plane, piece in product(qs[band], a, b, band, backward_ref, number == 2):
                for tile in range(a, b):
                    part = piece[:, (tile - a) * SUB:(tile - a + 1) * SUB, :]
                    at = slice(plane, plane + pairs)
                    acc[at, rows(tile), :] = acc[at, rows(tile), :] + part if tile in done else part
            done.update(range(a, b))

        def inside(tile, side):
            row = gy * height + tile * SUB - off + lax.broadcasted_iota(jnp.int32, (SUB, breadth), 0)
            here = lax.broadcasted_iota(jnp.int32, (SUB, breadth), 1)
            if side:
                part = lax.rem(here, quarter)
                here = jnp.where(lax.rem(here // quarter, 2) == 0, breadth + part, part - quarter)
            col = gx * breadth + here
            return (row >= 0) & (row < ny * height) & (col >= 0) & (col < nx * breadth)

        def update(tile):
            keep = [inside(tile, side) for side in range(2)]
            for plane in range(planes):
                here = x[plane, rows(tile), :]
                total = acc[plane, rows(tile), :] + DAMPING * here
                before = flux[plane, tile * SUB - 1:(tile + 1) * SUB - 1, :]
                total = total + WEIGHT_TV * (div[plane, rows(tile), :] + before)
                total = jnp.where(keep[plane // layers], total, 0.0)
                if number == 0:
                    xs[1][plane, rows(tile), :] = here - START_STEP * total
                    if plane < layers and begin <= tile < end:
                        g0[plane, rows(tile), :] = total
                else:
                    xs[2][plane, rows(tile), :] = total

        def slopes(a, b):
            if number < 2:
                for tile in range(a, b):
                    slope_tile(s, x, 0, tile, div, flux, where, tile < back_low)

        middle = (begin + end) // 2
        columns(0)
        slopes(back_low - 1, middle)
        columns(1)
        blur_rows(0)
        columns(2)
        back_rows(0)
        blur_rows(1)
        back_columns(0)
        back_rows(1)
        back_columns(1)
        blur_rows(2)
        slopes(middle, back_high)
        back_rows(2)
        back_columns(2)
        if number == 1:
            pull_ref[...] = acc[:layers, rows(begin, end), :]
        if number < 2:
            for tile in range(back_low, back_high):
                update(tile)

    for number in range(3):
        one_pass(number)
    again_ref[...] = acc[:layers, rows(begin, end), :]
    low, high = reach(s, 2 * radius)
    x1_ref[...] = x1[:, rows(low, high), :]
    g1_ref[...] = x2[:, rows(low, high), :]

    zero_sq = cross = one_sq = jnp.zeros((SUB, breadth), F32)
    for tile in range(begin, end):
        for layer in range(layers):
            a, b = g0[layer, rows(tile), :], x2[layer, rows(tile), :]
            zero_sq, cross, one_sq = zero_sq + a * a, cross + a * (b - a), one_sq + b * b
    zero_sq, cross, one_sq = [jnp.sum(t, axis=(0, 1), keepdims=True) for t in (zero_sq, cross, one_sq)]
    row = jnp.where(lane == 0, zero_sq, jnp.where(lane == 1, cross, one_sq))
    part_ref[...] = jnp.broadcast_to(row, part_ref.shape)


def step_kernel(s, sums_ref, x1_ref, g1_ref, pull_ref, again_ref, x2_ref, g2_ref, part_ref, keep_ref, x2, div, flux):
    where = place()
    layers, height, breadth = s["layers"], s["height"], s["breadth"]
    low, high = reach(s, 2 * s["radius"])
    lane = lax.broadcasted_iota(jnp.int32, (1, breadth), 1)
    total = jnp.sum(sums_ref[...], axis=0, keepdims=True)
    zero_sq, cross, one_sq = [
        jnp.sum(jnp.where(lane == number, total, 0.0), axis=(0, 1), keepdims=True) for number in range(3)
    ]
    step = (START_STEP * START_STEP * zero_sq) / (-START_STEP * cross)
    count = (high - low) * SUB
    for plane in range(s["planes"]):
        x2[plane, :count, :] = x1_ref[plane] - step * g1_ref[plane]
    begin = s["first"] - low
    total = jnp.zeros((SUB, breadth), F32)
    for tile in range(begin - 1, begin + height // SUB):
        slope_tile(s, x2, low * SUB, tile, div, flux, where, tile < begin, True)
        if tile < begin:
            continue
        at, out = slice(tile * SUB, (tile + 1) * SUB), slice((tile - begin) * SUB, (tile - begin + 1) * SUB)
        for layer in range(layers):
            here = x2[layer, at, :]
            slope = pull_ref[layer, out, :] - step * again_ref[layer, out, :] + DAMPING * here
            slope = slope + WEIGHT_TV * (div[layer, at, :] + flux[layer, tile * SUB - 1:(tile + 1) * SUB - 1, :])
            x2_ref[layer, out, :] = here
            g2_ref[layer, out, :] = slope
            old = g1_ref[layer, at, :]
            total = total + old * (slope - old)
    growth = -step * jnp.sum(total, axis=(0, 1), keepdims=True)
    part_ref[...] = jnp.broadcast_to(growth, part_ref.shape)
    keep_ref[...] = jnp.broadcast_to(step * step * one_sq, keep_ref.shape)


def final_kernel(sums_ref, keep_ref, x2_ref, g2_ref, out_ref):
    step = keep_ref[:1, :] / jnp.sum(sums_ref[...], axis=0, keepdims=True)
    for layer in range(x2_ref.shape[0]):
        out_ref[layer] = x2_ref[layer] - step * g2_ref[layer]


def pairings(count):
    def both(start):
        pairs = []
        for i in range(start, count - 1, 2):
            pairs += [(i, i + 1), (i + 1, i)]
        return pairs

    return both(0), both(1)


def call(kernel, outs, scratch=(), inputs=None):
    whole = pl.BlockSpec(memory_space=pltpu.VMEM)
    return pl.pallas_call(
        kernel,
        out_shape=outs,
        in_specs=inputs,
        out_specs=jax.tree.map(lambda _: whole, outs),
        scratch_shapes=list(scratch),
        compiler_params=pltpu.CompilerParams(vmem_limit_bytes=VMEM_BYTES),
    )


def per_device(observed, profiles, tile_index):
    layers, height, breadth = observed.shape
    s = plan(layers, height, breadth, profiles.shape[2])
    halo, rows, taps = s["halo"], s["rows"], s["taps"]
    ring = 2 * breadth
    gy = lax.axis_index("gy")
    n = lax.axis_size("gy") * lax.axis_size("gx")
    vmem, smem = pl.BlockSpec(memory_space=pltpu.VMEM), pl.BlockSpec(memory_space=pltpu.SMEM)
    sds = jax.ShapeDtypeStruct

    even = lax.rem(gy, 2) == 0
    bottom, top = jnp.int32(height - halo), jnp.int32(0)
    to_even = lax.dynamic_slice_in_dim(observed, jnp.where(even, bottom, top), halo, axis=1)
    to_odd = lax.dynamic_slice_in_dim(observed, jnp.where(even, top, bottom), halo, axis=1)
    first_pairs, second_pairs = pairings(lax.axis_size("gy"))
    from_even = lax.ppermute(to_even, "gy", first_pairs)
    from_odd = lax.ppermute(to_odd, "gy", second_pairs)

    packed = (s["groups"], height + 2 * halo, breadth)
    anywhere = pl.BlockSpec(memory_space=pl.ANY)
    taps_all, columns = call(
        functools.partial(weights_kernel, s),
        (sds((3, 2, 2, taps, SUB, breadth), F32), sds((3, taps, SUB, ring), F32)), inputs=[smem, smem],
    )(tile_index, profiles.transpose(2, 1, 0))
    tile_here = call(copy_kernel, sds(observed.shape, F32), inputs=[vmem])(observed)
    second, centre = call(
        functools.partial(pack_kernel, s),
        (sds(packed, F32), sds((layers, height + 2 * halo, breadth), F32)),
        inputs=[vmem] * 3 + [anywhere],
    )(tile_here, from_even, from_odd, taps_all)
    matrices = sds((6, 3 * ring, ring), BF16)
    size = layers * (SUB + 2 * s["radius"])
    forward, backward, depth, first = call(
        functools.partial(matrices_kernel, s), (matrices, matrices, sds((6, layers * SUB, 3 * size), BF16), sds(packed, F32)),
        scratch=[pltpu.VMEM((ring, ring), F32)], inputs=[vmem, vmem, anywhere, vmem],
    )(columns, taps_all, second, centre)
    first_pairs, second_pairs = pairings(lax.axis_size("gx"))
    got_first = lax.ppermute(first, "gx", first_pairs)
    got_second = lax.ppermute(second, "gx", second_pairs)

    big = (s["planes"], rows, breadth)
    low, high = reach(s, 2 * s["radius"])
    wide = (s["planes"], (high - low) * SUB, breadth)
    tile = sds((layers, height, breadth), F32)
    x1, g1, pull, again, part = call(
        functools.partial(main_kernel, s),
        (sds(wide, F32), sds(wide, F32), tile, tile, sds((n, breadth), F32)),
        scratch=[pltpu.VMEM(shape, F32) for shape in [big] * 3 + [(layers, rows, breadth)] + [big] * 12],
        inputs=[vmem] * 7,
    )(centre, got_first, got_second, taps_all, forward, backward, depth)
    sums = lax.all_to_all(part, ("gy", "gx"), 0, 0, tiled=True)
    work = pltpu.VMEM((s["planes"], (high - low + 1) * SUB, breadth), F32)
    x2, g2, part, keep = call(
        functools.partial(step_kernel, s),
        (tile, tile, sds((n, breadth), F32), sds((SUB, breadth), F32)),
        scratch=[work] * 3,
        inputs=[vmem] * 5,
    )(sums, x1, g1, pull, again)
    sums = lax.all_to_all(part, ("gy", "gx"), 0, 0, tiled=True)
    return call(final_kernel, tile, inputs=[vmem] * 4)(sums, keep, x2, g2)


def solution(mesh):
    in_specs = (P(None, "gy", "gx"), P(), P())
    out_specs = P(None, "gy", "gx")
    return jax.shard_map(
        per_device, mesh=mesh, in_specs=in_specs, out_specs=out_specs, check_vma=False
    )
```
